256 devices in a mesh: dp: 8 (over z), seq: 32 (over y, x, core).
Axes of the slice: x: 4, y: 4, z: 8, core: 2. Of those that a mesh axis runs over, the one named last changes fastest.
Arguments:
- latents: bfloat16 [8, 32, 256, 1152], P('dp', 'seq'), may hold values from -6 to 6
- cotangent: bfloat16 [8, 32, 256, 1152], P('dp', 'seq'), may hold values from -6 to 6
- qkv_weight: bfloat16 [1152, 3456], replicated, may hold values from -0.1875 to 0.1875
- out_weight: bfloat16 [1152, 1152], replicated, may hold values from -0.1875 to 0.1875
- modulation: float32 [8, 4, 3, 1152], P('dp'), may hold values from -3 to 3
- frame_clip: int32 [8, 32], P('dp'), may hold values from 0 to 3, never falling along the last dimension, each value on 1 to 16 neighbouring positions
- clip_patches: int32 [8, 4], P('dp'), may hold values from 32 to 256, as said below
Outputs:
- block_out: bfloat16 [8, 32, 256, 1152], P('dp', 'seq')
- latent_grad: bfloat16 [8, 32, 256, 1152], P('dp', 'seq')
- weight_grads: float32 [1152, 1152], P('seq')
The draws below stay inside these ranges and needn't reach their ends.
Inputs may be any that keep to these rules, and one draw needn't show every extreme that they name: `frame_clip`: frames of one clip are consecutive in their group; every group holds 4 clips of 1 to 16 frames, one of exactly 16. `clip_patches`: in every group some clip fills all 256 patch slots.
All inputs are finite; a program needn't handle non-finite values.
Results may differ from the reference program's by a relative error of at most 0.029.
Values may be sent and summed in bfloat16 or wider, within the bound.
No kernel may reach another device: no remote copies, remote signals or barrier semaphores. Data moves between devices by JAX's collectives and lax.ppermute only.
A program may use at most 128 MiB of HBM per device.

```python
import math
import jax
import jax.numpy as jnp
import numpy as np
from jax import lax

D = 1152
HEADS = 16
PATCHES = 256
CLIPS = 4
GROUPS = 8
FRAMES = 32
MOST_FRAMES = 16


def draw_clip_patches(key, part):
    key = jax.random.fold_in(key, 5)
    first_key, second_key = jax.random.split(key)
    drawn = jax.random.randint(first_key, (GROUPS, CLIPS), PATCHES // 8, PATCHES + 1)
    chosen = jax.random.randint(second_key, (GROUPS, 1), 0, CLIPS)
    filled = jnp.where(jnp.arange(CLIPS)[None, :] == chosen, PATCHES, drawn)
    return filled.astype(jnp.int32)


def with_spikes(result, own_key, source, target, parts, factor):
    def block_of(dim):
        return (jnp.arange(result.shape[dim]) // (result.shape[dim] // parts)).reshape((-1,) + (1,) * (result.ndim - 1 - dim))

    first = jax.random.permutation(own_key, parts)[block_of(target)]
    other_side = (block_of(target) + parts // 2) % parts
    return jnp.where((block_of(source) == first) | (block_of(source) == other_side), factor * result, result)


def steps_of(stream_key, shape, shards, low, top_value):
    factor_of, own = 1.0, jax.random.fold_in(stream_key, 6)
    for position, shards_of in shards:
        draws = jnp.exp(jax.random.uniform(jax.random.fold_in(own, position), (shards_of,), jnp.float32, low / len(shards), top_value / len(shards)))
        factor_of = factor_of * jnp.repeat(draws, shape[position] // shards_of).reshape([-1 if axis == position else 1 for axis in range(len(shape))])
    return factor_of


def split_up(amount, total, limit, lean):
    portions = [(1 << 20) // math.isqrt(standing ** lean) + 1 for standing in range(2, amount + 1)]
    surplus, given = total - limit - (amount - 1), [1] * (amount - 1)
    while surplus > 0:
        free = [i for i in range(amount - 1) if given[i] < limit]
        mass, remaining = sum([portions[i] for i in free]), surplus
        for i in free:
            more = min(limit - given[i], max(1, remaining * portions[i] // mass), surplus)
            given[i] = given[i] + more
            surplus = surplus - more
    return np.array([limit] + given)


def uneven_parts(rng, number_of, total, bound, skew):
    if number_of == 2:
        one = jax.random.randint(rng, (), max(1, total - bound), min(bound, total - 1) + 1)
        return jnp.stack([one, total - one])
    sizes = jnp.asarray(split_up(number_of, total, bound, skew), jnp.int32)
    couples = (number_of - 1) // 2
    source_of, receiver = sizes[1:1 + 2 * couples:2], sizes[2:2 + 2 * couples:2]
    margin = jnp.minimum(source_of - 1, bound - receiver)
    moved = jax.random.randint(jax.random.fold_in(rng, 1), (couples,), 0, 1 << 20) % (margin + 1)
    sizes = sizes.at[1:1 + 2 * couples:2].set(source_of - moved).at[2:2 + 2 * couples:2].set(receiver + moved)
    return sizes[jax.random.permutation(jax.random.fold_in(rng, 2), number_of)]


def noise(own_key, extent, scale, limit, cuts=(), held_as=jnp.bfloat16):
    gain = steps_of(own_key, extent, cuts, -0.22, 0.18) if cuts else 1.0
    array = jax.random.normal(own_key, extent, jnp.float32) * scale * gain
    return jnp.minimum(jnp.maximum(array, -limit), limit).astype(held_as)


def gaussian_with(own_key, shape, scale, bound, cuts, heavy, kind=jnp.bfloat16):
    values = scale * jax.random.normal(own_key, shape, jnp.float32)
    if cuts:
        values = values * steps_of(own_key, shape, cuts, -0.22, 0.18)
    return jnp.clip(with_spikes(values, jax.random.fold_in(own_key, 3), *heavy), -bound, bound).astype(kind)


def setup_inputs(seed: int = 0) -> dict:
    seeds = jax.random.split(jax.random.key(seed), 8)
    latents = noise(seeds[0], (GROUPS, FRAMES, PATCHES, D), 1.0, 6.0, ((0, 8), (1, 32)))
    cotangent = gaussian_with(seeds[1], (GROUPS, FRAMES, PATCHES, D), 1.0, 6.0, ((0, 8), (1, 32)), (1, 3, 32, 2.75))
    qkv_weight = noise(seeds[2], (D, 3 * D), D ** -0.5, 0.1875)
    out_weight = noise(seeds[3], (D, D), D ** -0.5, 0.1875)
    modulation = noise(seeds[4], (GROUPS, CLIPS, 3, D), 0.5, 3.0, ((0, 8),), jnp.float32)
    frame_clip = jax.vmap(lambda own: jnp.searchsorted(jnp.cumsum(uneven_parts(own, CLIPS, FRAMES, MOST_FRAMES, 0)), jnp.arange(FRAMES), side="right"))(jax.random.split(seeds[5], GROUPS)).reshape((GROUPS, FRAMES)).astype(jnp.int32)
    clip_patches = draw_clip_patches(jax.random.fold_in(seeds[7], 71), 0)
    return dict(latents=latents, cotangent=cotangent, qkv_weight=qkv_weight, out_weight=out_weight, modulation=modulation, frame_clip=frame_clip, clip_patches=clip_patches)


def norm_parts(values):
    center = values - lax.optimization_barrier(jnp.mean(values, axis=-1, keepdims=True))
    spread = lax.optimization_barrier(jnp.mean(center * center, axis=-1, keepdims=True))
    inv_std = lax.rsqrt(spread + 1e-06)
    return (center * inv_std, inv_std)

def contract_rows(left, right):
    return lax.dot_general(left, right, (((0,), (0,)), ((), ())), preferred_element_type=jnp.float32)

def reference(latents, cotangent, qkv_weight, out_weight, modulation, frame_clip, clip_patches):
    groups_n, frames_n, patches_n, model_w = latents.shape
    head_dim = model_w // HEADS
    att_scale = head_dim ** (-0.5)
    per_frame = jnp.take_along_axis(modulation, frame_clip[:, :, None, None].astype(jnp.int32), axis=1)
    shifts = per_frame[:, :, 0][:, :, None, :]
    scales = per_frame[:, :, 1][:, :, None, :]
    gates = per_frame[:, :, 2][:, :, None, :]
    frame_count = jnp.take_along_axis(clip_patches, frame_clip.astype(jnp.int32), axis=1)
    valid_rows = (jnp.arange(patches_n, dtype=jnp.int32)[None, None, :] < frame_count[:, :, None]).astype(jnp.float32)[..., None]
    latent_f = latents.astype(jnp.float32)
    normed, inv_std = norm_parts(latent_f)
    xmod = (normed * (1.0 + scales) + shifts).astype(jnp.bfloat16)
    xmod_flat = xmod.reshape(-1, model_w)
    qkv = jnp.dot(xmod_flat, qkv_weight, preferred_element_type=jnp.float32).astype(jnp.bfloat16)
    qkv = qkv.reshape(groups_n, frames_n, patches_n, 3 * model_w)
    query_h = qkv[..., :model_w].reshape(groups_n, frames_n, patches_n, HEADS, head_dim).astype(jnp.float32)
    key_h = qkv[..., model_w:2 * model_w].reshape(groups_n, frames_n, patches_n, HEADS, head_dim).astype(jnp.float32)
    value_h = qkv[..., 2 * model_w:].reshape(groups_n, frames_n, patches_n, HEADS, head_dim).astype(jnp.float32)
    same_clip = (frame_clip[:, :, None] == frame_clip[:, None, :]).astype(jnp.float32)[:, None, None]
    scores = jnp.einsum('gfphd,gephd->gphfe', query_h, key_h)
    expo = jnp.exp(scores * att_scale) * same_clip
    attn_prob = expo / lax.optimization_barrier(jnp.sum(expo, axis=-1, keepdims=True))
    prob_low = attn_prob.astype(jnp.bfloat16).astype(jnp.float32)
    attended = jnp.einsum('gphfe,gephd->gfphd', prob_low, value_h).astype(jnp.bfloat16)
    att_flat = attended.reshape(-1, model_w)
    proj = jnp.dot(att_flat, out_weight, preferred_element_type=jnp.float32).reshape(latents.shape)
    block_out = (latent_f + valid_rows * gates * proj).astype(jnp.bfloat16)
    cot_f = cotangent.astype(jnp.float32)
    gdy = (valid_rows * gates * cot_f).astype(jnp.bfloat16)
    gdy_flat = gdy.reshape(-1, model_w)
    d_att = lax.dot_general(gdy_flat, out_weight, (((1,), (1,)), ((), ())), preferred_element_type=jnp.float32).astype(jnp.bfloat16)
    d_att = d_att.reshape(groups_n, frames_n, patches_n, HEADS, head_dim).astype(jnp.float32)
    grad_v = jnp.einsum('gphfe,gfphd->gephd', prob_low, d_att).astype(jnp.bfloat16)
    d_prob = jnp.einsum('gfphd,gephd->gphfe', d_att, value_h)
    d_score = attn_prob * (d_prob - lax.optimization_barrier(jnp.sum(attn_prob * d_prob, axis=-1, keepdims=True)))
    score_low = (d_score * att_scale).astype(jnp.bfloat16).astype(jnp.float32)
    grad_q = jnp.einsum('gphfe,gephd->gfphd', score_low, key_h).astype(jnp.bfloat16)
    grad_k = jnp.einsum('gphfe,gfphd->gephd', score_low, query_h).astype(jnp.bfloat16)
    dqkv = jnp.concatenate([grad_q.reshape(-1, model_w), grad_k.reshape(-1, model_w), grad_v.reshape(-1, model_w)], axis=1)
    dxmod = lax.dot_general(dqkv, qkv_weight, (((1,), (1,)), ((), ())), preferred_element_type=jnp.float32).reshape(latents.shape)
    dnorm = dxmod * (1.0 + scales)
    branch = inv_std * (dnorm - lax.optimization_barrier(jnp.mean(dnorm, axis=-1, keepdims=True)) - normed * lax.optimization_barrier(jnp.mean(dnorm * normed, axis=-1, keepdims=True)))
    latent_grad = (cot_f + branch).astype(jnp.bfloat16)
    weight_grads = contract_rows(gdy_flat, att_flat)
    return (block_out, latent_grad, weight_grads)
```

```python
import jax
import jax.numpy as jnp
from jax import lax
from jax.experimental import pallas as pl
from jax.experimental.pallas import tpu as pltpu
from jax.sharding import PartitionSpec as P

HEADS = 16
LANES = 128
CHUNK = 384
MIB = 1024 * 1024

NN = (((1,), (0,)), ((), ()))
NT = (((1,), (1,)), ((), ()))
TN = (((0,), (0,)), ((), ()))


def dot(left, right, dims):
    return lax.dot_general(left, right, dims, preferred_element_type=jnp.float32)


def head_span(head, head_dim):
    first, last = head * head_dim, (head + 1) * head_dim
    low = first // LANES * LANES
    high = -(-last // LANES) * LANES
    return first, last, low, high


def head_mask(first, last, low, high):
    lane = lax.broadcasted_iota(jnp.int32, (1, high - low), 1) + low
    return jnp.where((lane >= first) & (lane < last), 1.0, 0.0).astype(jnp.bfloat16)


def add_tiles(parts, low, value):
    for start in range(0, value.shape[1], LANES):
        tile = (low + start) // LANES
        piece = value[:, start : start + LANES]
        parts[tile] = parts[tile] + piece if tile in parts else piece


def flush_tiles(parts, done, store):
    for tile in sorted(parts):
        if (tile + 1) * LANES <= done:
            store(tile * LANES, parts.pop(tile))


def normalize(tokens):
    center = tokens - jnp.mean(tokens, axis=-1, keepdims=True)
    spread = jnp.mean(center * center, axis=-1, keepdims=True)
    inv_std = lax.rsqrt(spread + 1e-06)
    return center * inv_std, inv_std


def valid_patches(base, count, patches):
    index = base + lax.broadcasted_iota(jnp.int32, (patches, 1), 0)
    return (index < count).astype(jnp.float32)


def forward_kernel(
    clip_ref, count_ref, place_ref,
    tokens_ref, mod_ref, wqkv_ref,
    qkv_ref, prob_ref, att_ref, gdy_ref, grad_ref,
    xmod_ref, same_ref, sum_ref,
):
    frames, both, model = tokens_ref.shape
    patches = both // 2
    rows = frames * patches
    head_dim = model // HEADS
    base = place_ref[0]
    core = place_ref[1]

    def pair_step(step, carry):
        xmods, gdys = [], []
        for k in range(2):
            frame = 2 * step + k
            clip = clip_ref[0, frame]
            shift = mod_ref[clip, pl.ds(0, 1), :]
            scale = mod_ref[clip, pl.ds(1, 1), :]
            gate = mod_ref[clip, pl.ds(2, 1), :]
            both_f = tokens_ref[frame].astype(jnp.float32)
            normed, _ = normalize(both_f[:patches])
            xmods.append(normed * (1.0 + scale) + shift)
            valid = valid_patches(base, count_ref[0, clip], patches)
            gdys.append(valid * gate * both_f[patches:])
        where = pl.ds(pl.multiple_of(step * both, both), both)
        xmod_ref[where, :] = jnp.concatenate(xmods, axis=0).astype(jnp.bfloat16)
        gdy_ref[where, :] = jnp.concatenate(gdys, axis=0).astype(jnp.bfloat16)
        return carry

    lax.fori_loop(0, frames // 2, pair_step, 0)

    starts = []
    for clip in range(1, mod_ref.shape[0]):
        start = jnp.int32(0)
        for frame in range(frames):
            start = start + jnp.where(clip_ref[0, frame] < clip, 1, 0)
        starts.append(start)

    def key_of(index):
        frame = index // patches
        key = index % patches
        for start in starts:
            key = key + jnp.where(frame >= start, patches, 0)
        return key

    key_e = key_of(lax.broadcasted_iota(jnp.int32, (rows, 1), 0))
    key_f = key_of(lax.broadcasted_iota(jnp.int32, (1, rows), 1))
    same_ref[...] = (key_e == key_f).astype(jnp.float32)

    xmod = xmod_ref[...]
    for start in range(0, 3 * model, CHUNK):
        qkv_ref[:, start : start + CHUNK] = dot(
            xmod, wqkv_ref[:, start : start + CHUNK], NN
        ).astype(jnp.bfloat16)

    def store_att(low, value):
        att_ref[:, low : low + LANES] = value.astype(jnp.bfloat16)

    parts = {}
    for head in range(HEADS):
        first, last, low, high = head_span(head, head_dim)
        mask = head_mask(first, last, low, high)
        query = qkv_ref[:, low:high] * mask
        key = qkv_ref[:, model + low : model + high]
        value = qkv_ref[:, 2 * model + low : 2 * model + high] * mask
        expo = jnp.exp(dot(key, query, NT) * head_dim ** (-0.5)) * same_ref[...]
        prob = (expo * (1.0 / jnp.sum(expo, axis=0, keepdims=True))).astype(jnp.bfloat16)
        prob_ref[head] = prob
        add_tiles(parts, low, dot(prob, value, TN))
        flush_tiles(parts, last, store_att)

    att = att_ref[...]
    for start in range(0, model, LANES):
        sum_ref[start : start + LANES, :] = dot(gdy_ref[:, start : start + LANES], att, TN)
    chips = grad_ref.shape[1]
    held = grad_ref.shape[2]
    share = model // (2 * chips)
    for chip in range(0, chips):
        for side in range(2):
            start = (2 * chip + side) * share
            slot = jnp.where(core == side, 0, 1)
            grad_ref[slot, chip] = sum_ref[start : start + held, :].astype(jnp.bfloat16)


def backward_kernel(
    clip_ref, count_ref, place_ref,
    tokens_ref, mod_ref, wqkv_ref, wout_ref, qkv_ref, prob_ref, att_ref, gdy_ref,
    out_ref,
    datt_ref, dqkv_ref, proj_ref, dxmod_ref,
):
    frames, both, model = tokens_ref.shape
    patches = both // 2
    head_dim = model // HEADS
    att_scale = head_dim ** (-0.5)
    base = place_ref[0]

    gdy = gdy_ref[...]
    att = att_ref[...]
    for start in range(0, model, CHUNK):
        datt_ref[:, start : start + CHUNK] = dot(
            gdy, wout_ref[start : start + CHUNK, :], NT
        ).astype(jnp.bfloat16)
    for start in range(0, model, CHUNK):
        proj_ref[:, start : start + CHUNK] = dot(att, wout_ref[:, start : start + CHUNK], NN)

    def store_at(offset, factor):
        def store(low, value):
            dqkv_ref[:, offset + low : offset + low + LANES] = (value * factor).astype(jnp.bfloat16)
        return store

    parts_q, parts_k, parts_v = {}, {}, {}
    for head in range(HEADS):
        first, last, low, high = head_span(head, head_dim)
        mask = head_mask(first, last, low, high)
        query = qkv_ref[:, low:high] * mask
        key = qkv_ref[:, model + low : model + high] * mask
        value = qkv_ref[:, 2 * model + low : 2 * model + high]
        datt = datt_ref[:, low:high] * mask
        prob_low = prob_ref[head]
        add_tiles(parts_v, low, dot(prob_low, datt, NN))
        prob = prob_low.astype(jnp.float32)
        dprob = dot(value, datt, NT)
        total = jnp.sum(prob * dprob, axis=0, keepdims=True)
        dscore = (prob * (dprob - total)).astype(jnp.bfloat16)
        add_tiles(parts_k, low, dot(dscore, query, NN))
        add_tiles(parts_q, low, dot(dscore, key, TN))
        flush_tiles(parts_q, last, store_at(0, att_scale))
        flush_tiles(parts_k, last, store_at(model, att_scale))
        flush_tiles(parts_v, last, store_at(2 * model, 1.0))

    dqkv = dqkv_ref[...]
    for start in range(0, model, CHUNK):
        dxmod_ref[:, start : start + CHUNK] = dot(dqkv, wqkv_ref[start : start + CHUNK, :], NT)

    def frame_step(frame, carry):
        clip = clip_ref[0, frame]
        scale = mod_ref[clip, pl.ds(1, 1), :]
        gate = mod_ref[clip, pl.ds(2, 1), :]
        valid = valid_patches(base, count_ref[0, clip], patches)
        where = pl.ds(pl.multiple_of(frame * patches, patches), patches)
        both_f = tokens_ref[frame].astype(jnp.float32)
        latent = both_f[:patches]
        block_out = latent + valid * gate * proj_ref[where, :]
        normed, inv_std = normalize(latent)
        dnorm = dxmod_ref[where, :] * (1.0 + scale)
        branch = inv_std * (
            dnorm
            - jnp.mean(dnorm, axis=-1, keepdims=True)
            - normed * jnp.mean(dnorm * normed, axis=-1, keepdims=True)
        )
        out_ref[frame] = jnp.concatenate(
            [block_out, both_f[patches:] + branch], axis=0
        ).astype(jnp.bfloat16)
        return carry

    lax.fori_loop(0, frames, frame_step, 0)


def smem():
    return pl.BlockSpec(memory_space=pltpu.SMEM)


def vmem():
    return pl.BlockSpec(memory_space=pltpu.VMEM)


def run_forward(frame_clip, clip_patches, place, tokens, modulation, qkv_weight, chips, held):
    frames, both, model = tokens.shape
    rows = frames * both // 2
    low = jnp.bfloat16
    return pl.pallas_call(
        forward_kernel,
        out_shape=(
            jax.ShapeDtypeStruct((rows, 3 * model), low),
            jax.ShapeDtypeStruct((HEADS, rows, rows), low),
            jax.ShapeDtypeStruct((rows, model), low),
            jax.ShapeDtypeStruct((rows, model), low),
            jax.ShapeDtypeStruct((2, chips, held, model), low),
        ),
        in_specs=[smem()] * 3 + [vmem()] * 3,
        out_specs=(vmem(),) * 5,
        scratch_shapes=[
            pltpu.VMEM((rows, model), low),
            pltpu.VMEM((rows, rows), jnp.float32),
            pltpu.VMEM((model + 16, model), jnp.float32),
        ],
        compiler_params=pltpu.CompilerParams(vmem_limit_bytes=48 * MIB),
        cost_estimate=pl.CostEstimate(
            flops=2 * rows * model * 4 * model, bytes_accessed=12 * MIB, transcendentals=0
        ),
        name="forward",
    )(frame_clip, clip_patches, place, tokens, modulation, qkv_weight)


def run_backward(
    frame_clip, clip_patches, place, tokens, modulation, qkv_weight, out_weight, qkv, prob, att, gdy
):
    frames, both, model = tokens.shape
    rows = frames * both // 2
    low = jnp.bfloat16
    return pl.pallas_call(
        backward_kernel,
        out_shape=jax.ShapeDtypeStruct((frames, both, model), low),
        in_specs=[smem()] * 3 + [vmem()] * 8,
        out_specs=vmem(),
        scratch_shapes=[
            pltpu.VMEM((rows, model), low),
            pltpu.VMEM((rows, 3 * model), low),
            pltpu.VMEM((rows, model), jnp.float32),
            pltpu.VMEM((rows, model), jnp.float32),
        ],
        compiler_params=pltpu.CompilerParams(vmem_limit_bytes=48 * MIB),
        cost_estimate=pl.CostEstimate(
            flops=2 * rows * model * 6 * model, bytes_accessed=16 * MIB, transcendentals=0
        ),
        name="backward",
    )(frame_clip, clip_patches, place, tokens, modulation, qkv_weight, out_weight, qkv, prob, att, gdy)


def per_device(latents, cotangent, qkv_weight, out_weight, modulation, frame_clip, clip_patches):
    seq = lax.axis_size("seq")
    groups = lax.axis_size("dp")
    chips = seq // 2
    patches, model = latents.shape[2], latents.shape[3]
    mine = patches // seq
    share = model // seq
    held = -(-share // 8) * 8
    index = lax.axis_index("seq")
    place = jnp.stack([index * mine, index % 2]).astype(jnp.int32)

    outgoing = jnp.concatenate(
        [latents.reshape(seq, mine, model), cotangent.reshape(seq, mine, model)], axis=1
    )
    tokens = lax.all_to_all(outgoing, "seq", 0, 0, tiled=True)
    qkv, prob, att, gdy, grad = run_forward(
        frame_clip, clip_patches, place, tokens, modulation[0], qkv_weight, chips, held
    )
    other = lax.ppermute(grad[1], "seq", [(i, i ^ 1) for i in range(seq)])
    pair = (grad[0].astype(jnp.float32) + other.astype(jnp.float32)).astype(jnp.bfloat16)
    same_core = [[2 * chip + core for chip in range(chips)] for core in range(2)]
    terms = lax.all_to_all(pair, "seq", 0, 0, tiled=True, axis_index_groups=same_core)
    results = run_backward(
        frame_clip, clip_patches, place, tokens, modulation[0], qkv_weight, out_weight,
        qkv, prob, att, gdy,
    )
    returned = lax.all_to_all(results, "seq", 0, 0, tiled=True)
    block_out = returned[:, :mine].reshape(latents.shape)
    latent_grad = returned[:, mine:].reshape(latents.shape)
    own = jnp.sum(terms.astype(jnp.float32), axis=0).astype(jnp.bfloat16)
    total = own.astype(jnp.float32)
    for step in range(1, groups):
        total = total + lax.ppermute(
            own, "dp", [(i, (i + step) % groups) for i in range(groups)]
        ).astype(jnp.float32)
    return block_out, latent_grad, total[:share]


def solution(mesh):
    in_specs = (
        P("dp", "seq", None, None),
        P("dp", "seq", None, None),
        P(),
        P(),
        P("dp", None, None, None),
        P("dp", None),
        P("dp", None),
    )
    out_specs = (P("dp", "seq", None, None), P("dp", "seq", None, None), P("seq", None))
    return jax.shard_map(
        per_device, mesh=mesh, in_specs=in_specs, out_specs=out_specs, check_vma=False
    )
```

```python
import jax
import jax.numpy as jnp
from jax import lax
from jax.experimental import pallas as pl
from jax.experimental.pallas import tpu as pltpu
from jax.sharding import PartitionSpec as P

HEADS = 16
LANES = 128
CHUNK = 384
MIB = 1024 * 1024

NN = (((1,), (0,)), ((), ()))
NT = (((1,), (1,)), ((), ()))
TN = (((0,), (0,)), ((), ()))


def dot(left, right, dims):
    return lax.dot_general(left, right, dims, preferred_element_type=jnp.float32)


def head_span(head, head_dim):
    first, last = head * head_dim, (head + 1) * head_dim
    low = first // LANES * LANES
    high = -(-last // LANES) * LANES
    return first, last, low, high


def head_mask(first, last, low, high):
    lane = lax.broadcasted_iota(jnp.int32, (1, high - low), 1) + low
    return jnp.where((lane >= first) & (lane < last), 1.0, 0.0).astype(jnp.bfloat16)


def add_tiles(parts, low, value):
    for start in range(0, value.shape[1], LANES):
        tile = (low + start) // LANES
        piece = value[:, start : start + LANES]
        parts[tile] = parts[tile] + piece if tile in parts else piece


def flush_tiles(parts, done, store):
    for tile in sorted(parts):
        if (tile + 1) * LANES <= done:
            store(tile * LANES, parts.pop(tile))


def normalize(tokens):
    center = tokens - jnp.mean(tokens, axis=-1, keepdims=True)
    spread = jnp.mean(center * center, axis=-1, keepdims=True)
    inv_std = lax.rsqrt(spread + 1e-06)
    return center * inv_std, inv_std


def valid_patches(base, count, patches):
    index = base + lax.broadcasted_iota(jnp.int32, (patches, 1), 0)
    return (index < count).astype(jnp.float32)


def forward_kernel(
    clip_ref, count_ref, place_ref,
    tokens_ref, mod_ref, wqkv_ref,
    qkv_ref, prob_ref, att_ref, gdy_ref, keep_ref, send_ref,
    xmod_ref, same_ref, sum_ref,
):
    frames, both, model = tokens_ref.shape
    patches = both // 2
    rows = frames * patches
    head_dim = model // HEADS
    base = place_ref[0]
    core = place_ref[1]

    def pair_step(step, carry):
        xmods, gdys = [], []
        for k in range(2):
            frame = 2 * step + k
            clip = clip_ref[0, frame]
            shift = mod_ref[0, pl.ds(clip, 1), :]
            scale = mod_ref[1, pl.ds(clip, 1), :]
            gate = mod_ref[2, pl.ds(clip, 1), :]
            both_f = tokens_ref[frame].astype(jnp.float32)
            normed, _ = normalize(both_f[:patches])
            xmods.append(normed * (1.0 + scale) + shift)
            valid = valid_patches(base, count_ref[0, clip], patches)
            gdys.append(valid * gate * both_f[patches:])
        where = pl.ds(pl.multiple_of(step * both, both), both)
        xmod_ref[where, :] = jnp.concatenate(xmods, axis=0).astype(jnp.bfloat16)
        gdy_ref[where, :] = jnp.concatenate(gdys, axis=0).astype(jnp.bfloat16)
        return carry

    lax.fori_loop(0, frames // 2, pair_step, 0, unroll=4)

    starts = []
    for clip in range(1, mod_ref.shape[1]):
        start = jnp.int32(0)
        for frame in range(frames):
            start = start + jnp.where(clip_ref[0, frame] < clip, 1, 0)
        starts.append(start)

    def key_of(index):
        frame = index // patches
        key = index % patches
        for start in starts:
            key = key + jnp.where(frame >= start, patches, 0)
        return key

    key_e = key_of(lax.broadcasted_iota(jnp.int32, (rows, 1), 0))
    key_f = key_of(lax.broadcasted_iota(jnp.int32, (1, rows), 1))
    same_ref[...] = (key_e == key_f).astype(jnp.float32)

    xmod = xmod_ref[...]
    for start in range(0, 3 * model, CHUNK):
        qkv_ref[:, start : start + CHUNK] = dot(
            xmod, wqkv_ref[:, start : start + CHUNK], NN
        ).astype(jnp.bfloat16)

    def store_att(low, value):
        att_ref[:, low : low + LANES] = value.astype(jnp.bfloat16)

    parts = {}
    for head in range(HEADS):
        first, last, low, high = head_span(head, head_dim)
        mask = head_mask(first, last, low, high)
        query = qkv_ref[:, low:high] * mask
        key = qkv_ref[:, model + low : model + high]
        value = qkv_ref[:, 2 * model + low : 2 * model + high] * mask
        expo = jnp.exp(dot(key, query, NT) * head_dim ** (-0.5)) * same_ref[...]
        prob = (expo * (1.0 / jnp.sum(expo, axis=0, keepdims=True))).astype(jnp.bfloat16)
        prob_ref[head] = prob
        add_tiles(parts, low, dot(prob, value, TN))
        flush_tiles(parts, last, store_att)

    att = att_ref[...]
    for start in range(0, model, LANES):
        sum_ref[start : start + LANES, :] = dot(gdy_ref[:, start : start + LANES], att, TN)
    chips, held, _ = keep_ref.shape
    share = model // (2 * chips)
    for side in range(2):

        def store_share(target_ref, side=side):
            for chip in range(chips):
                start = (2 * chip + side) * share
                target_ref[chip] = sum_ref[start : start + held, :].astype(jnp.bfloat16)

        pl.when(core == side)(lambda: store_share(keep_ref))
        pl.when(core != side)(lambda: store_share(send_ref))


def backward_kernel(
    clip_ref, count_ref, place_ref,
    tokens_ref, mod_ref, wqkv_ref, wout_ref, qkv_ref, prob_ref, att_ref, gdy_ref,
    out_ref,
    datt_ref, dqkv_ref, proj_ref, dxmod_ref,
):
    frames, both, model = tokens_ref.shape
    patches = both // 2
    head_dim = model // HEADS
    att_scale = head_dim ** (-0.5)
    base = place_ref[0]

    gdy = gdy_ref[...]
    att = att_ref[...]
    for start in range(0, model, CHUNK):
        datt_ref[:, start : start + CHUNK] = dot(
            gdy, wout_ref[start : start + CHUNK, :], NT
        ).astype(jnp.bfloat16)
    for start in range(0, model, CHUNK):
        proj_ref[:, start : start + CHUNK] = dot(att, wout_ref[:, start : start + CHUNK], NN)

    def store_at(offset, factor):
        def store(low, value):
            dqkv_ref[:, offset + low : offset + low + LANES] = (value * factor).astype(jnp.bfloat16)
        return store

    parts_q, parts_k, parts_v = {}, {}, {}
    for head in range(HEADS):
        first, last, low, high = head_span(head, head_dim)
        mask = head_mask(first, last, low, high)
        query = qkv_ref[:, low:high] * mask
        key = qkv_ref[:, model + low : model + high] * mask
        value = qkv_ref[:, 2 * model + low : 2 * model + high]
        datt = datt_ref[:, low:high] * mask
        prob_low = prob_ref[head]
        add_tiles(parts_v, low, dot(prob_low, datt, NN))
        prob = prob_low.astype(jnp.float32)
        dprob = dot(value, datt, NT)
        total = jnp.sum(prob * dprob, axis=0, keepdims=True)
        dscore = (prob * (dprob - total)).astype(jnp.bfloat16)
        add_tiles(parts_k, low, dot(dscore, query, NN))
        add_tiles(parts_q, low, dot(dscore, key, TN))
        flush_tiles(parts_q, last, store_at(0, att_scale))
        flush_tiles(parts_k, last, store_at(model, att_scale))
        flush_tiles(parts_v, last, store_at(2 * model, 1.0))

    dqkv = dqkv_ref[...]
    for start in range(0, model, CHUNK):
        dxmod_ref[:, start : start + CHUNK] = dot(dqkv, wqkv_ref[start : start + CHUNK, :], NT)

    def frame_step(frame, carry):
        clip = clip_ref[0, frame]
        scale = mod_ref[1, pl.ds(clip, 1), :]
        gate = mod_ref[2, pl.ds(clip, 1), :]
        valid = valid_patches(base, count_ref[0, clip], patches)
        where = pl.ds(pl.multiple_of(frame * patches, patches), patches)
        both_f = tokens_ref[frame].astype(jnp.float32)
        latent = both_f[:patches]
        block_out = latent + valid * gate * proj_ref[where, :]
        normed, inv_std = normalize(latent)
        dnorm = dxmod_ref[where, :] * (1.0 + scale)
        branch = inv_std * (
            dnorm
            - jnp.mean(dnorm, axis=-1, keepdims=True)
            - normed * jnp.mean(dnorm * normed, axis=-1, keepdims=True)
        )
        out_ref[frame] = jnp.concatenate(
            [block_out, both_f[patches:] + branch], axis=0
        ).astype(jnp.bfloat16)
        return carry

    lax.fori_loop(0, frames, frame_step, 0, unroll=8)


def smem():
    return pl.BlockSpec(memory_space=pltpu.SMEM)


def vmem():
    return pl.BlockSpec(memory_space=pltpu.VMEM)


def run_forward(frame_clip, clip_patches, place, tokens, modulation, qkv_weight, chips, held):
    frames, both, model = tokens.shape
    rows = frames * both // 2
    low = jnp.bfloat16
    return pl.pallas_call(
        forward_kernel,
        out_shape=(
            jax.ShapeDtypeStruct((rows, 3 * model), low),
            jax.ShapeDtypeStruct((HEADS, rows, rows), low),
            jax.ShapeDtypeStruct((rows, model), low),
            jax.ShapeDtypeStruct((rows, model), low),
            jax.ShapeDtypeStruct((chips, held, model), low),
            jax.ShapeDtypeStruct((chips, held, model), low),
        ),
        in_specs=[smem()] * 3 + [vmem()] * 3,
        out_specs=(vmem(),) * 6,
        scratch_shapes=[
            pltpu.VMEM((rows, model), low),
            pltpu.VMEM((rows, rows), jnp.float32),
            pltpu.VMEM((model + 16, model), jnp.float32),
        ],
        compiler_params=pltpu.CompilerParams(vmem_limit_bytes=30 * MIB),
        cost_estimate=pl.CostEstimate(
            flops=2 * rows * model * 4 * model, bytes_accessed=12 * MIB, transcendentals=0
        ),
        name="forward",
    )(frame_clip, clip_patches, place, tokens, modulation, qkv_weight)


def run_backward(
    frame_clip, clip_patches, place, tokens, modulation, qkv_weight, out_weight, qkv, prob, att, gdy
):
    frames, both, model = tokens.shape
    rows = frames * both // 2
    low = jnp.bfloat16
    return pl.pallas_call(
        backward_kernel,
        out_shape=jax.ShapeDtypeStruct((frames, both, model), low),
        in_specs=[smem()] * 3 + [vmem()] * 8,
        out_specs=vmem(),
        scratch_shapes=[
            pltpu.VMEM((rows, model), low),
            pltpu.VMEM((rows, 3 * model), low),
            pltpu.VMEM((rows, model), jnp.float32),
            pltpu.VMEM((rows, model), jnp.float32),
        ],
        compiler_params=pltpu.CompilerParams(vmem_limit_bytes=30 * MIB),
        cost_estimate=pl.CostEstimate(
            flops=2 * rows * model * 6 * model, bytes_accessed=16 * MIB, transcendentals=0
        ),
        name="backward",
    )(frame_clip, clip_patches, place, tokens, modulation, qkv_weight, out_weight, qkv, prob, att, gdy)


def finish_kernel(returned_ref, own_ref, *refs):
    other_refs, (block_ref, latent_ref, grad_ref) = refs[:-3], refs[-3:]
    groups, both, _ = returned_ref.shape
    patches = both // 2
    for step in range(groups // 2):
        pair = [returned_ref[2 * step + k].astype(jnp.float32) for k in range(2)]
        where = slice(step * both, (step + 1) * both)
        block_ref[where, :] = jnp.concatenate([part[:patches] for part in pair], axis=0).astype(
            jnp.bfloat16
        )
        latent_ref[where, :] = jnp.concatenate([part[patches:] for part in pair], axis=0).astype(
            jnp.bfloat16
        )
    total = own_ref[...].astype(jnp.float32)
    for other_ref in other_refs:
        total = total + other_ref[...].astype(jnp.float32)
    grad_ref[...] = total[: grad_ref.shape[0]]


def run_finish(returned, own, others, share):
    groups, both, model = returned.shape
    low = jnp.bfloat16
    rows = groups * both // 2
    return pl.pallas_call(
        finish_kernel,
        out_shape=(
            jax.ShapeDtypeStruct((rows, model), low),
            jax.ShapeDtypeStruct((rows, model), low),
            jax.ShapeDtypeStruct((share, model), jnp.float32),
        ),
        in_specs=[vmem()] * (2 + len(others)),
        out_specs=(vmem(),) * 3,
        compiler_params=pltpu.CompilerParams(vmem_limit_bytes=12 * MIB),
        cost_estimate=pl.CostEstimate(flops=0, bytes_accessed=4 * MIB, transcendentals=0),
        name="finish",
    )(returned, own, *others)


def per_device(latents, cotangent, qkv_weight, out_weight, modulation, frame_clip, clip_patches):
    seq = lax.axis_size("seq")
    groups = lax.axis_size("dp")
    chips = seq // 2
    patches, model = latents.shape[2], latents.shape[3]
    mine = patches // seq
    share = model // seq
    held = -(-share // 8) * 8
    index = lax.axis_index("seq")
    place = jnp.stack([index * mine, index % 2]).astype(jnp.int32)

    outgoing = jnp.concatenate(
        [latents.reshape(seq, mine, model), cotangent.reshape(seq, mine, model)], axis=1
    )
    tokens = lax.all_to_all(outgoing, "seq", 0, 0, tiled=True)
    mod = modulation[0].transpose(1, 0, 2)
    qkv, prob, att, gdy, keep, send = run_forward(
        frame_clip, clip_patches, place, tokens, mod, qkv_weight, chips, held
    )
    other = lax.ppermute(send, "seq", [(i, i ^ 1) for i in range(seq)])
    pair = (keep.astype(jnp.float32) + other.astype(jnp.float32)).astype(jnp.bfloat16)
    same_core = [[2 * chip + core for chip in range(chips)] for core in range(2)]
    terms = lax.all_to_all(pair, "seq", 0, 0, tiled=True, axis_index_groups=same_core)
    results = run_backward(
        frame_clip, clip_patches, place, tokens, mod, qkv_weight, out_weight, qkv, prob, att, gdy
    )
    own = jnp.sum(terms.astype(jnp.float32), axis=0).astype(jnp.bfloat16)
    others = [
        lax.ppermute(own, "dp", [(i, (i + step) % groups) for i in range(groups)])
        for step in range(1, groups)
    ]
    returned = lax.all_to_all(results, "seq", 0, 0, tiled=True)
    block_out, latent_grad, total = run_finish(returned, own, others, share)
    return block_out.reshape(latents.shape), latent_grad.reshape(latents.shape), total


def solution(mesh):
    in_specs = (
        P("dp", "seq", None, None),
        P("dp", "seq", None, None),
        P(),
        P(),
        P("dp", None, None, None),
        P("dp", None),
        P("dp", None),
    )
    out_specs = (P("dp", "seq", None, None), P("dp", "seq", None, None), P("seq", None))
    return jax.shard_map(
        per_device, mesh=mesh, in_specs=in_specs, out_specs=out_specs, check_vma=False
    )
```

```python
import jax
import jax.numpy as jnp
from jax import lax
from jax.experimental import pallas as pl
from jax.experimental.pallas import tpu as pltpu
from jax.sharding import PartitionSpec as P

HEADS = 16
LANES = 128
CHUNK = 384
SHARE_ROWS = 40
MIB = 1024 * 1024

NN = (((1,), (0,)), ((), ()))
NT = (((1,), (1,)), ((), ()))
TN = (((0,), (0,)), ((), ()))


def dot(left, right, dims):
    return lax.dot_general(left, right, dims, preferred_element_type=jnp.float32)


def head_span(head, head_dim):
    first, last = head * head_dim, (head + 1) * head_dim
    low = first // LANES * LANES
    high = -(-last // LANES) * LANES
    return first, last, low, high


def head_mask(first, last, low, high):
    lane = lax.broadcasted_iota(jnp.int32, (1, high - low), 1) + low
    return jnp.where((lane >= first) & (lane < last), 1.0, 0.0).astype(jnp.bfloat16)


def add_tiles(parts, low, value):
    for start in range(0, value.shape[1], LANES):
        tile = (low + start) // LANES
        piece = value[:, start : start + LANES]
        parts[tile] = parts[tile] + piece if tile in parts else piece


def flush_tiles(parts, done, store):
    for tile in sorted(parts):
        if (tile + 1) * LANES <= done:
            store(tile * LANES, parts.pop(tile))


def normalize(tokens):
    center = tokens - jnp.mean(tokens, axis=-1, keepdims=True)
    spread = jnp.mean(center * center, axis=-1, keepdims=True)
    inv_std = lax.rsqrt(spread + 1e-06)
    return center * inv_std, inv_std


def valid_patches(base, count, patches):
    index = base + lax.broadcasted_iota(jnp.int32, (patches, 1), 0)
    return (index < count).astype(jnp.float32)


def forward_kernel(
    clip_ref, count_ref, place_ref, tokens_ref, mod_ref, wqkv_hbm,
    qkv_hbm, prob_hbm, att_hbm, gdy_hbm, keep_ref, send_ref,
    wqkv_ref, qkv_ref, prob_ref, att_ref, gdy_ref, xmod_ref, same_ref, turned_ref, share_ref,
    load_sems, store_sems,
):
    frames, both, model = tokens_ref.shape
    patches = both // 2
    rows = frames * patches
    head_dim = model // HEADS
    base = place_ref[0]
    core = place_ref[1]

    loads = []
    for step, start in enumerate(range(0, 3 * model, CHUNK)):
        columns = slice(start, start + CHUNK)
        load = pltpu.make_async_copy(
            wqkv_hbm.at[:, columns], wqkv_ref.at[:, columns], load_sems.at[step]
        )
        load.start()
        loads.append(load)

    def pair_step(step, carry):
        xmods, gdys = [], []
        for k in range(2):
            frame = 2 * step + k
            clip = clip_ref[0, frame]
            shift = mod_ref[0, pl.ds(clip, 1), :]
            scale = mod_ref[1, pl.ds(clip, 1), :]
            gate = mod_ref[2, pl.ds(clip, 1), :]
            both_f = tokens_ref[frame].astype(jnp.float32)
            normed, _ = normalize(both_f[:patches])
            xmods.append(normed * (1.0 + scale) + shift)
            valid = valid_patches(base, count_ref[0, clip], patches)
            gdys.append(valid * gate * both_f[patches:])
        where = pl.ds(pl.multiple_of(step * both, both), both)
        xmod_ref[where, :] = jnp.concatenate(xmods, axis=0).astype(jnp.bfloat16)
        gdy_ref[where, :] = jnp.concatenate(gdys, axis=0).astype(jnp.bfloat16)
        return carry

    lax.fori_loop(0, frames // 2, pair_step, 0, unroll=4)

    stores = []

    def store_out(source_ref, target_hbm):
        store = pltpu.make_async_copy(source_ref, target_hbm, store_sems.at[len(stores)])
        store.start()
        stores.append(store)

    store_out(gdy_ref, gdy_hbm)

    starts = []
    for clip in range(1, mod_ref.shape[1]):
        start = jnp.int32(0)
        for frame in range(frames):
            start = start + jnp.where(clip_ref[0, frame] < clip, 1, 0)
        starts.append(start)

    def key_of(index):
        frame = index // patches
        key = index % patches
        for start in starts:
            key = key + jnp.where(frame >= start, patches, 0)
        return key

    key_e = key_of(lax.broadcasted_iota(jnp.int32, (rows, 1), 0))
    key_f = key_of(lax.broadcasted_iota(jnp.int32, (1, rows), 1))
    same_ref[...] = (key_e == key_f).astype(jnp.float32)

    chips, held = share_ref.shape[1] // SHARE_ROWS, SHARE_ROWS
    share = model // (2 * chips)
    for start in range(0, model, LANES):
        turned_ref[start : start + LANES, :] = gdy_ref[:, start : start + LANES].astype(
            jnp.float32
        ).T
    turned_ref[model:, :] = jnp.zeros((turned_ref.shape[0] - model, rows), jnp.float32)
    for side in range(2):
        for chip in range(0, chips, 2):
            pieces = []
            for k in range(2):
                start = (2 * (chip + k) + side) * share
                pieces.append(turned_ref[start : start + held, :])
            share_ref[side, chip * held : (chip + 2) * held, :] = jnp.concatenate(
                pieces, axis=0
            ).astype(jnp.bfloat16)

    xmod = xmod_ref[...]
    for step, start in enumerate(range(0, 3 * model, CHUNK)):
        loads[step].wait()
        qkv_ref[:, start : start + CHUNK] = dot(
            xmod, wqkv_ref[:, start : start + CHUNK], NN
        ).astype(jnp.bfloat16)
    store_out(qkv_ref, qkv_hbm)

    def store_att(low, value):
        att_ref[:, low : low + LANES] = value.astype(jnp.bfloat16)

    parts = {}
    for head in range(HEADS):
        first, last, low, high = head_span(head, head_dim)
        mask = head_mask(first, last, low, high)
        query = qkv_ref[:, low:high] * mask
        key = qkv_ref[:, model + low : model + high]
        value = qkv_ref[:, 2 * model + low : 2 * model + high] * mask
        expo = jnp.exp(dot(key, query, NT) * head_dim ** (-0.5)) * same_ref[...]
        prob = (expo * (1.0 / jnp.sum(expo, axis=0, keepdims=True))).astype(jnp.bfloat16)
        prob_ref[head] = prob
        add_tiles(parts, low, dot(prob, value, TN))
        flush_tiles(parts, last, store_att)
    store_out(att_ref, att_hbm)
    store_out(prob_ref, prob_hbm)

    for target_ref, side in ((send_ref, 1 - core), (keep_ref, core)):
        for start in range(0, model, CHUNK):
            target_ref[:, start : start + CHUNK] = dot(
                share_ref[side], att_ref[:, start : start + CHUNK], NN
            ).astype(jnp.bfloat16)
    for store in stores:
        store.wait()


def backward_kernel(
    clip_ref, count_ref, place_ref, tokens_ref, mod_ref,
    gdy_hbm, wout_hbm, att_hbm, qkv_hbm, prob_hbm, wqkv_hbm,
    out_ref,
    gdy_ref, wout_ref, att_ref, qkv_ref, prob_ref, wqkv_ref,
    datt_ref, dqkv_ref, proj_ref, dxmod_ref, sems,
):
    frames, both, model = tokens_ref.shape
    patches = both // 2
    head_dim = model // HEADS
    att_scale = head_dim ** (-0.5)
    base = place_ref[0]

    loads = []
    for source_hbm, target_ref in (
        (gdy_hbm, gdy_ref), (wout_hbm, wout_ref), (att_hbm, att_ref),
        (qkv_hbm, qkv_ref), (prob_hbm, prob_ref), (wqkv_hbm, wqkv_ref),
    ):
        load = pltpu.make_async_copy(source_hbm, target_ref, sems.at[len(loads)])
        load.start()
        loads.append(load)

    loads[0].wait()
    loads[1].wait()
    gdy = gdy_ref[...]
    for start in range(0, model, CHUNK):
        datt_ref[:, start : start + CHUNK] = dot(
            gdy, wout_ref[start : start + CHUNK, :], NT
        ).astype(jnp.bfloat16)
    loads[2].wait()
    att = att_ref[...]
    for start in range(0, model, CHUNK):
        proj_ref[:, start : start + CHUNK] = dot(att, wout_ref[:, start : start + CHUNK], NN)
    loads[3].wait()
    loads[4].wait()

    def store_at(offset, factor):
        def store(low, value):
            dqkv_ref[:, offset + low : offset + low + LANES] = (value * factor).astype(jnp.bfloat16)
        return store

    parts_q, parts_k, parts_v = {}, {}, {}
    for head in range(HEADS):
        first, last, low, high = head_span(head, head_dim)
        mask = head_mask(first, last, low, high)
        query = qkv_ref[:, low:high] * mask
        key = qkv_ref[:, model + low : model + high] * mask
        value = qkv_ref[:, 2 * model + low : 2 * model + high]
        datt = datt_ref[:, low:high] * mask
        prob_low = prob_ref[head]
        add_tiles(parts_v, low, dot(prob_low, datt, NN))
        prob = prob_low.astype(jnp.float32)
        dprob = dot(value, datt, NT)
        total = jnp.sum(prob * dprob, axis=0, keepdims=True)
        dscore = (prob * (dprob - total)).astype(jnp.bfloat16)
        add_tiles(parts_k, low, dot(dscore, query, NN))
        add_tiles(parts_q, low, dot(dscore, key, TN))
        flush_tiles(parts_q, last, store_at(0, att_scale))
        flush_tiles(parts_k, last, store_at(model, att_scale))
        flush_tiles(parts_v, last, store_at(2 * model, 1.0))

    loads[5].wait()
    dqkv = dqkv_ref[...]
    for start in range(0, model, CHUNK):
        dxmod_ref[:, start : start + CHUNK] = dot(dqkv, wqkv_ref[start : start + CHUNK, :], NT)

    def frame_step(frame, carry):
        clip = clip_ref[0, frame]
        scale = mod_ref[1, pl.ds(clip, 1), :]
        gate = mod_ref[2, pl.ds(clip, 1), :]
        valid = valid_patches(base, count_ref[0, clip], patches)
        where = pl.ds(pl.multiple_of(frame * patches, patches), patches)
        both_f = tokens_ref[frame].astype(jnp.float32)
        latent = both_f[:patches]
        block_out = latent + valid * gate * proj_ref[where, :]
        normed, inv_std = normalize(latent)
        dnorm = dxmod_ref[where, :] * (1.0 + scale)
        branch = inv_std * (
            dnorm
            - jnp.mean(dnorm, axis=-1, keepdims=True)
            - normed * jnp.mean(dnorm * normed, axis=-1, keepdims=True)
        )
        out_ref[frame] = jnp.concatenate(
            [block_out, both_f[patches:] + branch], axis=0
        ).astype(jnp.bfloat16)
        return carry

    lax.fori_loop(0, frames, frame_step, 0, unroll=8)


def smem():
    return pl.BlockSpec(memory_space=pltpu.SMEM)


def vmem():
    return pl.BlockSpec(memory_space=pltpu.VMEM)


def hbm():
    return pl.BlockSpec(memory_space=pltpu.HBM)


def run_forward(frame_clip, clip_patches, place, tokens, modulation, qkv_weight, chips):
    frames, both, model = tokens.shape
    rows = frames * both // 2
    low = jnp.bfloat16
    sizes = ((rows, 3 * model), (HEADS, rows, rows), (rows, model), (rows, model))
    return pl.pallas_call(
        forward_kernel,
        out_shape=tuple(jax.ShapeDtypeStruct(size, low) for size in sizes)
        + (jax.ShapeDtypeStruct((chips * SHARE_ROWS, model), low),) * 2,
        in_specs=[smem()] * 3 + [vmem()] * 2 + [hbm()],
        out_specs=(hbm(),) * 4 + (vmem(),) * 2,
        scratch_shapes=[pltpu.VMEM((model, 3 * model), low)]
        + [pltpu.VMEM(size, low) for size in sizes]
        + [
            pltpu.VMEM((rows, model), low),
            pltpu.VMEM((rows, rows), jnp.float32),
            pltpu.VMEM((model + 16, rows), jnp.float32),
            pltpu.VMEM((2, chips * SHARE_ROWS, rows), low),
            pltpu.SemaphoreType.DMA((3 * model // CHUNK,)),
            pltpu.SemaphoreType.DMA((4,)),
        ],
        compiler_params=pltpu.CompilerParams(vmem_limit_bytes=32 * MIB),
        cost_estimate=pl.CostEstimate(
            flops=2 * rows * model * 4 * model, bytes_accessed=12 * MIB, transcendentals=0
        ),
        name="forward",
    )(frame_clip, clip_patches, place, tokens, modulation, qkv_weight)


def run_backward(
    frame_clip, clip_patches, place, tokens, modulation, gdy, out_weight, att, qkv, prob, qkv_weight
):
    frames, both, model = tokens.shape
    rows = frames * both // 2
    low = jnp.bfloat16
    loaded = (gdy, out_weight, att, qkv, prob, qkv_weight)
    return pl.pallas_call(
        backward_kernel,
        out_shape=jax.ShapeDtypeStruct((frames, both, model), low),
        in_specs=[smem()] * 3 + [vmem()] * 2 + [hbm()] * len(loaded),
        out_specs=vmem(),
        scratch_shapes=[pltpu.VMEM(array.shape, low) for array in loaded]
        + [
            pltpu.VMEM((rows, model), low),
            pltpu.VMEM((rows, 3 * model), low),
            pltpu.VMEM((rows, model), jnp.float32),
            pltpu.VMEM((rows, model), jnp.float32),
            pltpu.SemaphoreType.DMA((len(loaded),)),
        ],
        compiler_params=pltpu.CompilerParams(vmem_limit_bytes=32 * MIB),
        cost_estimate=pl.CostEstimate(
            flops=2 * rows * model * 6 * model, bytes_accessed=16 * MIB, transcendentals=0
        ),
        name="backward",
    )(frame_clip, clip_patches, place, tokens, modulation, *loaded)


def pack_kernel(latent_ref, cotangent_ref, out_ref):
    both = out_ref.shape[1]
    patches = both // 2
    for step in range(out_ref.shape[0] // 2):
        where = slice(step * both, (step + 1) * both)
        latent = latent_ref[where, :].astype(jnp.float32)
        cotangent = cotangent_ref[where, :].astype(jnp.float32)
        for k in range(2):
            half = slice(k * patches, (k + 1) * patches)
            out_ref[2 * step + k] = jnp.concatenate([latent[half], cotangent[half]], axis=0).astype(
                jnp.bfloat16
            )


def run_pack(latents, cotangent, seq):
    rows, model = latents.shape
    return pl.pallas_call(
        pack_kernel,
        out_shape=jax.ShapeDtypeStruct((seq, 2 * rows // seq, model), jnp.bfloat16),
        in_specs=[vmem()] * 2,
        out_specs=vmem(),
        compiler_params=pltpu.CompilerParams(vmem_limit_bytes=12 * MIB),
        name="pack",
    )(latents, cotangent)


def add_kernel(left_ref, right_ref, out_ref):
    step_rows = 64
    for start in range(0, left_ref.shape[0], step_rows):
        where = slice(start, start + step_rows)
        out_ref[where, :] = (
            left_ref[where, :].astype(jnp.float32) + right_ref[where, :].astype(jnp.float32)
        ).astype(jnp.bfloat16)


def run_add(left, right):
    return pl.pallas_call(
        add_kernel,
        out_shape=jax.ShapeDtypeStruct(left.shape, left.dtype),
        in_specs=[vmem()] * 2,
        out_specs=vmem(),
        compiler_params=pltpu.CompilerParams(vmem_limit_bytes=12 * MIB),
        name="add",
    )(left, right)


def finish_kernel(returned_ref, left_ref, right_ref, block_ref, latent_ref, grad_ref):
    groups, both, _ = returned_ref.shape
    patches = both // 2
    for step in range(groups // 2):
        pair = [returned_ref[2 * step + k].astype(jnp.float32) for k in range(2)]
        where = slice(step * both, (step + 1) * both)
        block_ref[where, :] = jnp.concatenate([part[:patches] for part in pair], axis=0).astype(
            jnp.bfloat16
        )
        latent_ref[where, :] = jnp.concatenate([part[patches:] for part in pair], axis=0).astype(
            jnp.bfloat16
        )
    total = left_ref[...].astype(jnp.float32) + right_ref[...].astype(jnp.float32)
    grad_ref[...] = total[: grad_ref.shape[0]]


def run_finish(returned, left, right, share):
    groups, both, model = returned.shape
    low = jnp.bfloat16
    rows = groups * both // 2
    return pl.pallas_call(
        finish_kernel,
        out_shape=(
            jax.ShapeDtypeStruct((rows, model), low),
            jax.ShapeDtypeStruct((rows, model), low),
            jax.ShapeDtypeStruct((share, model), jnp.float32),
        ),
        in_specs=[vmem()] * 3,
        out_specs=(vmem(),) * 3,
        compiler_params=pltpu.CompilerParams(vmem_limit_bytes=12 * MIB),
        cost_estimate=pl.CostEstimate(flops=0, bytes_accessed=4 * MIB, transcendentals=0),
        name="finish",
    )(returned, left, right)


def per_device(latents, cotangent, qkv_weight, out_weight, modulation, frame_clip, clip_patches):
    seq = lax.axis_size("seq")
    groups = lax.axis_size("dp")
    chips = seq // 2
    patches, model = latents.shape[2], latents.shape[3]
    mine = patches // seq
    share = model // seq
    index = lax.axis_index("seq")
    place = jnp.stack([index * mine, index % 2]).astype(jnp.int32)

    outgoing = run_pack(latents.reshape(patches, model), cotangent.reshape(patches, model), seq)
    tokens = lax.all_to_all(outgoing, "seq", 0, 0, tiled=True)
    mod = modulation[0].transpose(1, 0, 2)
    qkv, prob, att, gdy, keep, send = run_forward(
        frame_clip, clip_patches, place, tokens, mod, qkv_weight, chips
    )
    other = lax.ppermute(send, "seq", [(i, i ^ 1) for i in range(seq)])
    pair = run_add(keep, other).reshape(chips, SHARE_ROWS, model)
    same_core = [[2 * chip + core for chip in range(chips)] for core in range(2)]
    terms = lax.all_to_all(pair, "seq", 0, 0, tiled=True, axis_index_groups=same_core)
    results = run_backward(
        frame_clip, clip_patches, place, tokens, mod, gdy, out_weight, att, qkv, prob, qkv_weight
    )
    total = jnp.sum(terms.astype(jnp.float32), axis=0).astype(jnp.bfloat16)
    stride = 1
    while True:
        met = lax.ppermute(total, "dp", [(i, i ^ stride) for i in range(groups)])
        stride *= 2
        if stride >= groups:
            break
        total = (total.astype(jnp.float32) + met.astype(jnp.float32)).astype(jnp.bfloat16)
    returned = lax.all_to_all(results, "seq", 0, 0, tiled=True)
    block_out, latent_grad, grad = run_finish(returned, total, met, share)
    return block_out.reshape(latents.shape), latent_grad.reshape(latents.shape), grad


def solution(mesh):
    in_specs = (
        P("dp", "seq", None, None),
        P("dp", "seq", None, None),
        P(),
        P(),
        P("dp", None, None, None),
        P("dp", None),
        P("dp", None),
    )
    out_specs = (P("dp", "seq", None, None), P("dp", "seq", None, None), P("seq", None))
    return jax.shard_map(
        per_device, mesh=mesh, in_specs=in_specs, out_specs=out_specs, check_vma=False
    )
```

```python
import jax
import jax.numpy as jnp
from jax import lax
from jax.experimental import pallas as pl
from jax.experimental.pallas import tpu as pltpu
from jax.sharding import PartitionSpec as P

HEADS = 16
LANES = 128
CHUNK = 384
SHARE_ROWS = 40
MIB = 1024 * 1024

NN = (((1,), (0,)), ((), ()))
NT = (((1,), (1,)), ((), ()))
TN = (((0,), (0,)), ((), ()))


def dot(left, right, dims):
    return lax.dot_general(left, right, dims, preferred_element_type=jnp.float32)


def head_span(head, head_dim):
    first, last = head * head_dim, (head + 1) * head_dim
    low = first // LANES * LANES
    high = -(-last // LANES) * LANES
    return first, last, low, high


def head_mask(first, last, low, high):
    lane = lax.broadcasted_iota(jnp.int32, (1, high - low), 1) + low
    return jnp.where((lane >= first) & (lane < last), 1.0, 0.0).astype(jnp.bfloat16)


def add_tiles(parts, low, value):
    for start in range(0, value.shape[1], LANES):
        tile = (low + start) // LANES
        piece = value[:, start : start + LANES]
        parts[tile] = parts[tile] + piece if tile in parts else piece


def flush_tiles(parts, done, store):
    for tile in sorted(parts):
        if (tile + 1) * LANES <= done:
            store(tile * LANES, parts.pop(tile))


def normalize(tokens):
    center = tokens - jnp.mean(tokens, axis=-1, keepdims=True)
    spread = jnp.mean(center * center, axis=-1, keepdims=True)
    inv_std = lax.rsqrt(spread + 1e-06)
    return center * inv_std, inv_std


def valid_patches(base, count, patches):
    index = base + lax.broadcasted_iota(jnp.int32, (patches, 1), 0)
    return (index < count).astype(jnp.float32)


def forward_kernel(
    clip_ref, count_ref, place_ref, tokens_ref, mod_ref, wqkv_hbm,
    qkv_hbm, prob_hbm, att_hbm, gdy_hbm, keep_ref, send_ref,
    wqkv_ref, qkv_ref, prob_ref, att_ref, gdy_ref, xmod_ref, same_ref, turned_ref, share_ref,
    load_sems, store_sems,
):
    frames, both, model = tokens_ref.shape
    patches = both // 2
    rows = frames * patches
    head_dim = model // HEADS
    base = place_ref[0]
    core = place_ref[1]

    parts_n = model // CHUNK
    columns = [
        [slice(kind * model + part * CHUNK, kind * model + (part + 1) * CHUNK) for kind in range(3)]
        for part in range(parts_n)
    ]
    loads = [
        [
            pltpu.make_async_copy(
                wqkv_hbm.at[:, where], wqkv_ref.at[:, where], load_sems.at[part, kind]
            )
            for kind, where in enumerate(columns[part])
        ]
        for part in range(parts_n)
    ]

    def start_loads(part):
        if part < parts_n:
            for load in loads[part]:
                load.start()

    start_loads(0)

    def pair_step(step, carry):
        xmods, gdys = [], []
        for k in range(2):
            frame = 2 * step + k
            clip = clip_ref[0, frame]
            shift = mod_ref[0, pl.ds(clip, 1), :]
            scale = mod_ref[1, pl.ds(clip, 1), :]
            gate = mod_ref[2, pl.ds(clip, 1), :]
            both_f = tokens_ref[frame].astype(jnp.float32)
            normed, _ = normalize(both_f[:patches])
            xmods.append(normed * (1.0 + scale) + shift)
            valid = valid_patches(base, count_ref[0, clip], patches)
            gdys.append(valid * gate * both_f[patches:])
        where = pl.ds(pl.multiple_of(step * both, both), both)
        xmod_ref[where, :] = jnp.concatenate(xmods, axis=0).astype(jnp.bfloat16)
        gdy_ref[where, :] = jnp.concatenate(gdys, axis=0).astype(jnp.bfloat16)
        return carry

    lax.fori_loop(0, frames // 2, pair_step, 0, unroll=4)
    start_loads(1)

    stores = []

    def store_out(source_ref, target_hbm):
        store = pltpu.make_async_copy(source_ref, target_hbm, store_sems.at[len(stores)])
        store.start()
        stores.append(store)

    store_out(gdy_ref, gdy_hbm)

    starts = []
    for clip in range(1, mod_ref.shape[1]):
        start = jnp.int32(0)
        for frame in range(frames):
            start = start + jnp.where(clip_ref[0, frame] < clip, 1, 0)
        starts.append(start)

    def key_of(index):
        frame = index // patches
        key = index % patches
        for start in starts:
            key = key + jnp.where(frame >= start, patches, 0)
        return key

    key_e = key_of(lax.broadcasted_iota(jnp.int32, (rows, 1), 0))
    key_f = key_of(lax.broadcasted_iota(jnp.int32, (1, rows), 1))
    same_ref[...] = (key_e == key_f).astype(jnp.float32)

    chips, held = share_ref.shape[1] // SHARE_ROWS, SHARE_ROWS
    share = model // (2 * chips)
    for start in range(0, model, LANES):
        turned_ref[start : start + LANES, :] = gdy_ref[:, start : start + LANES].astype(
            jnp.float32
        ).T
    turned_ref[model:, :] = jnp.zeros((turned_ref.shape[0] - model, rows), jnp.float32)
    for side in range(2):
        for chip in range(0, chips, 2):
            pieces = []
            for k in range(2):
                start = (2 * (chip + k) + side) * share
                pieces.append(turned_ref[start : start + held, :])
            share_ref[side, chip * held : (chip + 2) * held, :] = jnp.concatenate(
                pieces, axis=0
            ).astype(jnp.bfloat16)

    def store_att(low, value):
        att_ref[:, low : low + LANES] = value.astype(jnp.bfloat16)

    xmod = xmod_ref[...]
    parts = {}
    head = 0
    for part in range(parts_n):
        for load in loads[part]:
            load.wait()
        start_loads(part + 2)
        for where in columns[part]:
            qkv_ref[:, where] = dot(xmod, wqkv_ref[:, where], NN).astype(jnp.bfloat16)
        if part == parts_n - 1:
            store_out(qkv_ref, qkv_hbm)
        first_head = head
        while head < HEADS and (head + 1) * head_dim <= (part + 1) * CHUNK:
            first, last, low, high = head_span(head, head_dim)
            mask = head_mask(first, last, low, high)
            query = qkv_ref[:, low:high] * mask
            key = qkv_ref[:, model + low : model + high]
            value = qkv_ref[:, 2 * model + low : 2 * model + high] * mask
            expo = jnp.exp(dot(key, query, NT) * head_dim ** (-0.5)) * same_ref[...]
            prob = (expo * (1.0 / jnp.sum(expo, axis=0, keepdims=True))).astype(jnp.bfloat16)
            prob_ref[head] = prob
            add_tiles(parts, low, dot(prob, value, TN))
            flush_tiles(parts, last, store_att)
            head += 1
        store_out(prob_ref.at[first_head:head], prob_hbm.at[first_head:head])
    store_out(att_ref, att_hbm)

    for target_ref, side in ((send_ref, 1 - core), (keep_ref, core)):
        for start in range(0, model, CHUNK):
            target_ref[:, start : start + CHUNK] = dot(
                share_ref[side], att_ref[:, start : start + CHUNK], NN
            ).astype(jnp.bfloat16)
    for store in stores:
        store.wait()


def backward_kernel(
    clip_ref, count_ref, place_ref, tokens_ref, mod_ref,
    gdy_hbm, wout_hbm, att_hbm, qkv_hbm, prob_hbm, wqkv_hbm,
    out_ref,
    gdy_ref, wout_ref, att_ref, qkv_ref, prob_ref, wqkv_ref,
    datt_ref, dqkv_ref, proj_ref, dxmod_ref, sems,
):
    frames, both, model = tokens_ref.shape
    patches = both // 2
    head_dim = model // HEADS
    att_scale = head_dim ** (-0.5)
    base = place_ref[0]

    loads = []
    for source_hbm, target_ref in (
        (gdy_hbm, gdy_ref), (wout_hbm, wout_ref), (att_hbm, att_ref),
        (qkv_hbm, qkv_ref), (prob_hbm, prob_ref), (wqkv_hbm, wqkv_ref),
    ):
        load = pltpu.make_async_copy(source_hbm, target_ref, sems.at[len(loads)])
        load.start()
        loads.append(load)

    loads[0].wait()
    loads[1].wait()
    gdy = gdy_ref[...]
    for start in range(0, model, CHUNK):
        datt_ref[:, start : start + CHUNK] = dot(
            gdy, wout_ref[start : start + CHUNK, :], NT
        ).astype(jnp.bfloat16)
    loads[2].wait()
    att = att_ref[...]
    for start in range(0, model, CHUNK):
        proj_ref[:, start : start + CHUNK] = dot(att, wout_ref[:, start : start + CHUNK], NN)
    loads[3].wait()
    loads[4].wait()

    def store_at(offset, factor):
        def store(low, value):
            dqkv_ref[:, offset + low : offset + low + LANES] = (value * factor).astype(jnp.bfloat16)
        return store

    parts_q, parts_k, parts_v = {}, {}, {}
    for head in range(HEADS):
        first, last, low, high = head_span(head, head_dim)
        mask = head_mask(first, last, low, high)
        query = qkv_ref[:, low:high] * mask
        key = qkv_ref[:, model + low : model + high] * mask
        value = qkv_ref[:, 2 * model + low : 2 * model + high]
        datt = datt_ref[:, low:high] * mask
        prob_low = prob_ref[head]
        add_tiles(parts_v, low, dot(prob_low, datt, NN))
        prob = prob_low.astype(jnp.float32)
        dprob = dot(value, datt, NT)
        total = jnp.sum(prob * dprob, axis=0, keepdims=True)
        dscore = (prob * (dprob - total)).astype(jnp.bfloat16)
        add_tiles(parts_k, low, dot(dscore, query, NN))
        add_tiles(parts_q, low, dot(dscore, key, TN))
        flush_tiles(parts_q, last, store_at(0, att_scale))
        flush_tiles(parts_k, last, store_at(model, att_scale))
        flush_tiles(parts_v, last, store_at(2 * model, 1.0))

    loads[5].wait()
    dqkv = dqkv_ref[...]
    for start in range(0, model, CHUNK):
        dxmod_ref[:, start : start + CHUNK] = dot(dqkv, wqkv_ref[start : start + CHUNK, :], NT)

    def frame_step(frame, carry):
        clip = clip_ref[0, frame]
        scale = mod_ref[1, pl.ds(clip, 1), :]
        gate = mod_ref[2, pl.ds(clip, 1), :]
        valid = valid_patches(base, count_ref[0, clip], patches)
        where = pl.ds(pl.multiple_of(frame * patches, patches), patches)
        both_f = tokens_ref[frame].astype(jnp.float32)
        latent = both_f[:patches]
        block_out = latent + valid * gate * proj_ref[where, :]
        normed, inv_std = normalize(latent)
        dnorm = dxmod_ref[where, :] * (1.0 + scale)
        branch = inv_std * (
            dnorm
            - jnp.mean(dnorm, axis=-1, keepdims=True)
            - normed * jnp.mean(dnorm * normed, axis=-1, keepdims=True)
        )
        out_ref[frame] = jnp.concatenate(
            [block_out, both_f[patches:] + branch], axis=0
        ).astype(jnp.bfloat16)
        return carry

    lax.fori_loop(0, frames, frame_step, 0, unroll=8)


def smem():
    return pl.BlockSpec(memory_space=pltpu.SMEM)


def vmem():
    return pl.BlockSpec(memory_space=pltpu.VMEM)


def hbm():
    return pl.BlockSpec(memory_space=pltpu.HBM)


def run_forward(frame_clip, clip_patches, place, tokens, modulation, qkv_weight, chips):
    frames, both, model = tokens.shape
    rows = frames * both // 2
    low = jnp.bfloat16
    sizes = ((rows, 3 * model), (HEADS, rows, rows), (rows, model), (rows, model))
    return pl.pallas_call(
        forward_kernel,
        out_shape=tuple(jax.ShapeDtypeStruct(size, low) for size in sizes)
        + (jax.ShapeDtypeStruct((chips * SHARE_ROWS, model), low),) * 2,
        in_specs=[smem()] * 3 + [vmem()] * 2 + [hbm()],
        out_specs=(hbm(),) * 4 + (vmem(),) * 2,
        scratch_shapes=[pltpu.VMEM((model, 3 * model), low)]
        + [pltpu.VMEM(size, low) for size in sizes]
        + [
            pltpu.VMEM((rows, model), low),
            pltpu.VMEM((rows, rows), jnp.float32),
            pltpu.VMEM((model + 16, rows), jnp.float32),
            pltpu.VMEM((2, chips * SHARE_ROWS, rows), low),
            pltpu.SemaphoreType.DMA((model // CHUNK, 3)),
            pltpu.SemaphoreType.DMA((3 + model // CHUNK,)),
        ],
        compiler_params=pltpu.CompilerParams(vmem_limit_bytes=58 * MIB),
        cost_estimate=pl.CostEstimate(
            flops=2 * rows * model * 4 * model, bytes_accessed=12 * MIB, transcendentals=0
        ),
        name="forward",
    )(frame_clip, clip_patches, place, tokens, modulation, qkv_weight)


def run_backward(
    frame_clip, clip_patches, place, tokens, modulation, gdy, out_weight, att, qkv, prob, qkv_weight
):
    frames, both, model = tokens.shape
    rows = frames * both // 2
    low = jnp.bfloat16
    loaded = (gdy, out_weight, att, qkv, prob, qkv_weight)
    return pl.pallas_call(
        backward_kernel,
        out_shape=jax.ShapeDtypeStruct((frames, both, model), low),
        in_specs=[smem()] * 3 + [vmem()] * 2 + [hbm()] * len(loaded),
        out_specs=vmem(),
        scratch_shapes=[pltpu.VMEM(array.shape, low) for array in loaded]
        + [
            pltpu.VMEM((rows, model), low),
            pltpu.VMEM((rows, 3 * model), low),
            pltpu.VMEM((rows, model), jnp.float32),
            pltpu.VMEM((rows, model), jnp.float32),
            pltpu.SemaphoreType.DMA((len(loaded),)),
        ],
        compiler_params=pltpu.CompilerParams(vmem_limit_bytes=58 * MIB),
        cost_estimate=pl.CostEstimate(
            flops=2 * rows * model * 6 * model, bytes_accessed=16 * MIB, transcendentals=0
        ),
        name="backward",
    )(frame_clip, clip_patches, place, tokens, modulation, *loaded)


def pack_kernel(latent_hbm, cotangent_hbm, out_ref, latent_ref, cotangent_ref, sems):
    both = out_ref.shape[1]
    patches = both // 2
    parts = sems.shape[1]
    rows = latent_ref.shape[0] // parts
    loads = []
    for part in range(parts):
        where = slice(part * rows, (part + 1) * rows)
        for k, (source, target) in enumerate(
            ((latent_hbm, latent_ref), (cotangent_hbm, cotangent_ref))
        ):
            load = pltpu.make_async_copy(source.at[where, :], target.at[where, :], sems.at[k, part])
            load.start()
            loads.append(load)
    for part in range(parts):
        loads[2 * part].wait()
        loads[2 * part + 1].wait()
        for start in range(part * rows, (part + 1) * rows, both):
            where = slice(start, start + both)
            latent = latent_ref[where, :].astype(jnp.float32)
            cotangent = cotangent_ref[where, :].astype(jnp.float32)
            for k in range(2):
                half = slice(k * patches, (k + 1) * patches)
                out_ref[start // patches + k] = jnp.concatenate(
                    [latent[half], cotangent[half]], axis=0
                ).astype(jnp.bfloat16)


def run_pack(latents, cotangent, seq):
    rows, model = latents.shape
    low = jnp.bfloat16
    return pl.pallas_call(
        pack_kernel,
        out_shape=jax.ShapeDtypeStruct((seq, 2 * rows // seq, model), low),
        in_specs=[hbm()] * 2,
        out_specs=vmem(),
        scratch_shapes=[pltpu.VMEM((rows, model), low)] * 2 + [pltpu.SemaphoreType.DMA((2, 4))],
        compiler_params=pltpu.CompilerParams(vmem_limit_bytes=60 * MIB),
        name="pack",
    )(latents, cotangent)


def add_kernel(left_ref, right_ref, out_ref):
    step_rows = 64
    for start in range(0, left_ref.shape[0], step_rows):
        where = slice(start, start + step_rows)
        out_ref[where, :] = (
            left_ref[where, :].astype(jnp.float32) + right_ref[where, :].astype(jnp.float32)
        ).astype(jnp.bfloat16)


def run_add(left, right):
    return pl.pallas_call(
        add_kernel,
        out_shape=jax.ShapeDtypeStruct(left.shape, left.dtype),
        in_specs=[vmem()] * 2,
        out_specs=vmem(),
        compiler_params=pltpu.CompilerParams(vmem_limit_bytes=12 * MIB),
        name="add",
    )(left, right)


def sum_kernel(terms_ref, after_ref, out_ref):
    del after_ref
    step_rows = 8
    for start in range(0, out_ref.shape[0], step_rows):
        where = slice(start, start + step_rows)
        total = terms_ref[0, where, :].astype(jnp.float32)
        for term in range(1, terms_ref.shape[0]):
            total = total + terms_ref[term, where, :].astype(jnp.float32)
        out_ref[where, :] = total


def run_sum(terms, after):
    return pl.pallas_call(
        sum_kernel,
        out_shape=jax.ShapeDtypeStruct(terms.shape[1:], jnp.float32),
        in_specs=[vmem(), pl.BlockSpec(memory_space=pl.ANY)],
        out_specs=vmem(),
        compiler_params=pltpu.CompilerParams(vmem_limit_bytes=12 * MIB),
        name="sum",
    )(terms, after)


def finish_kernel(returned_ref, left_ref, right_ref, block_ref, latent_ref, grad_ref):
    groups, both, _ = returned_ref.shape
    patches = both // 2
    for step in range(groups // 2):
        pair = [returned_ref[2 * step + k].astype(jnp.float32) for k in range(2)]
        where = slice(step * both, (step + 1) * both)
        block_ref[where, :] = jnp.concatenate([part[:patches] for part in pair], axis=0).astype(
            jnp.bfloat16
        )
        latent_ref[where, :] = jnp.concatenate([part[patches:] for part in pair], axis=0).astype(
            jnp.bfloat16
        )
    total = left_ref[...].astype(jnp.float32) + right_ref[...].astype(jnp.float32)
    grad_ref[...] = total[: grad_ref.shape[0]]


def run_finish(returned, left, right, share):
    groups, both, model = returned.shape
    low = jnp.bfloat16
    rows = groups * both // 2
    return pl.pallas_call(
        finish_kernel,
        out_shape=(
            jax.ShapeDtypeStruct((rows, model), low),
            jax.ShapeDtypeStruct((rows, model), low),
            jax.ShapeDtypeStruct((share, model), jnp.float32),
        ),
        in_specs=[vmem()] * 3,
        out_specs=(vmem(),) * 3,
        compiler_params=pltpu.CompilerParams(vmem_limit_bytes=12 * MIB),
        cost_estimate=pl.CostEstimate(flops=0, bytes_accessed=4 * MIB, transcendentals=0),
        name="finish",
    )(returned, left, right)


def per_device(latents, cotangent, qkv_weight, out_weight, modulation, frame_clip, clip_patches):
    seq = lax.axis_size("seq")
    groups = lax.axis_size("dp")
    chips = seq // 2
    patches, model = latents.shape[2], latents.shape[3]
    mine = patches // seq
    share = model // seq
    index = lax.axis_index("seq")
    place = jnp.stack([index * mine, index % 2]).astype(jnp.int32)

    outgoing = run_pack(latents.reshape(patches, model), cotangent.reshape(patches, model), seq)
    tokens = lax.all_to_all(outgoing, "seq", 0, 0, tiled=True)
    mod = modulation[0].transpose(1, 0, 2)
    qkv, prob, att, gdy, keep, send = run_forward(
        frame_clip, clip_patches, place, tokens, mod, qkv_weight, chips
    )
    other = lax.ppermute(send, "seq", [(i, i ^ 1) for i in range(seq)])
    pair = run_add(keep, other).reshape(chips, SHARE_ROWS, model)
    same_core = [[2 * chip + core for chip in range(chips)] for core in range(2)]
    terms = lax.all_to_all(pair, "seq", 0, 0, tiled=True, axis_index_groups=same_core)
    results = run_backward(
        frame_clip, clip_patches, place, tokens, mod, gdy, out_weight, att, qkv, prob, qkv_weight
    )
    total = run_sum(terms, results).astype(jnp.bfloat16)
    stride = 1
    while True:
        met = lax.ppermute(total, "dp", [(i, i ^ stride) for i in range(groups)])
        stride *= 2
        if stride >= groups:
            break
        total = (total.astype(jnp.float32) + met.astype(jnp.float32)).astype(jnp.bfloat16)
    returned = lax.all_to_all(results, "seq", 0, 0, tiled=True)
    block_out, latent_grad, grad = run_finish(returned, total, met, share)
    return block_out.reshape(latents.shape), latent_grad.reshape(latents.shape), grad


def solution(mesh):
    in_specs = (
        P("dp", "seq", None, None),
        P("dp", "seq", None, None),
        P(),
        P(),
        P("dp", None, None, None),
        P("dp", None),
        P("dp", None),
    )
    out_specs = (P("dp", "seq", None, None), P("dp", "seq", None, None), P("seq", None))
    return jax.shard_map(
        per_device, mesh=mesh, in_specs=in_specs, out_specs=out_specs, check_vma=False
    )
```

```python
import jax
import jax.numpy as jnp
from jax import lax
from jax.experimental import pallas as pl
from jax.experimental.pallas import tpu as pltpu
from jax.sharding import PartitionSpec as P

HEADS = 16
LANES = 128
CHUNK = 384
SHARE_ROWS = 40
MIB = 1024 * 1024

NN = (((1,), (0,)), ((), ()))
NT = (((1,), (1,)), ((), ()))
TN = (((0,), (0,)), ((), ()))


def dot(left, right, dims):
    return lax.dot_general(left, right, dims, preferred_element_type=jnp.float32)


def head_span(head, head_dim):
    first, last = head * head_dim, (head + 1) * head_dim
    low = first // LANES * LANES
    high = -(-last // LANES) * LANES
    return first, last, low, high


def head_mask(first, last, low, high):
    lane = lax.broadcasted_iota(jnp.int32, (1, high - low), 1) + low
    return jnp.where((lane >= first) & (lane < last), 1.0, 0.0).astype(jnp.bfloat16)


def add_tiles(parts, low, value):
    for start in range(0, value.shape[1], LANES):
        tile = (low + start) // LANES
        piece = value[:, start : start + LANES]
        parts[tile] = parts[tile] + piece if tile in parts else piece


def flush_tiles(parts, done, store):
    for tile in sorted(parts):
        if (tile + 1) * LANES <= done:
            store(tile * LANES, parts.pop(tile))


def normalize(tokens):
    center = tokens - jnp.mean(tokens, axis=-1, keepdims=True)
    spread = jnp.mean(center * center, axis=-1, keepdims=True)
    inv_std = lax.rsqrt(spread + 1e-06)
    return center * inv_std, inv_std


def valid_patches(base, count, patches):
    index = base + lax.broadcasted_iota(jnp.int32, (patches, 1), 0)
    return (index < count).astype(jnp.float32)


def forward_kernel(
    clip_ref, count_ref, place_ref, tokens_ref, mod_ref, wqkv_ref,
    qkv_ref, prob_ref, att_ref, gdy_ref, keep_ref, send_ref,
    xmod_ref, same_ref, turned_ref, share_ref,
):
    frames, both, model = tokens_ref.shape
    patches = both // 2
    rows = frames * patches
    head_dim = model // HEADS
    base = place_ref[0]
    core = place_ref[1]

    def pair_step(step, carry):
        xmods, gdys = [], []
        for k in range(2):
            frame = 2 * step + k
            clip = clip_ref[0, frame]
            shift = mod_ref[0, pl.ds(clip, 1), :]
            scale = mod_ref[1, pl.ds(clip, 1), :]
            gate = mod_ref[2, pl.ds(clip, 1), :]
            both_f = tokens_ref[frame].astype(jnp.float32)
            normed, _ = normalize(both_f[:patches])
            xmods.append(normed * (1.0 + scale) + shift)
            valid = valid_patches(base, count_ref[0, clip], patches)
            gdys.append(valid * gate * both_f[patches:])
        where = pl.ds(pl.multiple_of(step * both, both), both)
        xmod_ref[where, :] = jnp.concatenate(xmods, axis=0).astype(jnp.bfloat16)
        gdy_ref[where, :] = jnp.concatenate(gdys, axis=0).astype(jnp.bfloat16)
        return carry

    lax.fori_loop(0, frames // 2, pair_step, 0, unroll=4)

    starts = []
    for clip in range(1, mod_ref.shape[1]):
        start = jnp.int32(0)
        for frame in range(frames):
            start = start + jnp.where(clip_ref[0, frame] < clip, 1, 0)
        starts.append(start)

    def key_of(index):
        frame = index // patches
        key = index % patches
        for start in starts:
            key = key + jnp.where(frame >= start, patches, 0)
        return key

    key_e = key_of(lax.broadcasted_iota(jnp.int32, (rows, 1), 0))
    key_f = key_of(lax.broadcasted_iota(jnp.int32, (1, rows), 1))
    same_ref[...] = (key_e == key_f).astype(jnp.float32)

    chips, held = share_ref.shape[1] // SHARE_ROWS, SHARE_ROWS
    share = model // (2 * chips)
    for start in range(0, model, LANES):
        turned_ref[start : start + LANES, :] = gdy_ref[:, start : start + LANES].astype(
            jnp.float32
        ).T
    turned_ref[model:, :] = jnp.zeros((turned_ref.shape[0] - model, rows), jnp.float32)
    for side in range(2):
        for chip in range(0, chips, 2):
            pieces = []
            for k in range(2):
                start = (2 * (chip + k) + side) * share
                pieces.append(turned_ref[start : start + held, :])
            share_ref[side, chip * held : (chip + 2) * held, :] = jnp.concatenate(
                pieces, axis=0
            ).astype(jnp.bfloat16)

    def store_att(low, value):
        att_ref[:, low : low + LANES] = value.astype(jnp.bfloat16)

    xmod = xmod_ref[...]
    parts = {}
    head = 0
    for part in range(model // CHUNK):
        for kind in range(3):
            start = kind * model + part * CHUNK
            where = slice(start, start + CHUNK)
            qkv_ref[:, where] = dot(xmod, wqkv_ref[:, where], NN).astype(jnp.bfloat16)
        while head < HEADS and (head + 1) * head_dim <= (part + 1) * CHUNK:
            first, last, low, high = head_span(head, head_dim)
            mask = head_mask(first, last, low, high)
            query = qkv_ref[:, low:high] * mask
            key = qkv_ref[:, model + low : model + high]
            value = qkv_ref[:, 2 * model + low : 2 * model + high] * mask
            expo = jnp.exp(dot(key, query, NT) * head_dim ** (-0.5)) * same_ref[...]
            prob = (expo * (1.0 / jnp.sum(expo, axis=0, keepdims=True))).astype(jnp.bfloat16)
            prob_ref[head] = prob
            add_tiles(parts, low, dot(prob, value, TN))
            flush_tiles(parts, last, store_att)
            head += 1

    for target_ref, side in ((send_ref, 1 - core), (keep_ref, core)):
        for start in range(0, model, CHUNK):
            target_ref[:, start : start + CHUNK] = dot(
                share_ref[side], att_ref[:, start : start + CHUNK], NN
            ).astype(jnp.bfloat16)


def backward_kernel(
    clip_ref, count_ref, place_ref, tokens_ref, mod_ref,
    gdy_ref, wout_ref, att_ref, qkv_ref, prob_ref, wqkv_ref, after_ref,
    out_ref,
    datt_ref, dqkv_ref, proj_ref, dxmod_ref,
):
    del after_ref
    frames, both, model = tokens_ref.shape
    patches = both // 2
    head_dim = model // HEADS
    att_scale = head_dim ** (-0.5)
    base = place_ref[0]

    gdy = gdy_ref[...]
    for start in range(0, model, CHUNK):
        datt_ref[:, start : start + CHUNK] = dot(
            gdy, wout_ref[start : start + CHUNK, :], NT
        ).astype(jnp.bfloat16)
    att = att_ref[...]
    for start in range(0, model, CHUNK):
        proj_ref[:, start : start + CHUNK] = dot(att, wout_ref[:, start : start + CHUNK], NN)

    def store_at(offset, factor):
        def store(low, value):
            dqkv_ref[:, offset + low : offset + low + LANES] = (value * factor).astype(jnp.bfloat16)
        return store

    parts_q, parts_k, parts_v = {}, {}, {}
    for head in range(HEADS):
        first, last, low, high = head_span(head, head_dim)
        mask = head_mask(first, last, low, high)
        query = qkv_ref[:, low:high] * mask
        key = qkv_ref[:, model + low : model + high] * mask
        value = qkv_ref[:, 2 * model + low : 2 * model + high]
        datt = datt_ref[:, low:high] * mask
        prob_low = prob_ref[head]
        add_tiles(parts_v, low, dot(prob_low, datt, NN))
        prob = prob_low.astype(jnp.float32)
        dprob = dot(value, datt, NT)
        total = jnp.sum(prob * dprob, axis=0, keepdims=True)
        dscore = (prob * (dprob - total)).astype(jnp.bfloat16)
        add_tiles(parts_k, low, dot(dscore, query, NN))
        add_tiles(parts_q, low, dot(dscore, key, TN))
        flush_tiles(parts_q, last, store_at(0, att_scale))
        flush_tiles(parts_k, last, store_at(model, att_scale))
        flush_tiles(parts_v, last, store_at(2 * model, 1.0))

    dqkv = dqkv_ref[...]
    for start in range(0, model, CHUNK):
        dxmod_ref[:, start : start + CHUNK] = dot(dqkv, wqkv_ref[start : start + CHUNK, :], NT)

    def frame_step(frame, carry):
        clip = clip_ref[0, frame]
        scale = mod_ref[1, pl.ds(clip, 1), :]
        gate = mod_ref[2, pl.ds(clip, 1), :]
        valid = valid_patches(base, count_ref[0, clip], patches)
        where = pl.ds(pl.multiple_of(frame * patches, patches), patches)
        both_f = tokens_ref[frame].astype(jnp.float32)
        latent = both_f[:patches]
        block_out = latent + valid * gate * proj_ref[where, :]
        normed, inv_std = normalize(latent)
        dnorm = dxmod_ref[where, :] * (1.0 + scale)
        branch = inv_std * (
            dnorm
            - jnp.mean(dnorm, axis=-1, keepdims=True)
            - normed * jnp.mean(dnorm * normed, axis=-1, keepdims=True)
        )
        out_ref[frame] = jnp.concatenate(
            [block_out, both_f[patches:] + branch], axis=0
        ).astype(jnp.bfloat16)
        return carry

    lax.fori_loop(0, frames, frame_step, 0, unroll=8)


def smem():
    return pl.BlockSpec(memory_space=pltpu.SMEM)


def vmem():
    return pl.BlockSpec(memory_space=pltpu.VMEM)


def hbm():
    return pl.BlockSpec(memory_space=pltpu.HBM)


def in_hbm(array):
    return pltpu.with_memory_space_constraint(array, pltpu.HBM)


def in_vmem(array):
    return pltpu.with_memory_space_constraint(array, pltpu.VMEM)


def run_forward(frame_clip, clip_patches, place, tokens, modulation, qkv_weight, chips):
    frames, both, model = tokens.shape
    rows = frames * both // 2
    low = jnp.bfloat16
    sizes = ((rows, 3 * model), (HEADS, rows, rows), (rows, model), (rows, model))
    sizes += ((chips * SHARE_ROWS, model),) * 2
    return pl.pallas_call(
        forward_kernel,
        out_shape=tuple(pltpu.VMEM(size, low) for size in sizes),
        in_specs=[smem()] * 3 + [vmem()] * 3,
        out_specs=(vmem(),) * 6,
        scratch_shapes=[
            pltpu.VMEM((rows, model), low),
            pltpu.VMEM((rows, rows), jnp.float32),
            pltpu.VMEM((model + 16, rows), jnp.float32),
            pltpu.VMEM((2, chips * SHARE_ROWS, rows), low),
        ],
        compiler_params=pltpu.CompilerParams(vmem_limit_bytes=20 * MIB),
        cost_estimate=pl.CostEstimate(
            flops=2 * rows * model * 4 * model, bytes_accessed=12 * MIB, transcendentals=0
        ),
        name="forward",
    )(frame_clip, clip_patches, place, in_vmem(tokens), modulation, in_vmem(qkv_weight))


def run_backward(frame_clip, clip_patches, place, tokens, modulation, saved, after):
    frames, both, model = tokens.shape
    rows = frames * both // 2
    low = jnp.bfloat16
    return pl.pallas_call(
        backward_kernel,
        out_shape=pltpu.VMEM((frames, both, model), low),
        in_specs=[smem()] * 3 + [vmem()] * (2 + len(saved)) + [pl.BlockSpec(memory_space=pl.ANY)],
        out_specs=vmem(),
        scratch_shapes=[
            pltpu.VMEM((rows, model), low),
            pltpu.VMEM((rows, 3 * model), low),
            pltpu.VMEM((rows, model), jnp.float32),
            pltpu.VMEM((rows, model), jnp.float32),
        ],
        compiler_params=pltpu.CompilerParams(vmem_limit_bytes=20 * MIB),
        cost_estimate=pl.CostEstimate(
            flops=2 * rows * model * 6 * model, bytes_accessed=16 * MIB, transcendentals=0
        ),
        name="backward",
    )(
        frame_clip, clip_patches, place, in_vmem(tokens), modulation, *map(in_vmem, saved), after
    )


def load_kernel(*refs):
    count = len(refs) // 2
    sems = refs[-1]
    loads = [
        pltpu.make_async_copy(refs[k], refs[count + k], sems.at[k]) for k in range(count)
    ]
    for load in loads:
        load.start()
    for load in loads:
        load.wait()


def run_load(*weights):
    return pl.pallas_call(
        load_kernel,
        out_shape=tuple(pltpu.VMEM(weight.shape, weight.dtype) for weight in weights),
        in_specs=[hbm()] * len(weights),
        out_specs=(vmem(),) * len(weights),
        scratch_shapes=[pltpu.SemaphoreType.DMA((len(weights),))],
        compiler_params=pltpu.CompilerParams(vmem_limit_bytes=20 * MIB),
        cost_estimate=pl.CostEstimate(flops=0, bytes_accessed=22 * MIB, transcendentals=0),
        name="load",
    )(*map(in_hbm, weights))


def pack_kernel(latent_hbm, cotangent_hbm, out_ref, latent_ref, cotangent_ref, sems):
    both = out_ref.shape[1]
    patches = both // 2
    parts = sems.shape[1]
    rows = latent_ref.shape[0] // parts
    loads = []
    for part in range(parts):
        where = slice(part * rows, (part + 1) * rows)
        for k, (source, target) in enumerate(
            ((latent_hbm, latent_ref), (cotangent_hbm, cotangent_ref))
        ):
            load = pltpu.make_async_copy(source.at[where, :], target.at[where, :], sems.at[k, part])
            load.start()
            loads.append(load)
    for part in range(parts):
        loads[2 * part].wait()
        loads[2 * part + 1].wait()
        for start in range(part * rows, (part + 1) * rows, both):
            where = slice(start, start + both)
            latent = latent_ref[where, :].astype(jnp.float32)
            cotangent = cotangent_ref[where, :].astype(jnp.float32)
            for k in range(2):
                half = slice(k * patches, (k + 1) * patches)
                out_ref[start // patches + k] = jnp.concatenate(
                    [latent[half], cotangent[half]], axis=0
                ).astype(jnp.bfloat16)


def run_pack(latents, cotangent, seq):
    rows, model = latents.shape
    low = jnp.bfloat16
    return pl.pallas_call(
        pack_kernel,
        out_shape=pltpu.VMEM((seq, 2 * rows // seq, model), low),
        in_specs=[hbm()] * 2,
        out_specs=vmem(),
        scratch_shapes=[pltpu.VMEM((rows, model), low)] * 2 + [pltpu.SemaphoreType.DMA((2, 4))],
        compiler_params=pltpu.CompilerParams(vmem_limit_bytes=12 * MIB),
        name="pack",
    )(in_hbm(latents), in_hbm(cotangent))


def add_kernel(left_ref, right_ref, out_ref):
    step_rows = 64
    for start in range(0, left_ref.shape[0], step_rows):
        where = slice(start, start + step_rows)
        out_ref[where, :] = (
            left_ref[where, :].astype(jnp.float32) + right_ref[where, :].astype(jnp.float32)
        ).astype(jnp.bfloat16)


def run_add(left, right):
    return pl.pallas_call(
        add_kernel,
        out_shape=pltpu.VMEM(left.shape, left.dtype),
        in_specs=[vmem()] * 2,
        out_specs=vmem(),
        compiler_params=pltpu.CompilerParams(vmem_limit_bytes=12 * MIB),
        name="add",
    )(in_vmem(left), in_vmem(right))


def sum_kernel(terms_ref, after_ref, out_ref):
    del after_ref
    step_rows = 8
    for start in range(0, out_ref.shape[0], step_rows):
        where = slice(start, start + step_rows)
        total = terms_ref[0, where, :].astype(jnp.float32)
        for term in range(1, terms_ref.shape[0]):
            total = total + terms_ref[term, where, :].astype(jnp.float32)
        out_ref[where, :] = total


def run_sum(terms, after):
    return pl.pallas_call(
        sum_kernel,
        out_shape=jax.ShapeDtypeStruct(terms.shape[1:], jnp.float32),
        in_specs=[vmem(), pl.BlockSpec(memory_space=pl.ANY)],
        out_specs=vmem(),
        compiler_params=pltpu.CompilerParams(vmem_limit_bytes=12 * MIB),
        name="sum",
    )(terms, after)


def finish_kernel(returned_ref, left_ref, right_ref, block_ref, latent_ref, grad_ref):
    groups, both, _ = returned_ref.shape
    patches = both // 2
    for step in range(groups // 2):
        pair = [returned_ref[2 * step + k].astype(jnp.float32) for k in range(2)]
        where = slice(step * both, (step + 1) * both)
        block_ref[where, :] = jnp.concatenate([part[:patches] for part in pair], axis=0).astype(
            jnp.bfloat16
        )
        latent_ref[where, :] = jnp.concatenate([part[patches:] for part in pair], axis=0).astype(
            jnp.bfloat16
        )
    total = left_ref[...].astype(jnp.float32) + right_ref[...].astype(jnp.float32)
    grad_ref[...] = total[: grad_ref.shape[0]]


def run_finish(returned, left, right, share):
    groups, both, model = returned.shape
    low = jnp.bfloat16
    rows = groups * both // 2
    return pl.pallas_call(
        finish_kernel,
        out_shape=(
            jax.ShapeDtypeStruct((rows, model), low),
            jax.ShapeDtypeStruct((rows, model), low),
            jax.ShapeDtypeStruct((share, model), jnp.float32),
        ),
        in_specs=[vmem()] * 3,
        out_specs=(vmem(),) * 3,
        compiler_params=pltpu.CompilerParams(vmem_limit_bytes=12 * MIB),
        cost_estimate=pl.CostEstimate(flops=0, bytes_accessed=4 * MIB, transcendentals=0),
        name="finish",
    )(returned, left, right)


def per_device(latents, cotangent, qkv_weight, out_weight, modulation, frame_clip, clip_patches):
    seq = lax.axis_size("seq")
    groups = lax.axis_size("dp")
    chips = seq // 2
    patches, model = latents.shape[2], latents.shape[3]
    mine = patches // seq
    share = model // seq
    index = lax.axis_index("seq")
    place = jnp.stack([index * mine, index % 2]).astype(jnp.int32)

    outgoing = run_pack(latents.reshape(patches, model), cotangent.reshape(patches, model), seq)
    tokens = lax.all_to_all(outgoing, "seq", 0, 0, tiled=True)
    mod = modulation[0].transpose(1, 0, 2)
    qkv_weight, out_weight = run_load(qkv_weight, out_weight)
    qkv, prob, att, gdy, keep, send = run_forward(
        frame_clip, clip_patches, place, tokens, mod, qkv_weight, chips
    )
    other = lax.ppermute(send, "seq", [(i, i ^ 1) for i in range(seq)])
    pair = run_add(keep, other).reshape(chips, SHARE_ROWS, model)
    same_core = [[2 * chip + core for chip in range(chips)] for core in range(2)]
    terms = lax.all_to_all(pair, "seq", 0, 0, tiled=True, axis_index_groups=same_core)
    saved = (gdy, out_weight, att, qkv, prob, qkv_weight)
    results = run_backward(frame_clip, clip_patches, place, tokens, mod, saved, pair)
    total = run_sum(terms, results).astype(jnp.bfloat16)
    stride = 1
    while True:
        met = lax.ppermute(total, "dp", [(i, i ^ stride) for i in range(groups)])
        stride *= 2
        if stride >= groups:
            break
        total = (total.astype(jnp.float32) + met.astype(jnp.float32)).astype(jnp.bfloat16)
    returned = lax.all_to_all(results, "seq", 0, 0, tiled=True)
    block_out, latent_grad, grad = run_finish(returned, total, met, share)
    return block_out.reshape(latents.shape), latent_grad.reshape(latents.shape), grad


def solution(mesh):
    in_specs = (
        P("dp", "seq", None, None),
        P("dp", "seq", None, None),
        P(),
        P(),
        P("dp", None, None, None),
        P("dp", None),
        P("dp", None),
    )
    out_specs = (P("dp", "seq", None, None), P("dp", "seq", None, None), P("seq", None))
    return jax.shard_map(
        per_device, mesh=mesh, in_specs=in_specs, out_specs=out_specs, check_vma=False
    )
```

```python
import jax
import jax.numpy as jnp
from jax import lax
from jax.experimental import pallas as pl
from jax.experimental.pallas import tpu as pltpu
from jax.sharding import PartitionSpec as P

HEADS = 16
LANES = 128
CHUNK = 384
SHARE_ROWS = 40
MIB = 1024 * 1024

NN = (((1,), (0,)), ((), ()))
NT = (((1,), (1,)), ((), ()))
TN = (((0,), (0,)), ((), ()))


def dot(left, right, dims):
    return lax.dot_general(left, right, dims, preferred_element_type=jnp.float32)


def head_span(head, head_dim):
    first, last = head * head_dim, (head + 1) * head_dim
    low = first // LANES * LANES
    high = -(-last // LANES) * LANES
    return first, last, low, high


def head_mask(first, last, low, high):
    lane = lax.broadcasted_iota(jnp.int32, (1, high - low), 1) + low
    return jnp.where((lane >= first) & (lane < last), 1.0, 0.0).astype(jnp.bfloat16)


def add_tiles(parts, low, value):
    for start in range(0, value.shape[1], LANES):
        tile = (low + start) // LANES
        piece = value[:, start : start + LANES]
        parts[tile] = parts[tile] + piece if tile in parts else piece


def flush_tiles(parts, done, store):
    for tile in sorted(parts):
        if (tile + 1) * LANES <= done:
            store(tile * LANES, parts.pop(tile))


def normalize(tokens):
    center = tokens - jnp.mean(tokens, axis=-1, keepdims=True)
    spread = jnp.mean(center * center, axis=-1, keepdims=True)
    inv_std = lax.rsqrt(spread + 1e-06)
    return center * inv_std, inv_std


def valid_patches(base, count, patches):
    index = base + lax.broadcasted_iota(jnp.int32, (patches, 1), 0)
    return (index < count).astype(jnp.float32)


def forward_kernel(
    clip_ref, count_ref, place_ref, tokens_ref, mod_ref, wqkv_hbm,
    qkv_ref, prob_ref, att_ref, gdy_ref, share_ref, send_ref,
    wqkv_ref, xmod_ref, same_ref, turned_ref, load_sems,
):
    frames, both, model = tokens_ref.shape
    patches = both // 2
    rows = frames * patches
    head_dim = model // HEADS
    base = place_ref[0]
    core = place_ref[1]

    parts_n = model // CHUNK
    columns = [
        [slice(kind * model + part * CHUNK, kind * model + (part + 1) * CHUNK) for kind in range(3)]
        for part in range(parts_n)
    ]
    loads = [
        [
            pltpu.make_async_copy(
                wqkv_hbm.at[:, where], wqkv_ref.at[:, where], load_sems.at[part, kind]
            )
            for kind, where in enumerate(columns[part])
        ]
        for part in range(parts_n)
    ]

    def start_loads(part):
        if part < parts_n:
            for load in loads[part]:
                load.start()

    start_loads(0)

    def pair_step(step, carry):
        xmods, gdys = [], []
        for k in range(2):
            frame = 2 * step + k
            clip = clip_ref[0, frame]
            shift = mod_ref[0, pl.ds(clip, 1), :]
            scale = mod_ref[1, pl.ds(clip, 1), :]
            gate = mod_ref[2, pl.ds(clip, 1), :]
            both_f = tokens_ref[frame].astype(jnp.float32)
            normed, _ = normalize(both_f[:patches])
            xmods.append(normed * (1.0 + scale) + shift)
            valid = valid_patches(base, count_ref[0, clip], patches)
            gdys.append(valid * gate * both_f[patches:])
        where = pl.ds(pl.multiple_of(step * both, both), both)
        xmod_ref[where, :] = jnp.concatenate(xmods, axis=0).astype(jnp.bfloat16)
        gdy_ref[where, :] = jnp.concatenate(gdys, axis=0).astype(jnp.bfloat16)
        return carry

    lax.fori_loop(0, frames // 2, pair_step, 0, unroll=16)
    start_loads(1)

    starts = []
    for clip in range(1, mod_ref.shape[1]):
        start = jnp.int32(0)
        for frame in range(frames):
            start = start + jnp.where(clip_ref[0, frame] < clip, 1, 0)
        starts.append(start)

    def key_of(index):
        frame = index // patches
        key = index % patches
        for start in starts:
            key = key + jnp.where(frame >= start, patches, 0)
        return key

    key_e = key_of(lax.broadcasted_iota(jnp.int32, (rows, 1), 0))
    key_f = key_of(lax.broadcasted_iota(jnp.int32, (1, rows), 1))
    same_ref[...] = (key_e == key_f).astype(jnp.float32)

    held = SHARE_ROWS
    chips = share_ref.shape[1] // held
    share = model // (2 * chips)
    for start in range(0, model, LANES):
        turned_ref[start : start + LANES, :] = gdy_ref[:, start : start + LANES].astype(
            jnp.float32
        ).T
    turned_ref[model:, :] = jnp.zeros((turned_ref.shape[0] - model, rows), jnp.float32)
    for side in range(2):
        for chip in range(0, chips, 2):
            pieces = []
            for k in range(2):
                start = (2 * (chip + k) + side) * share
                pieces.append(turned_ref[start : start + held, :])
            share_ref[side, chip * held : (chip + 2) * held, :] = jnp.concatenate(
                pieces, axis=0
            ).astype(jnp.bfloat16)

    def store_att(low, value):
        att_ref[:, low : low + LANES] = value.astype(jnp.bfloat16)

    def score_of(head):
        first, last, low, high = head_span(head, head_dim)
        query = qkv_ref[:, low:high] * head_mask(first, last, low, high)
        return dot(qkv_ref[:, model + low : model + high], query, NT)

    xmod = xmod_ref[...]
    parts = {}
    head = 0
    for part in range(parts_n):
        for load in loads[part]:
            load.wait()
        start_loads(part + 2)
        for where in columns[part]:
            qkv_ref[:, where] = dot(xmod, wqkv_ref[:, where], NN).astype(jnp.bfloat16)
        scores = None
        while head < HEADS and (head + 1) * head_dim <= (part + 1) * CHUNK:
            first, last, low, high = head_span(head, head_dim)
            mask = head_mask(first, last, low, high)
            if scores is None:
                scores = score_of(head)
            last_head = (head + 2) * head_dim > (part + 1) * CHUNK
            later = None if last_head else score_of(head + 1)
            value = qkv_ref[:, 2 * model + low : 2 * model + high] * mask
            expo = jnp.exp(scores * head_dim ** (-0.5)) * same_ref[...]
            prob = (expo * (1.0 / jnp.sum(expo, axis=0, keepdims=True))).astype(jnp.bfloat16)
            prob_ref[head] = prob
            add_tiles(parts, low, dot(prob, value, TN))
            flush_tiles(parts, last, store_att)
            scores = later
            head += 1

    for start in range(0, model, CHUNK):
        send_ref[:, start : start + CHUNK] = dot(
            share_ref[1 - core], att_ref[:, start : start + CHUNK], NN
        ).astype(jnp.bfloat16)


def keep_kernel(place_ref, share_ref, qkv_ref, prob_ref, att_ref, gdy_ref, *refs):
    keep_ref, targets, sems = refs[0], refs[1:-1], refs[-1]
    stores = []
    for source, target in zip((qkv_ref, prob_ref, att_ref, gdy_ref), targets):
        store = pltpu.make_async_copy(source, target, sems.at[len(stores)])
        store.start()
        stores.append(store)
    core = place_ref[1]
    model = keep_ref.shape[1]
    for start in range(0, model, CHUNK):
        keep_ref[:, start : start + CHUNK] = dot(
            share_ref[core], att_ref[:, start : start + CHUNK], NN
        ).astype(jnp.bfloat16)
    for store in stores:
        store.wait()


def run_keep(place, share, saved):
    rows, model = share.shape[1], saved[2].shape[1]
    low = jnp.bfloat16
    return pl.pallas_call(
        keep_kernel,
        out_shape=(pltpu.VMEM((rows, model), low),)
        + tuple(pltpu.HBM(array.shape, low) for array in saved),
        in_specs=[smem()] + [vmem()] * (1 + len(saved)),
        out_specs=(vmem(),) + (hbm(),) * len(saved),
        scratch_shapes=[pltpu.SemaphoreType.DMA((len(saved),))],
        compiler_params=pltpu.CompilerParams(vmem_limit_bytes=12 * MIB),
        cost_estimate=pl.CostEstimate(
            flops=2 * rows * model * share.shape[2], bytes_accessed=6 * MIB, transcendentals=0
        ),
        name="keep",
    )(place, in_vmem(share), *map(in_vmem, saved))


def backward_kernel(
    clip_ref, count_ref, place_ref, tokens_ref, mod_ref,
    gdy_hbm, wout_hbm, att_hbm, qkv_hbm, prob_hbm, wqkv_hbm, after_ref,
    out_hbm,
    gdy_ref, wout_ref, att_ref, qkv_ref, prob_ref, wqkv_ref,
    datt_ref, dqkv_ref, proj_ref, dxmod_ref, out_ref, sems, store_sems,
):
    del after_ref
    frames, both, model = tokens_ref.shape
    patches = both // 2
    head_dim = model // HEADS
    att_scale = head_dim ** (-0.5)
    base = place_ref[0]

    loads = []
    for source_hbm, target_ref in (
        (gdy_hbm, gdy_ref), (wout_hbm, wout_ref), (att_hbm, att_ref),
        (qkv_hbm, qkv_ref), (prob_hbm, prob_ref), (wqkv_hbm, wqkv_ref),
    ):
        load = pltpu.make_async_copy(source_hbm, target_ref, sems.at[len(loads)])
        load.start()
        loads.append(load)

    loads[0].wait()
    loads[1].wait()
    gdy = gdy_ref[...]
    for start in range(0, model, CHUNK):
        datt_ref[:, start : start + CHUNK] = dot(
            gdy, wout_ref[start : start + CHUNK, :], NT
        ).astype(jnp.bfloat16)
    loads[2].wait()
    att = att_ref[...]
    for start in range(0, model, CHUNK):
        proj_ref[:, start : start + CHUNK] = dot(att, wout_ref[:, start : start + CHUNK], NN)
    loads[3].wait()
    loads[4].wait()

    def store_at(offset, factor):
        def store(low, value):
            dqkv_ref[:, offset + low : offset + low + LANES] = (value * factor).astype(jnp.bfloat16)
        return store

    parts_q, parts_k, parts_v = {}, {}, {}
    for head in range(HEADS):
        first, last, low, high = head_span(head, head_dim)
        mask = head_mask(first, last, low, high)
        query = qkv_ref[:, low:high] * mask
        key = qkv_ref[:, model + low : model + high] * mask
        value = qkv_ref[:, 2 * model + low : 2 * model + high]
        datt = datt_ref[:, low:high] * mask
        prob_low = prob_ref[head]
        add_tiles(parts_v, low, dot(prob_low, datt, NN))
        prob = prob_low.astype(jnp.float32)
        dprob = dot(value, datt, NT)
        total = jnp.sum(prob * dprob, axis=0, keepdims=True)
        dscore = (prob * (dprob - total)).astype(jnp.bfloat16)
        add_tiles(parts_k, low, dot(dscore, query, NN))
        add_tiles(parts_q, low, dot(dscore, key, TN))
        flush_tiles(parts_q, last, store_at(0, att_scale))
        flush_tiles(parts_k, last, store_at(model, att_scale))
        flush_tiles(parts_v, last, store_at(2 * model, 1.0))

    loads[5].wait()
    dqkv = dqkv_ref[...]
    for start in range(0, model, CHUNK):
        dxmod_ref[:, start : start + CHUNK] = dot(dqkv, wqkv_ref[start : start + CHUNK, :], NT)

    def frame_step(frame, carry):
        clip = clip_ref[0, frame]
        scale = mod_ref[1, pl.ds(clip, 1), :]
        gate = mod_ref[2, pl.ds(clip, 1), :]
        valid = valid_patches(base, count_ref[0, clip], patches)
        where = pl.ds(pl.multiple_of(frame * patches, patches), patches)
        both_f = tokens_ref[frame].astype(jnp.float32)
        latent = both_f[:patches]
        block_out = latent + valid * gate * proj_ref[where, :]
        normed, inv_std = normalize(latent)
        dnorm = dxmod_ref[where, :] * (1.0 + scale)
        branch = inv_std * (
            dnorm
            - jnp.mean(dnorm, axis=-1, keepdims=True)
            - normed * jnp.mean(dnorm * normed, axis=-1, keepdims=True)
        )
        out_ref[frame] = jnp.concatenate(
            [block_out, both_f[patches:] + branch], axis=0
        ).astype(jnp.bfloat16)
        return carry

    stores = []
    part_n = store_sems.shape[0]
    step = frames // part_n
    for part in range(part_n):
        lax.fori_loop(part * step, (part + 1) * step, frame_step, 0, unroll=step)
        where = slice(part * step, (part + 1) * step)
        store = pltpu.make_async_copy(out_ref.at[where], out_hbm.at[where], store_sems.at[part])
        store.start()
        stores.append(store)
    for store in stores:
        store.wait()


def smem():
    return pl.BlockSpec(memory_space=pltpu.SMEM)


def vmem():
    return pl.BlockSpec(memory_space=pltpu.VMEM)


def hbm():
    return pl.BlockSpec(memory_space=pltpu.HBM)


def in_hbm(array):
    return pltpu.with_memory_space_constraint(array, pltpu.HBM)


def in_vmem(array):
    return pltpu.with_memory_space_constraint(array, pltpu.VMEM)


def run_forward(frame_clip, clip_patches, place, tokens, modulation, qkv_weight, chips):
    frames, both, model = tokens.shape
    rows = frames * both // 2
    low = jnp.bfloat16
    groups = model // CHUNK
    sizes = ((rows, 3 * model), (HEADS, rows, rows), (rows, model), (rows, model))
    sizes += ((2, chips * SHARE_ROWS, rows), (chips * SHARE_ROWS, model))
    return pl.pallas_call(
        forward_kernel,
        out_shape=tuple(pltpu.VMEM(size, low) for size in sizes),
        in_specs=[smem()] * 3 + [vmem()] * 2 + [hbm()],
        out_specs=(vmem(),) * 6,
        scratch_shapes=[
            pltpu.VMEM((model, 3 * model), low),
            pltpu.VMEM((rows, model), low),
            pltpu.VMEM((rows, rows), jnp.float32),
            pltpu.VMEM((model + 16, rows), jnp.float32),
            pltpu.SemaphoreType.DMA((groups, 3)),
        ],
        compiler_params=pltpu.CompilerParams(vmem_limit_bytes=36 * MIB),
        cost_estimate=pl.CostEstimate(
            flops=2 * rows * model * 4 * model, bytes_accessed=12 * MIB, transcendentals=0
        ),
        name="forward",
    )(frame_clip, clip_patches, place, in_vmem(tokens), modulation, in_hbm(qkv_weight))


def run_backward(frame_clip, clip_patches, place, tokens, modulation, saved, after):
    frames, both, model = tokens.shape
    rows = frames * both // 2
    low = jnp.bfloat16
    return pl.pallas_call(
        backward_kernel,
        out_shape=pltpu.HBM((frames, both, model), low),
        in_specs=[smem()] * 3 + [vmem()] * 2 + [hbm()] * (len(saved) + 1),
        out_specs=hbm(),
        scratch_shapes=[pltpu.VMEM(array.shape, low) for array in saved]
        + [
            pltpu.VMEM((rows, model), low),
            pltpu.VMEM((rows, 3 * model), low),
            pltpu.VMEM((rows, model), jnp.float32),
            pltpu.VMEM((rows, model), jnp.float32),
            pltpu.VMEM((frames, both, model), low),
            pltpu.SemaphoreType.DMA((len(saved),)),
            pltpu.SemaphoreType.DMA((4,)),
        ],
        compiler_params=pltpu.CompilerParams(vmem_limit_bytes=36 * MIB),
        cost_estimate=pl.CostEstimate(
            flops=2 * rows * model * 6 * model, bytes_accessed=16 * MIB, transcendentals=0
        ),
        name="backward",
    )(
        frame_clip, clip_patches, place, in_vmem(tokens), modulation, *map(in_hbm, saved), in_hbm(after)
    )


def pack_kernel(
    latent_hbm, cotangent_hbm, out_hbm, latent_ref, cotangent_ref, out_ref, sems, store_sems
):
    both = out_ref.shape[1]
    patches = both // 2
    parts = sems.shape[1]
    rows = latent_ref.shape[0] // parts
    loads = []
    for part in range(parts):
        where = slice(part * rows, (part + 1) * rows)
        for k, (source, target) in enumerate(
            ((latent_hbm, latent_ref), (cotangent_hbm, cotangent_ref))
        ):
            load = pltpu.make_async_copy(source.at[where, :], target.at[where, :], sems.at[k, part])
            load.start()
            loads.append(load)
    stores = []
    for part in range(parts):
        loads[2 * part].wait()
        loads[2 * part + 1].wait()
        for start in range(part * rows, (part + 1) * rows, both):
            where = slice(start, start + both)
            latent = latent_ref[where, :].astype(jnp.float32)
            cotangent = cotangent_ref[where, :].astype(jnp.float32)
            for k in range(2):
                half = slice(k * patches, (k + 1) * patches)
                out_ref[start // patches + k] = jnp.concatenate(
                    [latent[half], cotangent[half]], axis=0
                ).astype(jnp.bfloat16)
        where = slice(part * rows // patches, (part + 1) * rows // patches)
        store = pltpu.make_async_copy(out_ref.at[where], out_hbm.at[where], store_sems.at[part])
        store.start()
        stores.append(store)
    for store in stores:
        store.wait()


def run_pack(latents, cotangent, seq):
    rows, model = latents.shape
    low = jnp.bfloat16
    size = (seq, 2 * rows // seq, model)
    return pl.pallas_call(
        pack_kernel,
        out_shape=pltpu.HBM(size, low),
        in_specs=[hbm()] * 2,
        out_specs=hbm(),
        scratch_shapes=[pltpu.VMEM((rows, model), low)] * 2
        + [
            pltpu.VMEM(size, low),
            pltpu.SemaphoreType.DMA((2, 4)),
            pltpu.SemaphoreType.DMA((4,)),
        ],
        compiler_params=pltpu.CompilerParams(vmem_limit_bytes=12 * MIB),
        name="pack",
    )(in_hbm(latents), in_hbm(cotangent))


def add_kernel(left_ref, right_ref, out_hbm, out_ref, store_sems):
    parts = store_sems.shape[0]
    rows = out_ref.shape[0] // parts
    stores = []
    for part in range(parts):
        where = slice(part * rows, (part + 1) * rows)
        out_ref[where, :] = (
            left_ref[where, :].astype(jnp.float32) + right_ref[where, :].astype(jnp.float32)
        ).astype(jnp.bfloat16)
        store = pltpu.make_async_copy(
            out_ref.at[where, :], out_hbm.at[where, :], store_sems.at[part]
        )
        store.start()
        stores.append(store)
    for store in stores:
        store.wait()


def run_add(left, right):
    return pl.pallas_call(
        add_kernel,
        out_shape=pltpu.HBM(left.shape, left.dtype),
        in_specs=[vmem()] * 2,
        out_specs=hbm(),
        scratch_shapes=[pltpu.VMEM(left.shape, left.dtype), pltpu.SemaphoreType.DMA((5,))],
        compiler_params=pltpu.CompilerParams(vmem_limit_bytes=12 * MIB),
        name="add",
    )(in_vmem(left), in_vmem(right))


def sum_kernel(terms_ref, after_ref, out_ref):
    del after_ref
    step_rows = 8
    for start in range(0, out_ref.shape[0], step_rows):
        where = slice(start, start + step_rows)
        total = terms_ref[0, where, :].astype(jnp.float32)
        for term in range(1, terms_ref.shape[0]):
            total = total + terms_ref[term, where, :].astype(jnp.float32)
        out_ref[where, :] = total


def run_sum(terms, after):
    return pl.pallas_call(
        sum_kernel,
        out_shape=jax.ShapeDtypeStruct(terms.shape[1:], jnp.float32),
        in_specs=[vmem(), hbm()],
        out_specs=vmem(),
        compiler_params=pltpu.CompilerParams(vmem_limit_bytes=12 * MIB),
        name="sum",
    )(terms, in_hbm(after))


def finish_kernel(returned_ref, left_ref, right_ref, block_ref, latent_ref, grad_ref):
    groups, both, _ = returned_ref.shape
    patches = both // 2
    for step in range(groups // 2):
        pair = [returned_ref[2 * step + k].astype(jnp.float32) for k in range(2)]
        where = slice(step * both, (step + 1) * both)
        block_ref[where, :] = jnp.concatenate([part[:patches] for part in pair], axis=0).astype(
            jnp.bfloat16
        )
        latent_ref[where, :] = jnp.concatenate([part[patches:] for part in pair], axis=0).astype(
            jnp.bfloat16
        )
    total = left_ref[...].astype(jnp.float32) + right_ref[...].astype(jnp.float32)
    grad_ref[...] = total[: grad_ref.shape[0]]


def run_finish(returned, left, right, share):
    groups, both, model = returned.shape
    low = jnp.bfloat16
    rows = groups * both // 2
    return pl.pallas_call(
        finish_kernel,
        out_shape=(
            jax.ShapeDtypeStruct((rows, model), low),
            jax.ShapeDtypeStruct((rows, model), low),
            jax.ShapeDtypeStruct((share, model), jnp.float32),
        ),
        in_specs=[vmem()] * 3,
        out_specs=(vmem(),) * 3,
        compiler_params=pltpu.CompilerParams(vmem_limit_bytes=12 * MIB),
        cost_estimate=pl.CostEstimate(flops=0, bytes_accessed=4 * MIB, transcendentals=0),
        name="finish",
    )(returned, left, right)


def per_device(latents, cotangent, qkv_weight, out_weight, modulation, frame_clip, clip_patches):
    seq = lax.axis_size("seq")
    groups = lax.axis_size("dp")
    chips = seq // 2
    patches, model = latents.shape[2], latents.shape[3]
    mine = patches // seq
    share = model // seq
    index = lax.axis_index("seq")
    place = jnp.stack([index * mine, index % 2]).astype(jnp.int32)

    outgoing = run_pack(latents.reshape(patches, model), cotangent.reshape(patches, model), seq)
    tokens = lax.all_to_all(outgoing, "seq", 0, 0, tiled=True)
    mod = modulation[0].transpose(1, 0, 2)
    qkv, prob, att, gdy, shares, send = run_forward(
        frame_clip, clip_patches, place, tokens, mod, qkv_weight, chips
    )
    other = lax.ppermute(send, "seq", [(i, i ^ 1) for i in range(seq)])
    keep, qkv, prob, att, gdy = run_keep(place, shares, (qkv, prob, att, gdy))
    pair = run_add(keep, other).reshape(chips, SHARE_ROWS, model)
    same_core = [[2 * chip + core for chip in range(chips)] for core in range(2)]
    terms = lax.all_to_all(pair, "seq", 0, 0, tiled=True, axis_index_groups=same_core)
    saved = (gdy, out_weight, att, qkv, prob, qkv_weight)
    results = run_backward(frame_clip, clip_patches, place, tokens, mod, saved, pair)
    total = run_sum(terms, results).astype(jnp.bfloat16)
    stride = 1
    while True:
        met = lax.ppermute(total, "dp", [(i, i ^ stride) for i in range(groups)])
        stride *= 2
        if stride >= groups:
            break
        total = (total.astype(jnp.float32) + met.astype(jnp.float32)).astype(jnp.bfloat16)
    returned = lax.all_to_all(results, "seq", 0, 0, tiled=True)
    block_out, latent_grad, grad = run_finish(returned, total, met, share)
    return block_out.reshape(latents.shape), latent_grad.reshape(latents.shape), grad


def solution(mesh):
    in_specs = (
        P("dp", "seq", None, None),
        P("dp", "seq", None, None),
        P(),
        P(),
        P("dp", None, None, None),
        P("dp", None),
        P("dp", None),
    )
    out_specs = (P("dp", "seq", None, None), P("dp", "seq", None, None), P("seq", None))
    return jax.shard_map(
        per_device, mesh=mesh, in_specs=in_specs, out_specs=out_specs, check_vma=False
    )
```

```python
import jax
import jax.numpy as jnp
from jax import lax
from jax.experimental import pallas as pl
from jax.experimental.pallas import tpu as pltpu
from jax.sharding import PartitionSpec as P

HEADS = 16
LANES = 128
EDGES = (0, 512, 1152)
SHARE_ROWS = 40
MIB = 1024 * 1024

NN = (((1,), (0,)), ((), ()))
NT = (((1,), (1,)), ((), ()))
TN = (((0,), (0,)), ((), ()))


def dot(left, right, dims):
    return lax.dot_general(left, right, dims, preferred_element_type=jnp.float32)


def wide_columns(width):
    edges = list(range(0, width - 511, 512))
    return [slice(low, high) for low, high in zip(edges, edges[1:] + [width])]


def head_span(head, head_dim):
    first, last = head * head_dim, (head + 1) * head_dim
    low = first // LANES * LANES
    high = -(-last // LANES) * LANES
    return first, last, low, high


def head_mask(first, last, low, high):
    lane = lax.broadcasted_iota(jnp.int32, (1, high - low), 1) + low
    return jnp.where((lane >= first) & (lane < last), 1.0, 0.0).astype(jnp.bfloat16)


def add_tiles(parts, low, value):
    for start in range(0, value.shape[1], LANES):
        tile = (low + start) // LANES
        piece = value[:, start : start + LANES]
        parts[tile] = parts[tile] + piece if tile in parts else piece


def flush_tiles(parts, done, store):
    for tile in sorted(parts):
        if (tile + 1) * LANES <= done:
            store(tile * LANES, parts.pop(tile))


def normalize(tokens):
    center = tokens - jnp.mean(tokens, axis=-1, keepdims=True)
    spread = jnp.mean(center * center, axis=-1, keepdims=True)
    inv_std = lax.rsqrt(spread + 1e-06)
    return center * inv_std, inv_std


def valid_patches(base, count, patches):
    index = base + lax.broadcasted_iota(jnp.int32, (patches, 1), 0)
    return (index < count).astype(jnp.float32)


def forward_kernel(
    clip_ref, count_ref, place_ref, tokens_ref, mod_ref, wqkv_hbm,
    qkv_ref, prob_ref, att_ref, gdy_ref, share_ref, send_ref,
    wqkv_ref, xmod_ref, same_ref, turned_ref, load_sems,
):
    rows, model = xmod_ref.shape
    frames = clip_ref.shape[1]
    patches = rows // frames
    head_dim = model // HEADS
    base = place_ref[0]
    core = place_ref[1]

    parts_n = len(EDGES) - 1
    columns = [
        [slice(kind * model + EDGES[part], kind * model + EDGES[part + 1]) for kind in range(3)]
        for part in range(parts_n)
    ]
    loads = [
        [
            pltpu.make_async_copy(
                wqkv_hbm.at[:, where], wqkv_ref.at[:, where], load_sems.at[part, kind]
            )
            for kind, where in enumerate(columns[part])
        ]
        for part in range(parts_n)
    ]

    def start_loads(part):
        if part < parts_n:
            for load in loads[part]:
                load.start()

    start_loads(0)

    def pair_step(step, carry):
        where = pl.ds(pl.multiple_of(2 * step * patches, 2 * patches), 2 * patches)
        latent = tokens_ref[where, :model].astype(jnp.float32)
        cotangent = tokens_ref[where, model:].astype(jnp.float32)
        xmods, gdys = [], []
        for k in range(2):
            half = slice(k * patches, (k + 1) * patches)
            clip = clip_ref[0, 2 * step + k]
            shift = mod_ref[0, pl.ds(clip, 1), :]
            scale = mod_ref[1, pl.ds(clip, 1), :]
            gate = mod_ref[2, pl.ds(clip, 1), :]
            normed, _ = normalize(latent[half])
            xmods.append(normed * (1.0 + scale) + shift)
            valid = valid_patches(base, count_ref[0, clip], patches)
            gdys.append(valid * gate * cotangent[half])
        xmod_ref[where, :] = jnp.concatenate(xmods, axis=0).astype(jnp.bfloat16)
        gdy_ref[where, :] = jnp.concatenate(gdys, axis=0).astype(jnp.bfloat16)
        return carry

    lax.fori_loop(0, frames // 2, pair_step, 0, unroll=4)
    start_loads(1)

    starts = []
    for clip in range(1, mod_ref.shape[1]):
        start = jnp.int32(0)
        for frame in range(frames):
            start = start + jnp.where(clip_ref[0, frame] < clip, 1, 0)
        starts.append(start)

    def key_of(index):
        frame = index // patches
        key = index % patches
        for start in starts:
            key = key + jnp.where(frame >= start, patches, 0)
        return key

    key_e = key_of(lax.broadcasted_iota(jnp.int32, (rows, 1), 0))
    key_f = key_of(lax.broadcasted_iota(jnp.int32, (1, rows), 1))
    same_ref[...] = (key_e == key_f).astype(jnp.float32)

    held = SHARE_ROWS
    chips = share_ref.shape[1] // held
    share = model // (2 * chips)
    for start in range(0, model, LANES):
        turned_ref[start : start + LANES, :] = gdy_ref[:, start : start + LANES].astype(
            jnp.float32
        ).T
    turned_ref[model:, :] = jnp.zeros((turned_ref.shape[0] - model, rows), jnp.float32)
    for side in range(2):
        for chip in range(0, chips, 2):
            pieces = []
            for k in range(2):
                start = (2 * (chip + k) + side) * share
                pieces.append(turned_ref[start : start + held, :])
            share_ref[side, chip * held : (chip + 2) * held, :] = jnp.concatenate(
                pieces, axis=0
            ).astype(jnp.bfloat16)

    def store_att(low, value):
        att_ref[:, low : low + LANES] = value.astype(jnp.bfloat16)

    def score_of(head):
        first, last, low, high = head_span(head, head_dim)
        query = qkv_ref[:, low:high] * head_mask(first, last, low, high)
        return dot(qkv_ref[:, model + low : model + high], query, NT)

    xmod = xmod_ref[...]
    parts = {}
    head = 0
    for part in range(parts_n):
        for load in loads[part]:
            load.wait()
        start_loads(part + 2)
        for where in columns[part]:
            qkv_ref[:, where] = dot(xmod, wqkv_ref[:, where], NN).astype(jnp.bfloat16)
        scores = None
        while head < HEADS and (head + 1) * head_dim <= EDGES[part + 1]:
            first, last, low, high = head_span(head, head_dim)
            mask = head_mask(first, last, low, high)
            if scores is None:
                scores = score_of(head)
            last_head = (head + 2) * head_dim > EDGES[part + 1]
            later = None if last_head else score_of(head + 1)
            value = qkv_ref[:, 2 * model + low : 2 * model + high] * mask
            expo = jnp.exp(scores * head_dim ** (-0.5)) * same_ref[...]
            prob = (expo * (1.0 / jnp.sum(expo, axis=0, keepdims=True))).astype(jnp.bfloat16)
            prob_ref[head] = prob
            add_tiles(parts, low, dot(prob, value, TN))
            flush_tiles(parts, last, store_att)
            scores = later
            head += 1

    for where in wide_columns(model):
        send_ref[:, where] = dot(share_ref[1 - core], att_ref[:, where], NN).astype(jnp.bfloat16)


def keep_kernel(place_ref, share_ref, qkv_ref, prob_ref, att_ref, gdy_ref, *refs):
    keep_ref, targets, sems = refs[0], refs[1:-1], refs[-1]
    stores = []
    for source, target in zip((qkv_ref, prob_ref, att_ref, gdy_ref), targets):
        store = pltpu.make_async_copy(source, target, sems.at[len(stores)])
        store.start()
        stores.append(store)
    core = place_ref[1]
    model = keep_ref.shape[1]
    for where in wide_columns(model):
        keep_ref[:, where] = dot(share_ref[core], att_ref[:, where], NN).astype(jnp.bfloat16)
    for store in stores:
        store.wait()


def run_keep(place, share, saved):
    rows, model = share.shape[1], saved[2].shape[1]
    low = jnp.bfloat16
    return pl.pallas_call(
        keep_kernel,
        out_shape=(pltpu.VMEM((rows, model), low),)
        + tuple(pltpu.HBM(array.shape, low) for array in saved),
        in_specs=[smem()] + [vmem()] * (1 + len(saved)),
        out_specs=(vmem(),) + (hbm(),) * len(saved),
        scratch_shapes=[pltpu.SemaphoreType.DMA((len(saved),))],
        compiler_params=pltpu.CompilerParams(vmem_limit_bytes=12 * MIB),
        cost_estimate=pl.CostEstimate(
            flops=2 * rows * model * share.shape[2], bytes_accessed=6 * MIB, transcendentals=0
        ),
        name="keep",
    )(place, in_vmem(share), *map(in_vmem, saved))


def backward_kernel(
    clip_ref, count_ref, place_ref, tokens_ref, mod_ref,
    gdy_hbm, wout_hbm, att_hbm, qkv_hbm, prob_hbm, wqkv_hbm, after_ref,
    out_hbm,
    gdy_ref, wout_ref, att_ref, qkv_ref, prob_ref, wqkv_ref,
    datt_ref, dqkv_ref, proj_ref, dxmod_ref, out_ref, sems, store_sems,
):
    del after_ref
    rows, model = gdy_ref.shape
    frames = clip_ref.shape[1]
    patches = rows // frames
    head_dim = model // HEADS
    att_scale = head_dim ** (-0.5)
    base = place_ref[0]

    loads = []
    for source_hbm, target_ref in (
        (gdy_hbm, gdy_ref), (wout_hbm, wout_ref), (att_hbm, att_ref),
        (qkv_hbm, qkv_ref), (prob_hbm, prob_ref), (wqkv_hbm, wqkv_ref),
    ):
        load = pltpu.make_async_copy(source_hbm, target_ref, sems.at[len(loads)])
        load.start()
        loads.append(load)

    loads[0].wait()
    loads[1].wait()
    gdy = gdy_ref[...]
    for where in wide_columns(model):
        datt_ref[:, where] = dot(gdy, wout_ref[where, :], NT).astype(jnp.bfloat16)
    loads[2].wait()
    att = att_ref[...]
    for where in wide_columns(model):
        proj_ref[:, where] = dot(att, wout_ref[:, where], NN)
    loads[3].wait()
    loads[4].wait()

    def store_at(offset, factor):
        def store(low, value):
            dqkv_ref[:, offset + low : offset + low + LANES] = (value * factor).astype(jnp.bfloat16)
        return store

    parts_q, parts_k, parts_v = {}, {}, {}
    for head in range(HEADS):
        first, last, low, high = head_span(head, head_dim)
        mask = head_mask(first, last, low, high)
        query = qkv_ref[:, low:high] * mask
        key = qkv_ref[:, model + low : model + high] * mask
        value = qkv_ref[:, 2 * model + low : 2 * model + high]
        datt = datt_ref[:, low:high] * mask
        prob_low = prob_ref[head]
        add_tiles(parts_v, low, dot(prob_low, datt, NN))
        prob = prob_low.astype(jnp.float32)
        dprob = dot(value, datt, NT)
        total = jnp.sum(prob * dprob, axis=0, keepdims=True)
        dscore = (prob * (dprob - total)).astype(jnp.bfloat16)
        add_tiles(parts_k, low, dot(dscore, query, NN))
        add_tiles(parts_q, low, dot(dscore, key, TN))
        flush_tiles(parts_q, last, store_at(0, att_scale))
        flush_tiles(parts_k, last, store_at(model, att_scale))
        flush_tiles(parts_v, last, store_at(2 * model, 1.0))

    loads[5].wait()
    dqkv = dqkv_ref[...]
    for where in wide_columns(model):
        dxmod_ref[:, where] = dot(dqkv, wqkv_ref[where, :], NT)

    def pair_step(step, carry):
        where = pl.ds(pl.multiple_of(2 * step * patches, 2 * patches), 2 * patches)
        latent_pair = tokens_ref[where, :model].astype(jnp.float32)
        cotangent = tokens_ref[where, model:].astype(jnp.float32)
        blocks, branches = [], []
        for k in range(2):
            half = slice(k * patches, (k + 1) * patches)
            clip = clip_ref[0, 2 * step + k]
            scale = mod_ref[1, pl.ds(clip, 1), :]
            gate = mod_ref[2, pl.ds(clip, 1), :]
            valid = valid_patches(base, count_ref[0, clip], patches)
            own = pl.ds(pl.multiple_of((2 * step + k) * patches, patches), patches)
            latent = latent_pair[half]
            blocks.append(latent + valid * gate * proj_ref[own, :])
            normed, inv_std = normalize(latent)
            dnorm = dxmod_ref[own, :] * (1.0 + scale)
            branches.append(
                inv_std
                * (
                    dnorm
                    - jnp.mean(dnorm, axis=-1, keepdims=True)
                    - normed * jnp.mean(dnorm * normed, axis=-1, keepdims=True)
                )
            )
        out_ref[where, :model] = jnp.concatenate(blocks, axis=0).astype(jnp.bfloat16)
        out_ref[where, model:] = (cotangent + jnp.concatenate(branches, axis=0)).astype(
            jnp.bfloat16
        )
        return carry

    stores = []
    part_n = store_sems.shape[0]
    steps = frames // (2 * part_n)
    for part in range(part_n):
        lax.fori_loop(part * steps, (part + 1) * steps, pair_step, 0, unroll=steps)
        where = slice(2 * part * steps * patches, 2 * (part + 1) * steps * patches)
        store = pltpu.make_async_copy(
            out_ref.at[where, :], out_hbm.at[where, :], store_sems.at[part]
        )
        store.start()
        stores.append(store)
    for store in stores:
        store.wait()


def smem():
    return pl.BlockSpec(memory_space=pltpu.SMEM)


def vmem():
    return pl.BlockSpec(memory_space=pltpu.VMEM)


def hbm():
    return pl.BlockSpec(memory_space=pltpu.HBM)


def in_hbm(array):
    return pltpu.with_memory_space_constraint(array, pltpu.HBM)


def in_vmem(array):
    return pltpu.with_memory_space_constraint(array, pltpu.VMEM)


def run_forward(frame_clip, clip_patches, place, tokens, modulation, qkv_weight, chips):
    rows, model = tokens.shape[0], tokens.shape[1] // 2
    low = jnp.bfloat16
    groups = len(EDGES) - 1
    sizes = ((rows, 3 * model), (HEADS, rows, rows), (rows, model), (rows, model))
    sizes += ((2, chips * SHARE_ROWS, rows), (chips * SHARE_ROWS, model))
    return pl.pallas_call(
        forward_kernel,
        out_shape=tuple(pltpu.VMEM(size, low) for size in sizes),
        in_specs=[smem()] * 3 + [vmem()] * 2 + [hbm()],
        out_specs=(vmem(),) * 6,
        scratch_shapes=[
            pltpu.VMEM((model, 3 * model), low),
            pltpu.VMEM((rows, model), low),
            pltpu.VMEM((rows, rows), jnp.float32),
            pltpu.VMEM((model + 16, rows), jnp.float32),
            pltpu.SemaphoreType.DMA((groups, 3)),
        ],
        compiler_params=pltpu.CompilerParams(vmem_limit_bytes=36 * MIB),
        cost_estimate=pl.CostEstimate(
            flops=2 * rows * model * 4 * model, bytes_accessed=12 * MIB, transcendentals=0
        ),
        name="forward",
    )(frame_clip, clip_patches, place, in_vmem(tokens), modulation, in_hbm(qkv_weight))


def run_backward(frame_clip, clip_patches, place, tokens, modulation, saved, after):
    rows, model = tokens.shape[0], tokens.shape[1] // 2
    low = jnp.bfloat16
    return pl.pallas_call(
        backward_kernel,
        out_shape=pltpu.HBM(tokens.shape, low),
        in_specs=[smem()] * 3 + [vmem()] * 2 + [hbm()] * (len(saved) + 1),
        out_specs=hbm(),
        scratch_shapes=[pltpu.VMEM(array.shape, low) for array in saved]
        + [
            pltpu.VMEM((rows, model), low),
            pltpu.VMEM((rows, 3 * model), low),
            pltpu.VMEM((rows, model), jnp.float32),
            pltpu.VMEM((rows, model), jnp.float32),
            pltpu.VMEM(tokens.shape, low),
            pltpu.SemaphoreType.DMA((len(saved),)),
            pltpu.SemaphoreType.DMA((4,)),
        ],
        compiler_params=pltpu.CompilerParams(vmem_limit_bytes=36 * MIB),
        cost_estimate=pl.CostEstimate(
            flops=2 * rows * model * 6 * model, bytes_accessed=16 * MIB, transcendentals=0
        ),
        name="backward",
    )(
        frame_clip, clip_patches, place, in_vmem(tokens), modulation, *map(in_hbm, saved), in_hbm(after)
    )


def pack_kernel(latent_hbm, cotangent_hbm, out_hbm, sems):
    model = latent_hbm.shape[1]
    copies = [
        pltpu.make_async_copy(latent_hbm, out_hbm.at[:, :model], sems.at[0]),
        pltpu.make_async_copy(cotangent_hbm, out_hbm.at[:, model:], sems.at[1]),
    ]
    for copy in copies:
        copy.start()
    for copy in copies:
        copy.wait()


def run_pack(latents, cotangent):
    rows, model = latents.shape
    return pl.pallas_call(
        pack_kernel,
        out_shape=pltpu.HBM((rows, 2 * model), latents.dtype),
        in_specs=[hbm()] * 2,
        out_specs=hbm(),
        scratch_shapes=[pltpu.SemaphoreType.DMA((2,))],
        compiler_params=pltpu.CompilerParams(vmem_limit_bytes=12 * MIB),
        name="pack",
    )(in_hbm(latents), in_hbm(cotangent))


def add_kernel(left_ref, right_ref, out_hbm, out_ref, store_sems):
    parts = store_sems.shape[0]
    rows = out_ref.shape[0] // parts
    stores = []
    for part in range(parts):
        where = slice(part * rows, (part + 1) * rows)
        out_ref[where, :] = (
            left_ref[where, :].astype(jnp.float32) + right_ref[where, :].astype(jnp.float32)
        ).astype(jnp.bfloat16)
        store = pltpu.make_async_copy(
            out_ref.at[where, :], out_hbm.at[where, :], store_sems.at[part]
        )
        store.start()
        stores.append(store)
    for store in stores:
        store.wait()


def run_add(left, right):
    return pl.pallas_call(
        add_kernel,
        out_shape=pltpu.HBM(left.shape, left.dtype),
        in_specs=[vmem()] * 2,
        out_specs=hbm(),
        scratch_shapes=[pltpu.VMEM(left.shape, left.dtype), pltpu.SemaphoreType.DMA((5,))],
        compiler_params=pltpu.CompilerParams(vmem_limit_bytes=12 * MIB),
        name="add",
    )(in_vmem(left), in_vmem(right))


def sum_kernel(terms_ref, after_ref, out_ref):
    del after_ref
    step_rows = 8
    for start in range(0, out_ref.shape[0], step_rows):
        where = slice(start, start + step_rows)
        total = terms_ref[0, where, :].astype(jnp.float32)
        for term in range(1, terms_ref.shape[0]):
            total = total + terms_ref[term, where, :].astype(jnp.float32)
        out_ref[where, :] = total


def run_sum(terms, after):
    return pl.pallas_call(
        sum_kernel,
        out_shape=jax.ShapeDtypeStruct(terms.shape[1:], jnp.float32),
        in_specs=[vmem(), hbm()],
        out_specs=vmem(),
        compiler_params=pltpu.CompilerParams(vmem_limit_bytes=12 * MIB),
        name="sum",
    )(terms, in_hbm(after))


def finish_kernel(returned_ref, left_ref, right_ref, block_hbm, latent_hbm, grad_ref, sems):
    model = block_hbm.shape[1]
    copies = [
        pltpu.make_async_copy(returned_ref.at[:, :model], block_hbm, sems.at[0]),
        pltpu.make_async_copy(returned_ref.at[:, model:], latent_hbm, sems.at[1]),
    ]
    for copy in copies:
        copy.start()
    total = left_ref[...].astype(jnp.float32) + right_ref[...].astype(jnp.float32)
    grad_ref[...] = total[: grad_ref.shape[0]]
    for copy in copies:
        copy.wait()


def run_finish(returned, left, right, share):
    rows, model = returned.shape[0], returned.shape[1] // 2
    low = jnp.bfloat16
    return pl.pallas_call(
        finish_kernel,
        out_shape=(
            pltpu.HBM((rows, model), low),
            pltpu.HBM((rows, model), low),
            jax.ShapeDtypeStruct((share, model), jnp.float32),
        ),
        in_specs=[vmem()] * 3,
        out_specs=(hbm(), hbm(), vmem()),
        scratch_shapes=[pltpu.SemaphoreType.DMA((2,))],
        compiler_params=pltpu.CompilerParams(vmem_limit_bytes=12 * MIB),
        cost_estimate=pl.CostEstimate(flops=0, bytes_accessed=4 * MIB, transcendentals=0),
        name="finish",
    )(returned, left, right)


def per_device(latents, cotangent, qkv_weight, out_weight, modulation, frame_clip, clip_patches):
    seq = lax.axis_size("seq")
    groups = lax.axis_size("dp")
    chips = seq // 2
    patches, model = latents.shape[2], latents.shape[3]
    mine = patches // seq
    share = model // seq
    index = lax.axis_index("seq")
    place = jnp.stack([index * mine, index % 2]).astype(jnp.int32)

    def exchange(rows):
        pieces = rows.reshape(seq, mine, rows.shape[1])
        return lax.all_to_all(pieces, "seq", 0, 0, tiled=True).reshape(rows.shape)

    tokens = exchange(run_pack(latents.reshape(patches, model), cotangent.reshape(patches, model)))
    mod = modulation[0].transpose(1, 0, 2)
    qkv, prob, att, gdy, shares, send = run_forward(
        frame_clip, clip_patches, place, tokens, mod, qkv_weight, chips
    )
    other = lax.ppermute(send, "seq", [(i, i ^ 1) for i in range(seq)])
    keep, qkv, prob, att, gdy = run_keep(place, shares, (qkv, prob, att, gdy))
    pair = run_add(keep, other).reshape(chips, SHARE_ROWS, model)
    same_core = [[2 * chip + core for chip in range(chips)] for core in range(2)]
    terms = lax.all_to_all(pair, "seq", 0, 0, tiled=True, axis_index_groups=same_core)
    saved = (gdy, out_weight, att, qkv, prob, qkv_weight)
    results = run_backward(frame_clip, clip_patches, place, tokens, mod, saved, pair)
    total = run_sum(terms, results).astype(jnp.bfloat16)
    stride = 1
    while True:
        met = lax.ppermute(total, "dp", [(i, i ^ stride) for i in range(groups)])
        stride *= 2
        if stride >= groups:
            break
        total = (total.astype(jnp.float32) + met.astype(jnp.float32)).astype(jnp.bfloat16)
    returned = exchange(results)
    block_out, latent_grad, grad = run_finish(returned, total, met, share)
    return block_out.reshape(latents.shape), latent_grad.reshape(latents.shape), grad


def solution(mesh):
    in_specs = (
        P("dp", "seq", None, None),
        P("dp", "seq", None, None),
        P(),
        P(),
        P("dp", None, None, None),
        P("dp", None),
        P("dp", None),
    )
    out_specs = (P("dp", "seq", None, None), P("dp", "seq", None, None), P("seq", None))
    return jax.shard_map(
        per_device, mesh=mesh, in_specs=in_specs, out_specs=out_specs, check_vma=False
    )
```

```python
import jax
import jax.numpy as jnp
from jax import lax
from jax.experimental import pallas as pl
from jax.experimental.pallas import tpu as pltpu
from jax.sharding import PartitionSpec as P

HEADS = 16
LANES = 128
EDGES = (0, 512, 1152)
PARTS = 2
SHARE_ROWS = 40
MIB = 1024 * 1024

NN = (((1,), (0,)), ((), ()))
NT = (((1,), (1,)), ((), ()))
TN = (((0,), (0,)), ((), ()))


def dot(left, right, dims):
    return lax.dot_general(left, right, dims, preferred_element_type=jnp.float32)


def wide_columns(width):
    edges = list(range(0, width - 511, 512))
    return [slice(low, high) for low, high in zip(edges, edges[1:] + [width])]


def head_span(head, head_dim):
    first, last = head * head_dim, (head + 1) * head_dim
    low = first // LANES * LANES
    high = -(-last // LANES) * LANES
    return first, last, low, high


def head_mask(first, last, low, high):
    lane = lax.broadcasted_iota(jnp.int32, (1, high - low), 1) + low
    return jnp.where((lane >= first) & (lane < last), 1.0, 0.0).astype(jnp.bfloat16)


def add_tiles(parts, low, value):
    for start in range(0, value.shape[1], LANES):
        tile = (low + start) // LANES
        piece = value[:, start : start + LANES]
        parts[tile] = parts[tile] + piece if tile in parts else piece


def flush_tiles(parts, done, store):
    for tile in sorted(parts):
        if (tile + 1) * LANES <= done:
            store(tile * LANES, parts.pop(tile))


def normalize(tokens):
    center = tokens - jnp.mean(tokens, axis=-1, keepdims=True)
    spread = jnp.mean(center * center, axis=-1, keepdims=True)
    inv_std = lax.rsqrt(spread + 1e-06)
    return center * inv_std, inv_std


def valid_patches(base, count, patches):
    index = base + lax.broadcasted_iota(jnp.int32, (patches, 1), 0)
    return (index < count).astype(jnp.float32)


def forward_kernel(
    clip_ref, count_ref, place_ref, tokens_ref, mod_ref, wqkv_hbm,
    qkv_ref, prob_ref, att_ref, gdy_ref, share_ref, send_ref,
    wqkv_ref, xmod_ref, same_ref, turned_ref, load_sems,
):
    rows, model = xmod_ref.shape
    frames = clip_ref.shape[1]
    patches = rows // frames
    head_dim = model // HEADS
    base = place_ref[0]
    core = place_ref[1]

    parts_n = len(EDGES) - 1
    columns = [
        [slice(kind * model + EDGES[part], kind * model + EDGES[part + 1]) for kind in range(3)]
        for part in range(parts_n)
    ]
    loads = [
        [
            pltpu.make_async_copy(
                wqkv_hbm.at[:, where], wqkv_ref.at[:, where], load_sems.at[part, kind]
            )
            for kind, where in enumerate(columns[part])
        ]
        for part in range(parts_n)
    ]

    def start_loads(part):
        if part < parts_n:
            for load in loads[part]:
                load.start()

    start_loads(0)

    def pair_step(step, carry):
        where = pl.ds(pl.multiple_of(2 * step * patches, 2 * patches), 2 * patches)
        latent = tokens_ref[where, :model].astype(jnp.float32)
        cotangent = tokens_ref[where, model:].astype(jnp.float32)
        xmods, gdys = [], []
        for k in range(2):
            half = slice(k * patches, (k + 1) * patches)
            clip = clip_ref[0, 2 * step + k]
            shift = mod_ref[0, pl.ds(clip, 1), :]
            scale = mod_ref[1, pl.ds(clip, 1), :]
            gate = mod_ref[2, pl.ds(clip, 1), :]
            normed, _ = normalize(latent[half])
            xmods.append(normed * (1.0 + scale) + shift)
            valid = valid_patches(base, count_ref[0, clip], patches)
            gdys.append(valid * gate * cotangent[half])
        xmod_ref[where, :] = jnp.concatenate(xmods, axis=0).astype(jnp.bfloat16)
        gdy_ref[where, :] = jnp.concatenate(gdys, axis=0).astype(jnp.bfloat16)
        return carry

    lax.fori_loop(0, frames // 2, pair_step, 0, unroll=4)
    start_loads(1)

    starts = []
    for clip in range(1, mod_ref.shape[1]):
        start = jnp.int32(0)
        for frame in range(frames):
            start = start + jnp.where(clip_ref[0, frame] < clip, 1, 0)
        starts.append(start)

    def key_of(index):
        frame = index // patches
        key = index % patches
        for start in starts:
            key = key + jnp.where(frame >= start, patches, 0)
        return key

    key_e = key_of(lax.broadcasted_iota(jnp.int32, (rows, 1), 0))
    key_f = key_of(lax.broadcasted_iota(jnp.int32, (1, rows), 1))
    same_ref[...] = (key_e == key_f).astype(jnp.float32)

    held = SHARE_ROWS
    chips = share_ref.shape[1] // held
    share = model // (2 * chips)
    for start in range(0, model, LANES):
        turned_ref[start : start + LANES, :] = gdy_ref[:, start : start + LANES].astype(
            jnp.float32
        ).T
    turned_ref[model:, :] = jnp.zeros((turned_ref.shape[0] - model, rows), jnp.float32)
    for side in range(2):
        for chip in range(0, chips, 2):
            pieces = []
            for k in range(2):
                start = (2 * (chip + k) + side) * share
                pieces.append(turned_ref[start : start + held, :])
            share_ref[side, chip * held : (chip + 2) * held, :] = jnp.concatenate(
                pieces, axis=0
            ).astype(jnp.bfloat16)

    def store_att(low, value):
        att_ref[:, low : low + LANES] = value.astype(jnp.bfloat16)

    def score_of(head):
        first, last, low, high = head_span(head, head_dim)
        query = qkv_ref[:, low:high] * head_mask(first, last, low, high)
        return dot(qkv_ref[:, model + low : model + high], query, NT)

    xmod = xmod_ref[...]
    parts = {}
    head = 0
    for part in range(parts_n):
        for load in loads[part]:
            load.wait()
        start_loads(part + 2)
        for where in columns[part]:
            qkv_ref[:, where] = dot(xmod, wqkv_ref[:, where], NN).astype(jnp.bfloat16)
        scores = None
        while head < HEADS and (head + 1) * head_dim <= EDGES[part + 1]:
            first, last, low, high = head_span(head, head_dim)
            mask = head_mask(first, last, low, high)
            if scores is None:
                scores = score_of(head)
            last_head = (head + 2) * head_dim > EDGES[part + 1]
            later = None if last_head else score_of(head + 1)
            value = qkv_ref[:, 2 * model + low : 2 * model + high] * mask
            expo = jnp.exp(scores * head_dim ** (-0.5)) * same_ref[...]
            prob = (expo * (1.0 / jnp.sum(expo, axis=0, keepdims=True))).astype(jnp.bfloat16)
            prob_ref[head] = prob
            add_tiles(parts, low, dot(prob, value, TN))
            flush_tiles(parts, last, store_att)
            scores = later
            head += 1

    for where in wide_columns(model):
        send_ref[:, where] = dot(share_ref[1 - core], att_ref[:, where], NN).astype(jnp.bfloat16)


def keep_kernel(place_ref, share_ref, qkv_ref, prob_ref, att_ref, gdy_ref, *refs):
    keep_ref, targets, sems = refs[0], refs[1:-1], refs[-1]
    stores = []
    for source, target in zip((qkv_ref, prob_ref, att_ref, gdy_ref), targets):
        store = pltpu.make_async_copy(source, target, sems.at[len(stores)])
        store.start()
        stores.append(store)
    core = place_ref[1]
    model = keep_ref.shape[1]
    for where in wide_columns(model):
        keep_ref[:, where] = dot(share_ref[core], att_ref[:, where], NN).astype(jnp.bfloat16)
    for store in stores:
        store.wait()


def run_keep(place, share, saved):
    rows, model = share.shape[1], saved[2].shape[1]
    low = jnp.bfloat16
    return pl.pallas_call(
        keep_kernel,
        out_shape=(pltpu.VMEM((rows, model), low),)
        + tuple(pltpu.HBM(array.shape, low) for array in saved),
        in_specs=[smem()] + [vmem()] * (1 + len(saved)),
        out_specs=(vmem(),) + (hbm(),) * len(saved),
        scratch_shapes=[pltpu.SemaphoreType.DMA((len(saved),))],
        compiler_params=pltpu.CompilerParams(vmem_limit_bytes=12 * MIB),
        cost_estimate=pl.CostEstimate(
            flops=2 * rows * model * share.shape[2], bytes_accessed=6 * MIB, transcendentals=0
        ),
        name="keep",
    )(place, in_vmem(share), *map(in_vmem, saved))


def backward_kernel(
    clip_ref, count_ref, place_ref, tokens_ref, mod_ref,
    gdy_hbm, wout_hbm, att_hbm, qkv_hbm, prob_hbm, wqkv_hbm, after_ref,
    out_hbm,
    gdy_ref, wout_ref, att_ref, qkv_ref, prob_ref, wqkv_ref,
    datt_ref, dqkv_ref, proj_ref, dxmod_ref, out_ref, sems, store_sems,
):
    del after_ref
    rows, model = gdy_ref.shape
    frames = clip_ref.shape[1]
    patches = rows // frames
    head_dim = model // HEADS
    att_scale = head_dim ** (-0.5)
    base = place_ref[0]

    loads = []
    for source_hbm, target_ref in (
        (gdy_hbm, gdy_ref), (wout_hbm, wout_ref), (att_hbm, att_ref),
        (qkv_hbm, qkv_ref), (prob_hbm, prob_ref), (wqkv_hbm, wqkv_ref),
    ):
        load = pltpu.make_async_copy(source_hbm, target_ref, sems.at[len(loads)])
        load.start()
        loads.append(load)

    loads[0].wait()
    loads[1].wait()
    gdy = gdy_ref[...]
    for where in wide_columns(model):
        datt_ref[:, where] = dot(gdy, wout_ref[where, :], NT).astype(jnp.bfloat16)
    loads[2].wait()
    att = att_ref[...]
    for where in wide_columns(model):
        proj_ref[:, where] = dot(att, wout_ref[:, where], NN)
    loads[3].wait()
    loads[4].wait()

    def store_at(offset, factor):
        def store(low, value):
            dqkv_ref[:, offset + low : offset + low + LANES] = (value * factor).astype(jnp.bfloat16)
        return store

    parts_q, parts_k, parts_v = {}, {}, {}
    for head in range(HEADS):
        first, last, low, high = head_span(head, head_dim)
        mask = head_mask(first, last, low, high)
        query = qkv_ref[:, low:high] * mask
        key = qkv_ref[:, model + low : model + high] * mask
        value = qkv_ref[:, 2 * model + low : 2 * model + high]
        datt = datt_ref[:, low:high] * mask
        prob_low = prob_ref[head]
        add_tiles(parts_v, low, dot(prob_low, datt, NN))
        prob = prob_low.astype(jnp.float32)
        dprob = dot(value, datt, NT)
        total = jnp.sum(prob * dprob, axis=0, keepdims=True)
        dscore = (prob * (dprob - total)).astype(jnp.bfloat16)
        add_tiles(parts_k, low, dot(dscore, query, NN))
        add_tiles(parts_q, low, dot(dscore, key, TN))
        flush_tiles(parts_q, last, store_at(0, att_scale))
        flush_tiles(parts_k, last, store_at(model, att_scale))
        flush_tiles(parts_v, last, store_at(2 * model, 1.0))

    loads[5].wait()
    dqkv = dqkv_ref[...]
    for where in wide_columns(model):
        dxmod_ref[:, where] = dot(dqkv, wqkv_ref[where, :], NT)

    def pair_step(step, carry):
        where = pl.ds(pl.multiple_of(2 * step * patches, 2 * patches), 2 * patches)
        latent_pair = tokens_ref[where, :model].astype(jnp.float32)
        cotangent = tokens_ref[where, model:].astype(jnp.float32)
        blocks, branches = [], []
        for k in range(2):
            half = slice(k * patches, (k + 1) * patches)
            clip = clip_ref[0, 2 * step + k]
            scale = mod_ref[1, pl.ds(clip, 1), :]
            gate = mod_ref[2, pl.ds(clip, 1), :]
            valid = valid_patches(base, count_ref[0, clip], patches)
            own = pl.ds(pl.multiple_of((2 * step + k) * patches, patches), patches)
            latent = latent_pair[half]
            blocks.append(latent + valid * gate * proj_ref[own, :])
            normed, inv_std = normalize(latent)
            dnorm = dxmod_ref[own, :] * (1.0 + scale)
            branches.append(
                inv_std
                * (
                    dnorm
                    - jnp.mean(dnorm, axis=-1, keepdims=True)
                    - normed * jnp.mean(dnorm * normed, axis=-1, keepdims=True)
                )
            )
        out_ref[where, :model] = jnp.concatenate(blocks, axis=0).astype(jnp.bfloat16)
        out_ref[where, model:] = (cotangent + jnp.concatenate(branches, axis=0)).astype(
            jnp.bfloat16
        )
        return carry

    stores = []
    part_n = store_sems.shape[0]
    steps = frames // (2 * part_n)
    for part in range(part_n):
        lax.fori_loop(part * steps, (part + 1) * steps, pair_step, 0, unroll=steps)
        where = slice(2 * part * steps * patches, 2 * (part + 1) * steps * patches)
        store = pltpu.make_async_copy(
            out_ref.at[where, :], out_hbm.at[where, :], store_sems.at[part]
        )
        store.start()
        stores.append(store)
    for store in stores:
        store.wait()


def smem():
    return pl.BlockSpec(memory_space=pltpu.SMEM)


def vmem():
    return pl.BlockSpec(memory_space=pltpu.VMEM)


def hbm():
    return pl.BlockSpec(memory_space=pltpu.HBM)


def in_hbm(array):
    return pltpu.with_memory_space_constraint(array, pltpu.HBM)


def in_vmem(array):
    return pltpu.with_memory_space_constraint(array, pltpu.VMEM)


def run_forward(frame_clip, clip_patches, place, tokens, modulation, qkv_weight, chips):
    rows, model = tokens.shape[0], tokens.shape[1] // 2
    low = jnp.bfloat16
    groups = len(EDGES) - 1
    sizes = ((rows, 3 * model), (HEADS, rows, rows), (rows, model), (rows, model))
    sizes += ((2, chips * SHARE_ROWS, rows), (chips * SHARE_ROWS, model))
    return pl.pallas_call(
        forward_kernel,
        out_shape=tuple(pltpu.VMEM(size, low) for size in sizes),
        in_specs=[smem()] * 3 + [vmem()] * 2 + [hbm()],
        out_specs=(vmem(),) * 6,
        scratch_shapes=[
            pltpu.VMEM((model, 3 * model), low),
            pltpu.VMEM((rows, model), low),
            pltpu.VMEM((rows, rows), jnp.float32),
            pltpu.VMEM((model + 16, rows), jnp.float32),
            pltpu.SemaphoreType.DMA((groups, 3)),
        ],
        compiler_params=pltpu.CompilerParams(vmem_limit_bytes=36 * MIB),
        cost_estimate=pl.CostEstimate(
            flops=2 * rows * model * 4 * model, bytes_accessed=12 * MIB, transcendentals=0
        ),
        name="forward",
    )(frame_clip, clip_patches, place, in_vmem(tokens), modulation, in_hbm(qkv_weight))


def run_backward(frame_clip, clip_patches, place, tokens, modulation, saved, after):
    rows, model = tokens.shape[0], tokens.shape[1] // 2
    low = jnp.bfloat16
    return pl.pallas_call(
        backward_kernel,
        out_shape=pltpu.HBM(tokens.shape, low),
        in_specs=[smem()] * 3 + [vmem()] * 2 + [hbm()] * (len(saved) + 1),
        out_specs=hbm(),
        scratch_shapes=[pltpu.VMEM(array.shape, low) for array in saved]
        + [
            pltpu.VMEM((rows, model), low),
            pltpu.VMEM((rows, 3 * model), low),
            pltpu.VMEM((rows, model), jnp.float32),
            pltpu.VMEM((rows, model), jnp.float32),
            pltpu.VMEM(tokens.shape, low),
            pltpu.SemaphoreType.DMA((len(saved),)),
            pltpu.SemaphoreType.DMA((4,)),
        ],
        compiler_params=pltpu.CompilerParams(vmem_limit_bytes=36 * MIB),
        cost_estimate=pl.CostEstimate(
            flops=2 * rows * model * 6 * model, bytes_accessed=16 * MIB, transcendentals=0
        ),
        name="backward",
    )(
        frame_clip, clip_patches, place, in_vmem(tokens), modulation, *map(in_hbm, saved), in_hbm(after)
    )


def pack_kernel(latent_hbm, cotangent_hbm, out_hbm, both_ref, load_sems, store_sems):
    rows, model = latent_hbm.shape
    parts = store_sems.shape[0]
    spans = [slice(part * rows // parts, (part + 1) * rows // parts) for part in range(parts)]
    loads = []
    for part, where in enumerate(spans):
        for side, source in enumerate((latent_hbm, cotangent_hbm)):
            columns = slice(side * model, (side + 1) * model)
            load = pltpu.make_async_copy(
                source.at[where, :], both_ref.at[where, columns], load_sems.at[part, side]
            )
            load.start()
            loads.append(load)
    stores = []
    for part, where in enumerate(spans):
        loads[2 * part].wait()
        loads[2 * part + 1].wait()
        store = pltpu.make_async_copy(
            both_ref.at[where, :], out_hbm.at[where, :], store_sems.at[part]
        )
        store.start()
        stores.append(store)
    for store in stores:
        store.wait()


def run_pack(latents, cotangent):
    rows, model = latents.shape
    size = (rows, 2 * model)
    return pl.pallas_call(
        pack_kernel,
        out_shape=pltpu.HBM(size, latents.dtype),
        in_specs=[hbm()] * 2,
        out_specs=hbm(),
        scratch_shapes=[
            pltpu.VMEM(size, latents.dtype),
            pltpu.SemaphoreType.DMA((PARTS, 2)),
            pltpu.SemaphoreType.DMA((PARTS,)),
        ],
        compiler_params=pltpu.CompilerParams(vmem_limit_bytes=12 * MIB),
        name="pack",
    )(in_hbm(latents), in_hbm(cotangent))


def add_kernel(left_ref, right_ref, out_hbm, out_ref, store_sems):
    parts = store_sems.shape[0]
    rows = out_ref.shape[0] // parts
    stores = []
    for part in range(parts):
        where = slice(part * rows, (part + 1) * rows)
        out_ref[where, :] = (
            left_ref[where, :].astype(jnp.float32) + right_ref[where, :].astype(jnp.float32)
        ).astype(jnp.bfloat16)
        store = pltpu.make_async_copy(
            out_ref.at[where, :], out_hbm.at[where, :], store_sems.at[part]
        )
        store.start()
        stores.append(store)
    for store in stores:
        store.wait()


def run_add(left, right):
    return pl.pallas_call(
        add_kernel,
        out_shape=pltpu.HBM(left.shape, left.dtype),
        in_specs=[vmem()] * 2,
        out_specs=hbm(),
        scratch_shapes=[pltpu.VMEM(left.shape, left.dtype), pltpu.SemaphoreType.DMA((5,))],
        compiler_params=pltpu.CompilerParams(vmem_limit_bytes=12 * MIB),
        name="add",
    )(in_vmem(left), in_vmem(right))


def sum_kernel(terms_ref, after_ref, out_ref):
    del after_ref
    step_rows = 8
    for start in range(0, out_ref.shape[0], step_rows):
        where = slice(start, start + step_rows)
        total = terms_ref[0, where, :].astype(jnp.float32)
        for term in range(1, terms_ref.shape[0]):
            total = total + terms_ref[term, where, :].astype(jnp.float32)
        out_ref[where, :] = total


def run_sum(terms, after):
    return pl.pallas_call(
        sum_kernel,
        out_shape=jax.ShapeDtypeStruct(terms.shape[1:], jnp.float32),
        in_specs=[vmem(), hbm()],
        out_specs=vmem(),
        compiler_params=pltpu.CompilerParams(vmem_limit_bytes=12 * MIB),
        name="sum",
    )(terms, in_hbm(after))


def finish_kernel(returned_ref, left_ref, right_ref, block_ref, latent_ref, grad_ref):
    model = block_ref.shape[1]
    block_ref[...] = returned_ref[:, :model]
    latent_ref[...] = returned_ref[:, model:]
    total = left_ref[...].astype(jnp.float32) + right_ref[...].astype(jnp.float32)
    grad_ref[...] = total[: grad_ref.shape[0]]


def run_finish(returned, left, right, share):
    rows, model = returned.shape[0], returned.shape[1] // 2
    low = jnp.bfloat16
    return pl.pallas_call(
        finish_kernel,
        out_shape=(
            jax.ShapeDtypeStruct((rows, model), low),
            jax.ShapeDtypeStruct((rows, model), low),
            jax.ShapeDtypeStruct((share, model), jnp.float32),
        ),
        in_specs=[vmem()] * 3,
        out_specs=(vmem(),) * 3,
        compiler_params=pltpu.CompilerParams(vmem_limit_bytes=12 * MIB),
        cost_estimate=pl.CostEstimate(flops=0, bytes_accessed=4 * MIB, transcendentals=0),
        name="finish",
    )(returned, left, right)


def per_device(latents, cotangent, qkv_weight, out_weight, modulation, frame_clip, clip_patches):
    seq = lax.axis_size("seq")
    groups = lax.axis_size("dp")
    chips = seq // 2
    patches, model = latents.shape[2], latents.shape[3]
    mine = patches // seq
    share = model // seq
    index = lax.axis_index("seq")
    place = jnp.stack([index * mine, index % 2]).astype(jnp.int32)

    def exchange(rows):
        pieces = rows.reshape(seq, mine, rows.shape[1])
        return lax.all_to_all(pieces, "seq", 0, 0, tiled=True).reshape(rows.shape)

    tokens = exchange(run_pack(latents.reshape(patches, model), cotangent.reshape(patches, model)))
    mod = modulation[0].transpose(1, 0, 2)
    qkv, prob, att, gdy, shares, send = run_forward(
        frame_clip, clip_patches, place, tokens, mod, qkv_weight, chips
    )
    other = lax.ppermute(send, "seq", [(i, i ^ 1) for i in range(seq)])
    keep, qkv, prob, att, gdy = run_keep(place, shares, (qkv, prob, att, gdy))
    pair = run_add(keep, other).reshape(chips, SHARE_ROWS, model)
    same_core = [[2 * chip + core for chip in range(chips)] for core in range(2)]
    terms = lax.all_to_all(pair, "seq", 0, 0, tiled=True, axis_index_groups=same_core)
    saved = (gdy, out_weight, att, qkv, prob, qkv_weight)
    results = run_backward(frame_clip, clip_patches, place, tokens, mod, saved, pair)
    total = run_sum(terms, results).astype(jnp.bfloat16)
    stride = 1
    while True:
        met = lax.ppermute(total, "dp", [(i, i ^ stride) for i in range(groups)])
        stride *= 2
        if stride >= groups:
            break
        total = (total.astype(jnp.float32) + met.astype(jnp.float32)).astype(jnp.bfloat16)
    returned = exchange(results)
    block_out, latent_grad, grad = run_finish(returned, total, met, share)
    return block_out.reshape(latents.shape), latent_grad.reshape(latents.shape), grad


def solution(mesh):
    in_specs = (
        P("dp", "seq", None, None),
        P("dp", "seq", None, None),
        P(),
        P(),
        P("dp", None, None, None),
        P("dp", None),
        P("dp", None),
    )
    out_specs = (P("dp", "seq", None, None), P("dp", "seq", None, None), P("seq", None))
    return jax.shard_map(
        per_device, mesh=mesh, in_specs=in_specs, out_specs=out_specs, check_vma=False
    )
```

```python
import jax
import jax.numpy as jnp
from jax import lax
from jax.experimental import pallas as pl
from jax.experimental.pallas import tpu as pltpu
from jax.sharding import PartitionSpec as P

HEADS = 16
LANES = 128
EDGES = (0, 512, 1152)
PARTS = 2
SHARE_ROWS = 40
MIB = 1024 * 1024

NN = (((1,), (0,)), ((), ()))
NT = (((1,), (1,)), ((), ()))
TN = (((0,), (0,)), ((), ()))


def dot(left, right, dims):
    return lax.dot_general(left, right, dims, preferred_element_type=jnp.float32)


def wide_columns(width):
    edges = list(range(0, width - 511, 512))
    return [slice(low, high) for low, high in zip(edges, edges[1:] + [width])]


def head_span(head, head_dim):
    first, last = head * head_dim, (head + 1) * head_dim
    low = first // LANES * LANES
    high = -(-last // LANES) * LANES
    return first, last, low, high


def head_mask(first, last, low, high):
    lane = lax.broadcasted_iota(jnp.int32, (1, high - low), 1) + low
    return jnp.where((lane >= first) & (lane < last), 1.0, 0.0).astype(jnp.bfloat16)


def add_tiles(parts, low, value):
    for start in range(0, value.shape[1], LANES):
        tile = (low + start) // LANES
        piece = value[:, start : start + LANES]
        parts[tile] = parts[tile] + piece if tile in parts else piece


def flush_tiles(parts, done, store):
    for tile in sorted(parts):
        if (tile + 1) * LANES <= done:
            store(tile * LANES, parts.pop(tile))


def normalize(tokens):
    center = tokens - jnp.mean(tokens, axis=-1, keepdims=True)
    spread = jnp.mean(center * center, axis=-1, keepdims=True)
    inv_std = lax.rsqrt(spread + 1e-06)
    return center * inv_std, inv_std


def valid_patches(base, count, patches):
    index = base + lax.broadcasted_iota(jnp.int32, (patches, 1), 0)
    return (index < count).astype(jnp.float32)


def forward_kernel(
    clip_ref, count_ref, place_ref, tokens_ref, mod_ref, wqkv_hbm,
    qkv_ref, prob_ref, att_ref, gdy_ref, share_ref, send_ref,
    wqkv_ref, xmod_ref, same_ref, turned_ref, load_sems,
):
    rows, model = xmod_ref.shape
    frames = clip_ref.shape[1]
    patches = rows // frames
    head_dim = model // HEADS
    base = place_ref[0]
    core = place_ref[1]

    parts_n = len(EDGES) - 1
    columns = [
        [slice(kind * model + EDGES[part], kind * model + EDGES[part + 1]) for kind in range(3)]
        for part in range(parts_n)
    ]
    loads = [
        [
            pltpu.make_async_copy(
                wqkv_hbm.at[:, where], wqkv_ref.at[:, where], load_sems.at[part, kind]
            )
            for kind, where in enumerate(columns[part])
        ]
        for part in range(parts_n)
    ]

    def start_loads(part):
        if part < parts_n:
            for load in loads[part]:
                load.start()

    start_loads(0)

    def pair_step(step, carry):
        where = pl.ds(pl.multiple_of(2 * step * patches, 2 * patches), 2 * patches)
        latent = tokens_ref[where, :model].astype(jnp.float32)
        cotangent = tokens_ref[where, model:].astype(jnp.float32)
        xmods, gdys = [], []
        for k in range(2):
            half = slice(k * patches, (k + 1) * patches)
            clip = clip_ref[0, 2 * step + k]
            shift = mod_ref[0, pl.ds(clip, 1), :]
            scale = mod_ref[1, pl.ds(clip, 1), :]
            gate = mod_ref[2, pl.ds(clip, 1), :]
            normed, _ = normalize(latent[half])
            xmods.append(normed * (1.0 + scale) + shift)
            valid = valid_patches(base, count_ref[0, clip], patches)
            gdys.append(valid * gate * cotangent[half])
        xmod_ref[where, :] = jnp.concatenate(xmods, axis=0).astype(jnp.bfloat16)
        gdy_ref[where, :] = jnp.concatenate(gdys, axis=0).astype(jnp.bfloat16)
        return carry

    lax.fori_loop(0, frames // 2, pair_step, 0, unroll=4)
    start_loads(1)

    starts = []
    for clip in range(1, mod_ref.shape[1]):
        start = jnp.int32(0)
        for frame in range(frames):
            start = start + jnp.where(clip_ref[0, frame] < clip, 1, 0)
        starts.append(start)

    def key_of(index):
        frame = index // patches
        key = index % patches
        for start in starts:
            key = key + jnp.where(frame >= start, patches, 0)
        return key

    key_e = key_of(lax.broadcasted_iota(jnp.int32, (rows, 1), 0))
    key_f = key_of(lax.broadcasted_iota(jnp.int32, (1, rows), 1))
    same_ref[...] = (key_e == key_f).astype(jnp.float32)

    held = SHARE_ROWS
    chips = share_ref.shape[1] // held
    share = model // (2 * chips)
    for start in range(0, model, LANES):
        turned_ref[start : start + LANES, :] = gdy_ref[:, start : start + LANES].astype(
            jnp.float32
        ).T
    turned_ref[model:, :] = jnp.zeros((turned_ref.shape[0] - model, rows), jnp.float32)
    for side in range(2):
        for chip in range(0, chips, 2):
            pieces = []
            for k in range(2):
                start = (2 * (chip + k) + side) * share
                pieces.append(turned_ref[start : start + held, :])
            share_ref[side, chip * held : (chip + 2) * held, :] = jnp.concatenate(
                pieces, axis=0
            ).astype(jnp.bfloat16)

    def store_att(low, value):
        att_ref[:, low : low + LANES] = value.astype(jnp.bfloat16)

    def score_of(head):
        first, last, low, high = head_span(head, head_dim)
        query = qkv_ref[:, low:high] * head_mask(first, last, low, high)
        return dot(qkv_ref[:, model + low : model + high], query, NT)

    xmod = xmod_ref[...]
    parts = {}
    head = 0
    for part in range(parts_n):
        for load in loads[part]:
            load.wait()
        start_loads(part + 2)
        for where in columns[part]:
            qkv_ref[:, where] = dot(xmod, wqkv_ref[:, where], NN).astype(jnp.bfloat16)
        scores = None
        while head < HEADS and (head + 1) * head_dim <= EDGES[part + 1]:
            first, last, low, high = head_span(head, head_dim)
            mask = head_mask(first, last, low, high)
            if scores is None:
                scores = score_of(head)
            last_head = (head + 2) * head_dim > EDGES[part + 1]
            later = None if last_head else score_of(head + 1)
            value = qkv_ref[:, 2 * model + low : 2 * model + high] * mask
            expo = jnp.exp(scores * head_dim ** (-0.5)) * same_ref[...]
            prob = (expo * (1.0 / jnp.sum(expo, axis=0, keepdims=True))).astype(jnp.bfloat16)
            prob_ref[head] = prob
            add_tiles(parts, low, dot(prob, value, TN))
            flush_tiles(parts, last, store_att)
            scores = later
            head += 1

    for where in wide_columns(model):
        send_ref[:, where] = dot(share_ref[1 - core], att_ref[:, where], NN).astype(jnp.bfloat16)


def keep_kernel(place_ref, share_ref, qkv_ref, prob_ref, att_ref, gdy_ref, *refs):
    keep_ref, targets, sems = refs[0], refs[1:-1], refs[-1]
    stores = []
    for source, target in zip((qkv_ref, prob_ref, att_ref, gdy_ref), targets):
        store = pltpu.make_async_copy(source, target, sems.at[len(stores)])
        store.start()
        stores.append(store)
    core = place_ref[1]
    model = keep_ref.shape[1]
    for where in wide_columns(model):
        keep_ref[:, where] = dot(share_ref[core], att_ref[:, where], NN).astype(jnp.bfloat16)
    for store in stores:
        store.wait()


def run_keep(place, share, saved):
    rows, model = share.shape[1], saved[2].shape[1]
    low = jnp.bfloat16
    return pl.pallas_call(
        keep_kernel,
        out_shape=(pltpu.VMEM((rows, model), low),)
        + tuple(pltpu.HBM(array.shape, low) for array in saved),
        in_specs=[smem()] + [vmem()] * (1 + len(saved)),
        out_specs=(vmem(),) + (hbm(),) * len(saved),
        scratch_shapes=[pltpu.SemaphoreType.DMA((len(saved),))],
        compiler_params=pltpu.CompilerParams(vmem_limit_bytes=12 * MIB),
        cost_estimate=pl.CostEstimate(
            flops=2 * rows * model * share.shape[2], bytes_accessed=6 * MIB, transcendentals=0
        ),
        name="keep",
    )(place, in_vmem(share), *map(in_vmem, saved))


def backward_kernel(
    clip_ref, count_ref, place_ref, tokens_ref, mod_ref,
    gdy_hbm, wout_hbm, att_hbm, qkv_hbm, prob_hbm, wqkv_hbm, after_ref,
    out_hbm,
    gdy_ref, wout_ref, att_ref, qkv_ref, prob_ref, wqkv_ref,
    datt_ref, dqkv_ref, proj_ref, dxmod_ref, out_ref, sems, store_sems,
):
    del after_ref
    rows, model = gdy_ref.shape
    frames = clip_ref.shape[1]
    patches = rows // frames
    head_dim = model // HEADS
    att_scale = head_dim ** (-0.5)
    base = place_ref[0]

    loads = []
    for source_hbm, target_ref in (
        (gdy_hbm, gdy_ref), (wout_hbm, wout_ref), (att_hbm, att_ref),
        (qkv_hbm, qkv_ref), (prob_hbm, prob_ref), (wqkv_hbm, wqkv_ref),
    ):
        load = pltpu.make_async_copy(source_hbm, target_ref, sems.at[len(loads)])
        load.start()
        loads.append(load)

    loads[0].wait()
    loads[1].wait()
    gdy = gdy_ref[...]
    for where in wide_columns(model):
        datt_ref[:, where] = dot(gdy, wout_ref[where, :], NT).astype(jnp.bfloat16)
    loads[2].wait()
    att = att_ref[...]
    for where in wide_columns(model):
        proj_ref[:, where] = dot(att, wout_ref[:, where], NN)
    loads[3].wait()
    loads[4].wait()

    def store_at(offset, factor):
        def store(low, value):
            dqkv_ref[:, offset + low : offset + low + LANES] = (value * factor).astype(jnp.bfloat16)
        return store

    parts_q, parts_k, parts_v = {}, {}, {}
    for head in range(HEADS):
        first, last, low, high = head_span(head, head_dim)
        mask = head_mask(first, last, low, high)
        query = qkv_ref[:, low:high] * mask
        key = qkv_ref[:, model + low : model + high] * mask
        value = qkv_ref[:, 2 * model + low : 2 * model + high]
        datt = datt_ref[:, low:high] * mask
        prob_low = prob_ref[head]
        add_tiles(parts_v, low, dot(prob_low, datt, NN))
        prob = prob_low.astype(jnp.float32)
        dprob = dot(value, datt, NT)
        total = jnp.sum(prob * dprob, axis=0, keepdims=True)
        dscore = (prob * (dprob - total)).astype(jnp.bfloat16)
        add_tiles(parts_k, low, dot(dscore, query, NN))
        add_tiles(parts_q, low, dot(dscore, key, TN))
        flush_tiles(parts_q, last, store_at(0, att_scale))
        flush_tiles(parts_k, last, store_at(model, att_scale))
        flush_tiles(parts_v, last, store_at(2 * model, 1.0))

    loads[5].wait()
    dqkv = dqkv_ref[...]
    for where in wide_columns(model):
        dxmod_ref[:, where] = dot(dqkv, wqkv_ref[where, :], NT)

    def pair_step(step, carry):
        where = pl.ds(pl.multiple_of(2 * step * patches, 2 * patches), 2 * patches)
        latent_pair = tokens_ref[where, :model].astype(jnp.float32)
        cotangent = tokens_ref[where, model:].astype(jnp.float32)
        blocks, branches = [], []
        for k in range(2):
            half = slice(k * patches, (k + 1) * patches)
            clip = clip_ref[0, 2 * step + k]
            scale = mod_ref[1, pl.ds(clip, 1), :]
            gate = mod_ref[2, pl.ds(clip, 1), :]
            valid = valid_patches(base, count_ref[0, clip], patches)
            own = pl.ds(pl.multiple_of((2 * step + k) * patches, patches), patches)
            latent = latent_pair[half]
            blocks.append(latent + valid * gate * proj_ref[own, :])
            normed, inv_std = normalize(latent)
            dnorm = dxmod_ref[own, :] * (1.0 + scale)
            branches.append(
                inv_std
                * (
                    dnorm
                    - jnp.mean(dnorm, axis=-1, keepdims=True)
                    - normed * jnp.mean(dnorm * normed, axis=-1, keepdims=True)
                )
            )
        out_ref[where, :model] = jnp.concatenate(blocks, axis=0).astype(jnp.bfloat16)
        out_ref[where, model:] = (cotangent + jnp.concatenate(branches, axis=0)).astype(
            jnp.bfloat16
        )
        return carry

    stores = []
    part_n = store_sems.shape[0]
    steps = frames // (2 * part_n)
    for part in range(part_n):
        lax.fori_loop(part * steps, (part + 1) * steps, pair_step, 0, unroll=steps)
        where = slice(2 * part * steps * patches, 2 * (part + 1) * steps * patches)
        store = pltpu.make_async_copy(
            out_ref.at[where, :], out_hbm.at[where, :], store_sems.at[part]
        )
        store.start()
        stores.append(store)
    for store in stores:
        store.wait()


def smem():
    return pl.BlockSpec(memory_space=pltpu.SMEM)


def vmem():
    return pl.BlockSpec(memory_space=pltpu.VMEM)


def hbm():
    return pl.BlockSpec(memory_space=pltpu.HBM)


def in_hbm(array):
    return pltpu.with_memory_space_constraint(array, pltpu.HBM)


def in_vmem(array):
    return pltpu.with_memory_space_constraint(array, pltpu.VMEM)


def run_forward(frame_clip, clip_patches, place, tokens, modulation, qkv_weight, chips):
    rows, model = tokens.shape[0], tokens.shape[1] // 2
    low = jnp.bfloat16
    groups = len(EDGES) - 1
    sizes = ((rows, 3 * model), (HEADS, rows, rows), (rows, model), (rows, model))
    sizes += ((2, chips * SHARE_ROWS, rows), (chips * SHARE_ROWS, model))
    return pl.pallas_call(
        forward_kernel,
        out_shape=tuple(pltpu.VMEM(size, low) for size in sizes),
        in_specs=[smem()] * 3 + [vmem()] * 2 + [hbm()],
        out_specs=(vmem(),) * 6,
        scratch_shapes=[
            pltpu.VMEM((model, 3 * model), low),
            pltpu.VMEM((rows, model), low),
            pltpu.VMEM((rows, rows), jnp.float32),
            pltpu.VMEM((model + 16, rows), jnp.float32),
            pltpu.SemaphoreType.DMA((groups, 3)),
        ],
        compiler_params=pltpu.CompilerParams(vmem_limit_bytes=36 * MIB),
        cost_estimate=pl.CostEstimate(
            flops=2 * rows * model * 4 * model, bytes_accessed=12 * MIB, transcendentals=0
        ),
        name="forward",
    )(frame_clip, clip_patches, place, in_vmem(tokens), modulation, in_hbm(qkv_weight))


def run_backward(frame_clip, clip_patches, place, tokens, modulation, saved, after):
    rows, model = tokens.shape[0], tokens.shape[1] // 2
    low = jnp.bfloat16
    return pl.pallas_call(
        backward_kernel,
        out_shape=pltpu.HBM(tokens.shape, low),
        in_specs=[smem()] * 3 + [vmem()] * 2 + [hbm()] * (len(saved) + 1),
        out_specs=hbm(),
        scratch_shapes=[pltpu.VMEM(array.shape, low) for array in saved]
        + [
            pltpu.VMEM((rows, model), low),
            pltpu.VMEM((rows, 3 * model), low),
            pltpu.VMEM((rows, model), jnp.float32),
            pltpu.VMEM((rows, model), jnp.float32),
            pltpu.VMEM(tokens.shape, low),
            pltpu.SemaphoreType.DMA((len(saved),)),
            pltpu.SemaphoreType.DMA((4,)),
        ],
        compiler_params=pltpu.CompilerParams(vmem_limit_bytes=36 * MIB),
        cost_estimate=pl.CostEstimate(
            flops=2 * rows * model * 6 * model, bytes_accessed=16 * MIB, transcendentals=0
        ),
        name="backward",
    )(
        frame_clip, clip_patches, place, in_vmem(tokens), modulation, *map(in_hbm, saved), in_hbm(after)
    )


def pack_kernel(latent_hbm, cotangent_hbm, out_hbm, both_ref, load_sems, store_sems):
    rows, model = latent_hbm.shape
    parts = store_sems.shape[0]
    spans = [slice(part * rows // parts, (part + 1) * rows // parts) for part in range(parts)]
    loads = []
    for part, where in enumerate(spans):
        for side, source in enumerate((latent_hbm, cotangent_hbm)):
            columns = slice(side * model, (side + 1) * model)
            load = pltpu.make_async_copy(
                source.at[where, :], both_ref.at[where, columns], load_sems.at[part, side]
            )
            load.start()
            loads.append(load)
    stores = []
    for part, where in enumerate(spans):
        loads[2 * part].wait()
        loads[2 * part + 1].wait()
        store = pltpu.make_async_copy(
            both_ref.at[where, :], out_hbm.at[where, :], store_sems.at[part]
        )
        store.start()
        stores.append(store)
    for store in stores:
        store.wait()


def run_pack(latents, cotangent):
    rows, model = latents.shape
    size = (rows, 2 * model)
    return pl.pallas_call(
        pack_kernel,
        out_shape=pltpu.HBM(size, latents.dtype),
        in_specs=[hbm()] * 2,
        out_specs=hbm(),
        scratch_shapes=[
            pltpu.VMEM(size, latents.dtype),
            pltpu.SemaphoreType.DMA((PARTS, 2)),
            pltpu.SemaphoreType.DMA((PARTS,)),
        ],
        compiler_params=pltpu.CompilerParams(vmem_limit_bytes=12 * MIB),
        name="pack",
    )(in_hbm(latents), in_hbm(cotangent))


def add_kernel(left_ref, right_ref, out_hbm, out_ref, store_sems):
    parts = store_sems.shape[0]
    rows = out_ref.shape[0] // parts
    stores = []
    for part in range(parts):
        where = slice(part * rows, (part + 1) * rows)
        out_ref[where, :] = (
            left_ref[where, :].astype(jnp.float32) + right_ref[where, :].astype(jnp.float32)
        ).astype(jnp.bfloat16)
        store = pltpu.make_async_copy(
            out_ref.at[where, :], out_hbm.at[where, :], store_sems.at[part]
        )
        store.start()
        stores.append(store)
    for store in stores:
        store.wait()


def run_add(left, right):
    return pl.pallas_call(
        add_kernel,
        out_shape=pltpu.HBM(left.shape, left.dtype),
        in_specs=[vmem()] * 2,
        out_specs=hbm(),
        scratch_shapes=[pltpu.VMEM(left.shape, left.dtype), pltpu.SemaphoreType.DMA((5,))],
        compiler_params=pltpu.CompilerParams(vmem_limit_bytes=12 * MIB),
        name="add",
    )(in_vmem(left), in_vmem(right))


def sum_kernel(terms_ref, after_ref, out_ref):
    del after_ref
    step_rows = 8
    for start in range(0, out_ref.shape[0], step_rows):
        where = slice(start, start + step_rows)
        total = terms_ref[0, where, :].astype(jnp.float32)
        for term in range(1, terms_ref.shape[0]):
            total = total + terms_ref[term, where, :].astype(jnp.float32)
        out_ref[where, :] = total


def run_sum(terms, after):
    return pl.pallas_call(
        sum_kernel,
        out_shape=jax.ShapeDtypeStruct(terms.shape[1:], jnp.float32),
        in_specs=[vmem(), hbm()],
        out_specs=vmem(),
        compiler_params=pltpu.CompilerParams(vmem_limit_bytes=12 * MIB),
        name="sum",
    )(terms, in_hbm(after))


def finish_kernel(returned_ref, left_ref, right_ref, block_ref, latent_ref, grad_ref):
    model = block_ref.shape[1]
    block_ref[...] = returned_ref[:, :model]
    latent_ref[...] = returned_ref[:, model:]
    total = left_ref[...].astype(jnp.float32) + right_ref[...].astype(jnp.float32)
    grad_ref[...] = total[: grad_ref.shape[0]]


def run_finish(returned, left, right, share):
    rows, model = returned.shape[0], returned.shape[1] // 2
    low = jnp.bfloat16
    return pl.pallas_call(
        finish_kernel,
        out_shape=(
            jax.ShapeDtypeStruct((rows, model), low),
            jax.ShapeDtypeStruct((rows, model), low),
            jax.ShapeDtypeStruct((share, model), jnp.float32),
        ),
        in_specs=[vmem()] * 3,
        out_specs=(vmem(),) * 3,
        compiler_params=pltpu.CompilerParams(vmem_limit_bytes=12 * MIB),
        cost_estimate=pl.CostEstimate(flops=0, bytes_accessed=4 * MIB, transcendentals=0),
        name="finish",
    )(returned, left, right)


def per_device(latents, cotangent, qkv_weight, out_weight, modulation, frame_clip, clip_patches):
    seq = lax.axis_size("seq")
    groups = lax.axis_size("dp")
    chips = seq // 2
    patches, model = latents.shape[2], latents.shape[3]
    mine = patches // seq
    share = model // seq
    index = lax.axis_index("seq")
    place = jnp.stack([index * mine, index % 2]).astype(jnp.int32)

    def exchange(rows):
        pieces = rows.reshape(seq, mine, rows.shape[1])
        return lax.all_to_all(pieces, "seq", 0, 0, tiled=True).reshape(rows.shape)

    tokens = exchange(run_pack(latents.reshape(patches, model), cotangent.reshape(patches, model)))
    mod = modulation[0].transpose(1, 0, 2)
    qkv, prob, att, gdy, shares, send = run_forward(
        frame_clip, clip_patches, place, tokens, mod, qkv_weight, chips
    )
    other = lax.ppermute(send, "seq", [(i, i ^ 1) for i in range(seq)])
    keep, qkv, prob, att, gdy = run_keep(place, shares, (qkv, prob, att, gdy))
    pair = run_add(keep, other).reshape(chips, SHARE_ROWS, model)
    same_core = [[2 * chip + core for chip in range(chips)] for core in range(2)]
    terms = lax.all_to_all(pair, "seq", 0, 0, tiled=True, axis_index_groups=same_core)
    saved = (gdy, out_weight, att, qkv, prob, qkv_weight)
    results = run_backward(frame_clip, clip_patches, place, tokens, mod, saved, pair)
    total = run_sum(terms, results).astype(jnp.bfloat16)
    strides = [groups // 2] + [1 << bit for bit in range(groups.bit_length() - 2)]
    for stride in strides[:-1]:
        met = lax.ppermute(total, "dp", [(i, i ^ stride) for i in range(groups)])
        total = (total.astype(jnp.float32) + met.astype(jnp.float32)).astype(jnp.bfloat16)
    met = lax.ppermute(total, "dp", [(i, i ^ strides[-1]) for i in range(groups)])
    returned = exchange(results)
    block_out, latent_grad, grad = run_finish(returned, total, met, share)
    return block_out.reshape(latents.shape), latent_grad.reshape(latents.shape), grad


def solution(mesh):
    in_specs = (
        P("dp", "seq", None, None),
        P("dp", "seq", None, None),
        P(),
        P(),
        P("dp", None, None, None),
        P("dp", None),
        P("dp", None),
    )
    out_specs = (P("dp", "seq", None, None), P("dp", "seq", None, None), P("seq", None))
    return jax.shard_map(
        per_device, mesh=mesh, in_specs=in_specs, out_specs=out_specs, check_vma=False
    )
```

```python
import jax
import jax.numpy as jnp
from jax import lax
from jax.experimental import pallas as pl
from jax.experimental.pallas import tpu as pltpu
from jax.sharding import PartitionSpec as P

HEADS = 16
LANES = 128
EDGES = (0, 512, 1152)
PARTS = 2
SHARE_ROWS = 40
MIB = 1024 * 1024

NN = (((1,), (0,)), ((), ()))
NT = (((1,), (1,)), ((), ()))
TN = (((0,), (0,)), ((), ()))


def dot(left, right, dims):
    return lax.dot_general(left, right, dims, preferred_element_type=jnp.float32)


def wide_columns(width):
    edges = list(range(0, width - 511, 512))
    return [slice(low, high) for low, high in zip(edges, edges[1:] + [width])]


def head_span(head, head_dim):
    first, last = head * head_dim, (head + 1) * head_dim
    low = first // LANES * LANES
    high = -(-last // LANES) * LANES
    return first, last, low, high


def head_mask(first, last, low, high):
    lane = lax.broadcasted_iota(jnp.int32, (1, high - low), 1) + low
    return jnp.where((lane >= first) & (lane < last), 1.0, 0.0).astype(jnp.bfloat16)


def add_tiles(parts, low, value):
    for start in range(0, value.shape[1], LANES):
        tile = (low + start) // LANES
        piece = value[:, start : start + LANES]
        parts[tile] = parts[tile] + piece if tile in parts else piece


def flush_tiles(parts, done, store):
    for tile in sorted(parts):
        if (tile + 1) * LANES <= done:
            store(tile * LANES, parts.pop(tile))


def normalize(tokens):
    center = tokens - jnp.mean(tokens, axis=-1, keepdims=True)
    spread = jnp.mean(center * center, axis=-1, keepdims=True)
    inv_std = lax.rsqrt(spread + 1e-06)
    return center * inv_std, inv_std


def valid_patches(base, count, patches):
    index = base + lax.broadcasted_iota(jnp.int32, (patches, 1), 0)
    return (index < count).astype(jnp.float32)


def forward_kernel(
    clip_ref, count_ref, place_ref, tokens_ref, mod_ref, wqkv_hbm,
    qkv_ref, prob_ref, att_ref, gdy_ref, share_ref, send_ref,
    wqkv_ref, xmod_ref, same_ref, turned_ref, load_sems,
):
    rows, model = xmod_ref.shape
    frames = clip_ref.shape[1]
    patches = rows // frames
    head_dim = model // HEADS
    base = place_ref[0]
    core = place_ref[1]

    parts_n = len(EDGES) - 1
    columns = [
        [slice(kind * model + EDGES[part], kind * model + EDGES[part + 1]) for kind in range(3)]
        for part in range(parts_n)
    ]
    loads = [
        [
            pltpu.make_async_copy(
                wqkv_hbm.at[:, where], wqkv_ref.at[:, where], load_sems.at[part, kind]
            )
            for kind, where in enumerate(columns[part])
        ]
        for part in range(parts_n)
    ]

    def start_loads(part):
        if part < parts_n:
            for load in loads[part]:
                load.start()

    start_loads(0)

    def pair_step(step, carry):
        where = pl.ds(pl.multiple_of(2 * step * patches, 2 * patches), 2 * patches)
        latent = tokens_ref[where, :model].astype(jnp.float32)
        cotangent = tokens_ref[where, model:].astype(jnp.float32)
        xmods, gdys = [], []
        for k in range(2):
            half = slice(k * patches, (k + 1) * patches)
            clip = clip_ref[0, 2 * step + k]
            shift = mod_ref[0, pl.ds(clip, 1), :]
            scale = mod_ref[1, pl.ds(clip, 1), :]
            gate = mod_ref[2, pl.ds(clip, 1), :]
            normed, _ = normalize(latent[half])
            xmods.append(normed * (1.0 + scale) + shift)
            valid = valid_patches(base, count_ref[0, clip], patches)
            gdys.append(valid * gate * cotangent[half])
        xmod_ref[where, :] = jnp.concatenate(xmods, axis=0).astype(jnp.bfloat16)
        gdy_ref[where, :] = jnp.concatenate(gdys, axis=0).astype(jnp.bfloat16)
        return carry

    lax.fori_loop(0, frames // 2, pair_step, 0, unroll=4)
    start_loads(1)

    starts = []
    for clip in range(1, mod_ref.shape[1]):
        start = jnp.int32(0)
        for frame in range(frames):
            start = start + jnp.where(clip_ref[0, frame] < clip, 1, 0)
        starts.append(start)

    def key_of(index):
        frame = index // patches
        key = index % patches
        for start in starts:
            key = key + jnp.where(frame >= start, patches, 0)
        return key

    key_e = key_of(lax.broadcasted_iota(jnp.int32, (rows, 1), 0))
    key_f = key_of(lax.broadcasted_iota(jnp.int32, (1, rows), 1))
    same_ref[...] = (key_e == key_f).astype(jnp.float32)

    held = SHARE_ROWS
    chips = share_ref.shape[1] // held
    share = model // (2 * chips)
    for start in range(0, model, LANES):
        turned_ref[start : start + LANES, :] = gdy_ref[:, start : start + LANES].astype(
            jnp.float32
        ).T
    turned_ref[model:, :] = jnp.zeros((turned_ref.shape[0] - model, rows), jnp.float32)
    for side in range(2):
        for chip in range(0, chips, 2):
            pieces = []
            for k in range(2):
                start = (2 * (chip + k) + side) * share
                pieces.append(turned_ref[start : start + held, :])
            share_ref[side, chip * held : (chip + 2) * held, :] = jnp.concatenate(
                pieces, axis=0
            ).astype(jnp.bfloat16)

    def store_att(low, value):
        att_ref[:, low : low + LANES] = value.astype(jnp.bfloat16)

    def score_of(head):
        first, last, low, high = head_span(head, head_dim)
        query = qkv_ref[:, low:high] * head_mask(first, last, low, high)
        return dot(qkv_ref[:, model + low : model + high], query, NT)

    xmod = xmod_ref[...]
    parts = {}
    head = 0
    for part in range(parts_n):
        for load in loads[part]:
            load.wait()
        start_loads(part + 2)
        for where in columns[part]:
            qkv_ref[:, where] = dot(xmod, wqkv_ref[:, where], NN).astype(jnp.bfloat16)
        scores = None
        while head < HEADS and (head + 1) * head_dim <= EDGES[part + 1]:
            first, last, low, high = head_span(head, head_dim)
            mask = head_mask(first, last, low, high)
            if scores is None:
                scores = score_of(head)
            last_head = (head + 2) * head_dim > EDGES[part + 1]
            later = None if last_head else score_of(head + 1)
            value = qkv_ref[:, 2 * model + low : 2 * model + high] * mask
            expo = jnp.exp(scores * head_dim ** (-0.5)) * same_ref[...]
            prob = (expo * (1.0 / jnp.sum(expo, axis=0, keepdims=True))).astype(jnp.bfloat16)
            prob_ref[head] = prob
            add_tiles(parts, low, dot(prob, value, TN))
            flush_tiles(parts, last, store_att)
            scores = later
            head += 1

    for where in wide_columns(model):
        send_ref[:, where] = dot(share_ref[1 - core], att_ref[:, where], NN).astype(jnp.bfloat16)


def keep_kernel(place_ref, share_ref, qkv_ref, prob_ref, att_ref, gdy_ref, *refs):
    keep_ref, targets, sems = refs[0], refs[1:-1], refs[-1]
    stores = []
    for source, target in zip((qkv_ref, prob_ref, att_ref, gdy_ref), targets):
        store = pltpu.make_async_copy(source, target, sems.at[len(stores)])
        store.start()
        stores.append(store)
    core = place_ref[1]
    model = keep_ref.shape[1]
    for where in wide_columns(model):
        keep_ref[:, where] = dot(share_ref[core], att_ref[:, where], NN).astype(jnp.bfloat16)
    for store in stores:
        store.wait()


def run_keep(place, share, saved):
    rows, model = share.shape[1], saved[2].shape[1]
    low = jnp.bfloat16
    return pl.pallas_call(
        keep_kernel,
        out_shape=(pltpu.VMEM((rows, model), low),)
        + tuple(pltpu.HBM(array.shape, low) for array in saved),
        in_specs=[smem()] + [vmem()] * (1 + len(saved)),
        out_specs=(vmem(),) + (hbm(),) * len(saved),
        scratch_shapes=[pltpu.SemaphoreType.DMA((len(saved),))],
        compiler_params=pltpu.CompilerParams(vmem_limit_bytes=12 * MIB),
        cost_estimate=pl.CostEstimate(
            flops=2 * rows * model * share.shape[2], bytes_accessed=6 * MIB, transcendentals=0
        ),
        name="keep",
    )(place, in_vmem(share), *map(in_vmem, saved))


def backward_kernel(
    clip_ref, count_ref, place_ref, tokens_ref, mod_ref,
    gdy_hbm, wout_hbm, att_hbm, qkv_hbm, prob_hbm, wqkv_hbm, after_ref,
    out_hbm,
    gdy_ref, wout_ref, att_ref, qkv_ref, prob_ref, wqkv_ref,
    datt_ref, dqkv_ref, proj_ref, dxmod_ref, out_ref, sems, store_sems,
):
    del after_ref
    rows, model = gdy_ref.shape
    frames = clip_ref.shape[1]
    patches = rows // frames
    head_dim = model // HEADS
    att_scale = head_dim ** (-0.5)
    base = place_ref[0]

    loads = []
    for source_hbm, target_ref in (
        (gdy_hbm, gdy_ref), (wout_hbm, wout_ref), (att_hbm, att_ref),
        (qkv_hbm, qkv_ref), (prob_hbm, prob_ref), (wqkv_hbm, wqkv_ref),
    ):
        load = pltpu.make_async_copy(source_hbm, target_ref, sems.at[len(loads)])
        load.start()
        loads.append(load)

    loads[0].wait()
    loads[1].wait()
    gdy = gdy_ref[...]
    for where in wide_columns(model):
        datt_ref[:, where] = dot(gdy, wout_ref[where, :], NT).astype(jnp.bfloat16)
    loads[2].wait()
    att = att_ref[...]
    for where in wide_columns(model):
        proj_ref[:, where] = dot(att, wout_ref[:, where], NN)
    loads[3].wait()
    loads[4].wait()

    def store_at(offset, factor):
        def store(low, value):
            dqkv_ref[:, offset + low : offset + low + LANES] = (value * factor).astype(jnp.bfloat16)
        return store

    parts_q, parts_k, parts_v = {}, {}, {}
    for head in range(HEADS):
        first, last, low, high = head_span(head, head_dim)
        mask = head_mask(first, last, low, high)
        query = qkv_ref[:, low:high] * mask
        key = qkv_ref[:, model + low : model + high] * mask
        value = qkv_ref[:, 2 * model + low : 2 * model + high]
        datt = datt_ref[:, low:high] * mask
        prob_low = prob_ref[head]
        add_tiles(parts_v, low, dot(prob_low, datt, NN))
        prob = prob_low.astype(jnp.float32)
        dprob = dot(value, datt, NT)
        total = jnp.sum(prob * dprob, axis=0, keepdims=True)
        dscore = (prob * (dprob - total)).astype(jnp.bfloat16)
        add_tiles(parts_k, low, dot(dscore, query, NN))
        add_tiles(parts_q, low, dot(dscore, key, TN))
        flush_tiles(parts_q, last, store_at(0, att_scale))
        flush_tiles(parts_k, last, store_at(model, att_scale))
        flush_tiles(parts_v, last, store_at(2 * model, 1.0))

    loads[5].wait()
    dqkv = dqkv_ref[...]
    for where in wide_columns(model):
        dxmod_ref[:, where] = dot(dqkv, wqkv_ref[where, :], NT)

    def pair_step(step, carry):
        where = pl.ds(pl.multiple_of(2 * step * patches, 2 * patches), 2 * patches)
        latent_pair = tokens_ref[where, :model].astype(jnp.float32)
        cotangent = tokens_ref[where, model:].astype(jnp.float32)
        blocks, branches = [], []
        for k in range(2):
            half = slice(k * patches, (k + 1) * patches)
            clip = clip_ref[0, 2 * step + k]
            scale = mod_ref[1, pl.ds(clip, 1), :]
            gate = mod_ref[2, pl.ds(clip, 1), :]
            valid = valid_patches(base, count_ref[0, clip], patches)
            own = pl.ds(pl.multiple_of((2 * step + k) * patches, patches), patches)
            latent = latent_pair[half]
            blocks.append(latent + valid * gate * proj_ref[own, :])
            normed, inv_std = normalize(latent)
            dnorm = dxmod_ref[own, :] * (1.0 + scale)
            branches.append(
                inv_std
                * (
                    dnorm
                    - jnp.mean(dnorm, axis=-1, keepdims=True)
                    - normed * jnp.mean(dnorm * normed, axis=-1, keepdims=True)
                )
            )
        out_ref[where, :model] = jnp.concatenate(blocks, axis=0).astype(jnp.bfloat16)
        out_ref[where, model:] = (cotangent + jnp.concatenate(branches, axis=0)).astype(
            jnp.bfloat16
        )
        return carry

    stores = []
    part_n = store_sems.shape[0]
    steps = frames // (2 * part_n)
    for part in range(part_n):
        lax.fori_loop(part * steps, (part + 1) * steps, pair_step, 0, unroll=steps)
        where = slice(2 * part * steps * patches, 2 * (part + 1) * steps * patches)
        store = pltpu.make_async_copy(
            out_ref.at[where, :], out_hbm.at[where, :], store_sems.at[part]
        )
        store.start()
        stores.append(store)
    for store in stores:
        store.wait()


def smem():
    return pl.BlockSpec(memory_space=pltpu.SMEM)


def vmem():
    return pl.BlockSpec(memory_space=pltpu.VMEM)


def hbm():
    return pl.BlockSpec(memory_space=pltpu.HBM)


def in_hbm(array):
    return pltpu.with_memory_space_constraint(array, pltpu.HBM)


def in_vmem(array):
    return pltpu.with_memory_space_constraint(array, pltpu.VMEM)


def run_forward(frame_clip, clip_patches, place, tokens, modulation, qkv_weight, chips):
    rows, model = tokens.shape[0], tokens.shape[1] // 2
    low = jnp.bfloat16
    groups = len(EDGES) - 1
    sizes = ((rows, 3 * model), (HEADS, rows, rows), (rows, model), (rows, model))
    sizes += ((2, chips * SHARE_ROWS, rows), (chips * SHARE_ROWS, model))
    return pl.pallas_call(
        forward_kernel,
        out_shape=tuple(pltpu.VMEM(size, low) for size in sizes),
        in_specs=[smem()] * 3 + [vmem()] * 2 + [hbm()],
        out_specs=(vmem(),) * 6,
        scratch_shapes=[
            pltpu.VMEM((model, 3 * model), low),
            pltpu.VMEM((rows, model), low),
            pltpu.VMEM((rows, rows), jnp.float32),
            pltpu.VMEM((model + 16, rows), jnp.float32),
            pltpu.SemaphoreType.DMA((groups, 3)),
        ],
        compiler_params=pltpu.CompilerParams(vmem_limit_bytes=36 * MIB),
        cost_estimate=pl.CostEstimate(
            flops=2 * rows * model * 4 * model, bytes_accessed=12 * MIB, transcendentals=0
        ),
        name="forward",
    )(frame_clip, clip_patches, place, in_vmem(tokens), modulation, in_hbm(qkv_weight))


def run_backward(frame_clip, clip_patches, place, tokens, modulation, saved, after):
    rows, model = tokens.shape[0], tokens.shape[1] // 2
    low = jnp.bfloat16
    return pl.pallas_call(
        backward_kernel,
        out_shape=pltpu.HBM(tokens.shape, low),
        in_specs=[smem()] * 3 + [vmem()] * 2 + [hbm()] * (len(saved) + 1),
        out_specs=hbm(),
        scratch_shapes=[pltpu.VMEM(array.shape, low) for array in saved]
        + [
            pltpu.VMEM((rows, model), low),
            pltpu.VMEM((rows, 3 * model), low),
            pltpu.VMEM((rows, model), jnp.float32),
            pltpu.VMEM((rows, model), jnp.float32),
            pltpu.VMEM(tokens.shape, low),
            pltpu.SemaphoreType.DMA((len(saved),)),
            pltpu.SemaphoreType.DMA((4,)),
        ],
        compiler_params=pltpu.CompilerParams(vmem_limit_bytes=36 * MIB),
        cost_estimate=pl.CostEstimate(
            flops=2 * rows * model * 6 * model, bytes_accessed=16 * MIB, transcendentals=0
        ),
        name="backward",
    )(
        frame_clip, clip_patches, place, in_vmem(tokens), modulation, *map(in_hbm, saved), in_hbm(after)
    )


def pack_kernel(latent_hbm, cotangent_hbm, out_hbm, both_ref, load_sems, store_sems):
    rows, model = latent_hbm.shape
    parts = store_sems.shape[0]
    spans = [slice(part * rows // parts, (part + 1) * rows // parts) for part in range(parts)]
    loads = []
    for part, where in enumerate(spans):
        for side, source in enumerate((latent_hbm, cotangent_hbm)):
            columns = slice(side * model, (side + 1) * model)
            load = pltpu.make_async_copy(
                source.at[where, :], both_ref.at[where, columns], load_sems.at[part, side]
            )
            load.start()
            loads.append(load)
    stores = []
    for part, where in enumerate(spans):
        loads[2 * part].wait()
        loads[2 * part + 1].wait()
        store = pltpu.make_async_copy(
            both_ref.at[where, :], out_hbm.at[where, :], store_sems.at[part]
        )
        store.start()
        stores.append(store)
    for store in stores:
        store.wait()


def run_pack(latents, cotangent):
    rows, model = latents.shape
    size = (rows, 2 * model)
    return pl.pallas_call(
        pack_kernel,
        out_shape=pltpu.HBM(size, latents.dtype),
        in_specs=[hbm()] * 2,
        out_specs=hbm(),
        scratch_shapes=[
            pltpu.VMEM(size, latents.dtype),
            pltpu.SemaphoreType.DMA((PARTS, 2)),
            pltpu.SemaphoreType.DMA((PARTS,)),
        ],
        compiler_params=pltpu.CompilerParams(vmem_limit_bytes=12 * MIB),
        name="pack",
    )(in_hbm(latents), in_hbm(cotangent))


def add_kernel(left_ref, right_ref, out_hbm, out_ref, store_sems):
    parts = store_sems.shape[0]
    rows = out_ref.shape[0] // parts
    stores = []
    for part in range(parts):
        where = slice(part * rows, (part + 1) * rows)
        out_ref[where, :] = (
            left_ref[where, :].astype(jnp.float32) + right_ref[where, :].astype(jnp.float32)
        ).astype(jnp.bfloat16)
        store = pltpu.make_async_copy(
            out_ref.at[where, :], out_hbm.at[where, :], store_sems.at[part]
        )
        store.start()
        stores.append(store)
    for store in stores:
        store.wait()


def run_add(left, right):
    return pl.pallas_call(
        add_kernel,
        out_shape=pltpu.HBM(left.shape, left.dtype),
        in_specs=[vmem()] * 2,
        out_specs=hbm(),
        scratch_shapes=[pltpu.VMEM(left.shape, left.dtype), pltpu.SemaphoreType.DMA((5,))],
        compiler_params=pltpu.CompilerParams(vmem_limit_bytes=12 * MIB),
        name="add",
    )(in_vmem(left), in_vmem(right))


def sum_kernel(terms_ref, after_ref, out_ref):
    del after_ref
    step_rows = 8
    for start in range(0, out_ref.shape[0], step_rows):
        where = slice(start, start + step_rows)
        total = terms_ref[0, where, :].astype(jnp.float32)
        for term in range(1, terms_ref.shape[0]):
            total = total + terms_ref[term, where, :].astype(jnp.float32)
        out_ref[where, :] = total


def run_sum(terms, after):
    return pl.pallas_call(
        sum_kernel,
        out_shape=jax.ShapeDtypeStruct(terms.shape[1:], jnp.float32),
        in_specs=[vmem(), hbm()],
        out_specs=vmem(),
        compiler_params=pltpu.CompilerParams(vmem_limit_bytes=12 * MIB),
        name="sum",
    )(terms, in_hbm(after))


def finish_kernel(returned_ref, own_ref, *refs):
    other_refs, (block_ref, latent_ref, grad_ref) = refs[:-3], refs[-3:]
    model = block_ref.shape[1]
    block_ref[...] = returned_ref[:, :model]
    latent_ref[...] = returned_ref[:, model:]
    total = own_ref[...].astype(jnp.float32)
    for other_ref in other_refs:
        total = total + other_ref[...].astype(jnp.float32)
    grad_ref[...] = total[: grad_ref.shape[0]]


def run_finish(returned, own, others, share):
    rows, model = returned.shape[0], returned.shape[1] // 2
    low = jnp.bfloat16
    return pl.pallas_call(
        finish_kernel,
        out_shape=(
            jax.ShapeDtypeStruct((rows, model), low),
            jax.ShapeDtypeStruct((rows, model), low),
            jax.ShapeDtypeStruct((share, model), jnp.float32),
        ),
        in_specs=[vmem()] * (2 + len(others)),
        out_specs=(vmem(),) * 3,
        compiler_params=pltpu.CompilerParams(vmem_limit_bytes=12 * MIB),
        cost_estimate=pl.CostEstimate(flops=0, bytes_accessed=4 * MIB, transcendentals=0),
        name="finish",
    )(returned, own, *others)


def per_device(latents, cotangent, qkv_weight, out_weight, modulation, frame_clip, clip_patches):
    seq = lax.axis_size("seq")
    groups = lax.axis_size("dp")
    chips = seq // 2
    patches, model = latents.shape[2], latents.shape[3]
    mine = patches // seq
    share = model // seq
    index = lax.axis_index("seq")
    place = jnp.stack([index * mine, index % 2]).astype(jnp.int32)

    def exchange(rows):
        pieces = rows.reshape(seq, mine, rows.shape[1])
        return lax.all_to_all(pieces, "seq", 0, 0, tiled=True).reshape(rows.shape)

    tokens = exchange(run_pack(latents.reshape(patches, model), cotangent.reshape(patches, model)))
    mod = modulation[0].transpose(1, 0, 2)
    qkv, prob, att, gdy, shares, send = run_forward(
        frame_clip, clip_patches, place, tokens, mod, qkv_weight, chips
    )
    other = lax.ppermute(send, "seq", [(i, i ^ 1) for i in range(seq)])
    keep, qkv, prob, att, gdy = run_keep(place, shares, (qkv, prob, att, gdy))
    pair = run_add(keep, other).reshape(chips, SHARE_ROWS, model)
    same_core = [[2 * chip + core for chip in range(chips)] for core in range(2)]
    terms = lax.all_to_all(pair, "seq", 0, 0, tiled=True, axis_index_groups=same_core)
    saved = (gdy, out_weight, att, qkv, prob, qkv_weight)
    results = run_backward(frame_clip, clip_patches, place, tokens, mod, saved, pair)
    total = run_sum(terms, results).astype(jnp.bfloat16)
    half = groups // 2
    met = lax.ppermute(total, "dp", [(i, i ^ half) for i in range(groups)])
    total = (total.astype(jnp.float32) + met.astype(jnp.float32)).astype(jnp.bfloat16)
    others = [
        lax.ppermute(total, "dp", [(i, i ^ stride) for i in range(groups)])
        for stride in range(1, half)
    ]
    returned = exchange(results)
    block_out, latent_grad, grad = run_finish(returned, total, others, share)
    return block_out.reshape(latents.shape), latent_grad.reshape(latents.shape), grad


def solution(mesh):
    in_specs = (
        P("dp", "seq", None, None),
        P("dp", "seq", None, None),
        P(),
        P(),
        P("dp", None, None, None),
        P("dp", None),
        P("dp", None),
    )
    out_specs = (P("dp", "seq", None, None), P("dp", "seq", None, None), P("seq", None))
    return jax.shard_map(
        per_device, mesh=mesh, in_specs=in_specs, out_specs=out_specs, check_vma=False
    )
```

```python
import jax
import jax.numpy as jnp
from jax import lax
from jax.experimental import pallas as pl
from jax.experimental.pallas import tpu as pltpu
from jax.sharding import PartitionSpec as P

HEADS = 16
LANES = 128
EDGES = (0, 512, 1152)
PARTS = 2
SHARE_ROWS = 40
MIB = 1024 * 1024

NN = (((1,), (0,)), ((), ()))
NT = (((1,), (1,)), ((), ()))
TN = (((0,), (0,)), ((), ()))


def dot(left, right, dims):
    return lax.dot_general(left, right, dims, preferred_element_type=jnp.float32)


def wide_columns(width):
    edges = list(range(0, width - 511, 512))
    return [slice(low, high) for low, high in zip(edges, edges[1:] + [width])]


def head_span(head, head_dim):
    first, last = head * head_dim, (head + 1) * head_dim
    low = first // LANES * LANES
    high = -(-last // LANES) * LANES
    return first, last, low, high


def head_mask(first, last, low, high):
    lane = lax.broadcasted_iota(jnp.int32, (1, high - low), 1) + low
    return jnp.where((lane >= first) & (lane < last), 1.0, 0.0).astype(jnp.bfloat16)


def add_tiles(parts, low, value):
    for start in range(0, value.shape[1], LANES):
        tile = (low + start) // LANES
        piece = value[:, start : start + LANES]
        parts[tile] = parts[tile] + piece if tile in parts else piece


def flush_tiles(parts, done, store):
    for tile in sorted(parts):
        if (tile + 1) * LANES <= done:
            store(tile * LANES, parts.pop(tile))


def normalize(tokens):
    center = tokens - jnp.mean(tokens, axis=-1, keepdims=True)
    spread = jnp.mean(center * center, axis=-1, keepdims=True)
    inv_std = lax.rsqrt(spread + 1e-06)
    return center * inv_std, inv_std


def valid_patches(base, count, patches):
    index = base + lax.broadcasted_iota(jnp.int32, (patches, 1), 0)
    return (index < count).astype(jnp.float32)


def forward_kernel(
    clip_ref, count_ref, place_ref, tokens_ref, mod_ref, wqkv_hbm,
    qkv_ref, prob_ref, att_ref, gdy_ref, share_ref, send_ref,
    wqkv_ref, xmod_ref, same_ref, turned_ref, load_sems,
):
    rows, model = xmod_ref.shape
    frames = clip_ref.shape[1]
    patches = rows // frames
    head_dim = model // HEADS
    base = place_ref[0]
    core = place_ref[1]

    parts_n = len(EDGES) - 1
    columns = [
        [slice(kind * model + EDGES[part], kind * model + EDGES[part + 1]) for kind in range(3)]
        for part in range(parts_n)
    ]
    loads = [
        [
            pltpu.make_async_copy(
                wqkv_hbm.at[:, where], wqkv_ref.at[:, where], load_sems.at[part, kind]
            )
            for kind, where in enumerate(columns[part])
        ]
        for part in range(parts_n)
    ]

    def start_loads(part):
        if part < parts_n:
            for load in loads[part]:
                load.start()

    start_loads(0)

    def pair_step(step, carry):
        where = pl.ds(pl.multiple_of(2 * step * patches, 2 * patches), 2 * patches)
        latent = tokens_ref[where, :model].astype(jnp.float32)
        cotangent = tokens_ref[where, model:].astype(jnp.float32)
        xmods, gdys = [], []
        for k in range(2):
            half = slice(k * patches, (k + 1) * patches)
            clip = clip_ref[0, 2 * step + k]
            shift = mod_ref[0, pl.ds(clip, 1), :]
            scale = mod_ref[1, pl.ds(clip, 1), :]
            gate = mod_ref[2, pl.ds(clip, 1), :]
            normed, _ = normalize(latent[half])
            xmods.append(normed * (1.0 + scale) + shift)
            valid = valid_patches(base, count_ref[0, clip], patches)
            gdys.append(valid * gate * cotangent[half])
        xmod_ref[where, :] = jnp.concatenate(xmods, axis=0).astype(jnp.bfloat16)
        gdy_ref[where, :] = jnp.concatenate(gdys, axis=0).astype(jnp.bfloat16)
        return carry

    lax.fori_loop(0, frames // 2, pair_step, 0, unroll=4)
    start_loads(1)

    starts = []
    for clip in range(1, mod_ref.shape[1]):
        start = jnp.int32(0)
        for frame in range(frames):
            start = start + jnp.where(clip_ref[0, frame] < clip, 1, 0)
        starts.append(start)

    def key_of(index):
        frame = index // patches
        key = index % patches
        for start in starts:
            key = key + jnp.where(frame >= start, patches, 0)
        return key

    key_e = key_of(lax.broadcasted_iota(jnp.int32, (rows, 1), 0))
    key_f = key_of(lax.broadcasted_iota(jnp.int32, (1, rows), 1))
    same_ref[...] = (key_e == key_f).astype(jnp.float32)

    held = SHARE_ROWS
    chips = share_ref.shape[1] // held
    share = model // (2 * chips)
    for start in range(0, model, LANES):
        turned_ref[start : start + LANES, :] = gdy_ref[:, start : start + LANES].astype(
            jnp.float32
        ).T
    turned_ref[model:, :] = jnp.zeros((turned_ref.shape[0] - model, rows), jnp.float32)
    for side in range(2):
        for chip in range(0, chips, 2):
            pieces = []
            for k in range(2):
                start = (2 * (chip + k) + side) * share
                pieces.append(turned_ref[start : start + held, :])
            share_ref[side, chip * held : (chip + 2) * held, :] = jnp.concatenate(
                pieces, axis=0
            ).astype(jnp.bfloat16)

    def store_att(low, value):
        att_ref[:, low : low + LANES] = value.astype(jnp.bfloat16)

    def score_of(head):
        first, last, low, high = head_span(head, head_dim)
        query = qkv_ref[:, low:high] * head_mask(first, last, low, high)
        return dot(qkv_ref[:, model + low : model + high], query, NT)

    xmod = xmod_ref[...]
    parts = {}
    head = 0
    for part in range(parts_n):
        for load in loads[part]:
            load.wait()
        start_loads(part + 2)
        for where in columns[part]:
            qkv_ref[:, where] = dot(xmod, wqkv_ref[:, where], NN).astype(jnp.bfloat16)
        scores = None
        while head < HEADS and (head + 1) * head_dim <= EDGES[part + 1]:
            first, last, low, high = head_span(head, head_dim)
            mask = head_mask(first, last, low, high)
            if scores is None:
                scores = score_of(head)
            last_head = (head + 2) * head_dim > EDGES[part + 1]
            later = None if last_head else score_of(head + 1)
            value = qkv_ref[:, 2 * model + low : 2 * model + high] * mask
            expo = jnp.exp(scores * head_dim ** (-0.5)) * same_ref[...]
            prob = (expo * (1.0 / jnp.sum(expo, axis=0, keepdims=True))).astype(jnp.bfloat16)
            prob_ref[head] = prob
            add_tiles(parts, low, dot(prob, value, TN))
            flush_tiles(parts, last, store_att)
            scores = later
            head += 1

    for where in wide_columns(model):
        send_ref[:, where] = dot(share_ref[1 - core], att_ref[:, where], NN).astype(jnp.bfloat16)


def keep_kernel(place_ref, share_ref, qkv_ref, prob_ref, att_ref, gdy_ref, *refs):
    keep_ref, targets, sems = refs[0], refs[1:-1], refs[-1]
    stores = []
    for source, target in zip((qkv_ref, prob_ref, att_ref, gdy_ref), targets):
        store = pltpu.make_async_copy(source, target, sems.at[len(stores)])
        store.start()
        stores.append(store)
    core = place_ref[1]
    model = keep_ref.shape[1]
    for where in wide_columns(model):
        keep_ref[:, where] = dot(share_ref[core], att_ref[:, where], NN).astype(jnp.bfloat16)
    for store in stores:
        store.wait()


def run_keep(place, share, saved):
    rows, model = share.shape[1], saved[2].shape[1]
    low = jnp.bfloat16
    return pl.pallas_call(
        keep_kernel,
        out_shape=(pltpu.VMEM((rows, model), low),)
        + tuple(pltpu.HBM(array.shape, low) for array in saved),
        in_specs=[smem()] + [vmem()] * (1 + len(saved)),
        out_specs=(vmem(),) + (hbm(),) * len(saved),
        scratch_shapes=[pltpu.SemaphoreType.DMA((len(saved),))],
        compiler_params=pltpu.CompilerParams(vmem_limit_bytes=12 * MIB),
        cost_estimate=pl.CostEstimate(
            flops=2 * rows * model * share.shape[2], bytes_accessed=6 * MIB, transcendentals=0
        ),
        name="keep",
    )(place, in_vmem(share), *map(in_vmem, saved))


def backward_kernel(
    clip_ref, count_ref, place_ref, tokens_ref, mod_ref,
    gdy_hbm, wout_hbm, att_hbm, qkv_hbm, prob_hbm, wqkv_hbm, after_ref,
    out_hbm,
    gdy_ref, wout_ref, att_ref, qkv_ref, prob_ref, wqkv_ref,
    datt_ref, dqkv_ref, proj_ref, dxmod_ref, out_ref, sems, store_sems,
):
    del after_ref
    rows, model = gdy_ref.shape
    frames = clip_ref.shape[1]
    patches = rows // frames
    head_dim = model // HEADS
    att_scale = head_dim ** (-0.5)
    base = place_ref[0]

    loads = []
    for source_hbm, target_ref in (
        (gdy_hbm, gdy_ref), (wout_hbm, wout_ref), (att_hbm, att_ref),
        (qkv_hbm, qkv_ref), (prob_hbm, prob_ref), (wqkv_hbm, wqkv_ref),
    ):
        load = pltpu.make_async_copy(source_hbm, target_ref, sems.at[len(loads)])
        load.start()
        loads.append(load)

    loads[0].wait()
    loads[1].wait()
    gdy = gdy_ref[...]
    for where in wide_columns(model):
        datt_ref[:, where] = dot(gdy, wout_ref[where, :], NT).astype(jnp.bfloat16)
    loads[2].wait()
    att = att_ref[...]
    for where in wide_columns(model):
        proj_ref[:, where] = dot(att, wout_ref[:, where], NN)
    loads[3].wait()
    loads[4].wait()

    def store_at(offset, factor):
        def store(low, value):
            dqkv_ref[:, offset + low : offset + low + LANES] = (value * factor).astype(jnp.bfloat16)
        return store

    parts_q, parts_k, parts_v = {}, {}, {}
    for head in range(HEADS):
        first, last, low, high = head_span(head, head_dim)
        mask = head_mask(first, last, low, high)
        query = qkv_ref[:, low:high] * mask
        key = qkv_ref[:, model + low : model + high] * mask
        value = qkv_ref[:, 2 * model + low : 2 * model + high]
        datt = datt_ref[:, low:high] * mask
        prob_low = prob_ref[head]
        add_tiles(parts_v, low, dot(prob_low, datt, NN))
        prob = prob_low.astype(jnp.float32)
        dprob = dot(value, datt, NT)
        total = jnp.sum(prob * dprob, axis=0, keepdims=True)
        dscore = (prob * (dprob - total)).astype(jnp.bfloat16)
        add_tiles(parts_k, low, dot(dscore, query, NN))
        add_tiles(parts_q, low, dot(dscore, key, TN))
        flush_tiles(parts_q, last, store_at(0, att_scale))
        flush_tiles(parts_k, last, store_at(model, att_scale))
        flush_tiles(parts_v, last, store_at(2 * model, 1.0))

    loads[5].wait()
    dqkv = dqkv_ref[...]
    for where in wide_columns(model):
        dxmod_ref[:, where] = dot(dqkv, wqkv_ref[where, :], NT)

    def pair_step(step, carry):
        where = pl.ds(pl.multiple_of(2 * step * patches, 2 * patches), 2 * patches)
        latent_pair = tokens_ref[where, :model].astype(jnp.float32)
        cotangent = tokens_ref[where, model:].astype(jnp.float32)
        blocks, branches = [], []
        for k in range(2):
            half = slice(k * patches, (k + 1) * patches)
            clip = clip_ref[0, 2 * step + k]
            scale = mod_ref[1, pl.ds(clip, 1), :]
            gate = mod_ref[2, pl.ds(clip, 1), :]
            valid = valid_patches(base, count_ref[0, clip], patches)
            own = pl.ds(pl.multiple_of((2 * step + k) * patches, patches), patches)
            latent = latent_pair[half]
            blocks.append(latent + valid * gate * proj_ref[own, :])
            normed, inv_std = normalize(latent)
            dnorm = dxmod_ref[own, :] * (1.0 + scale)
            branches.append(
                inv_std
                * (
                    dnorm
                    - jnp.mean(dnorm, axis=-1, keepdims=True)
                    - normed * jnp.mean(dnorm * normed, axis=-1, keepdims=True)
                )
            )
        out_ref[where, :model] = jnp.concatenate(blocks, axis=0).astype(jnp.bfloat16)
        out_ref[where, model:] = (cotangent + jnp.concatenate(branches, axis=0)).astype(
            jnp.bfloat16
        )
        return carry

    stores = []
    part_n = store_sems.shape[0]
    steps = frames // (2 * part_n)
    for part in range(part_n):
        lax.fori_loop(part * steps, (part + 1) * steps, pair_step, 0, unroll=steps)
        where = slice(2 * part * steps * patches, 2 * (part + 1) * steps * patches)
        store = pltpu.make_async_copy(
            out_ref.at[where, :], out_hbm.at[where, :], store_sems.at[part]
        )
        store.start()
        stores.append(store)
    for store in stores:
        store.wait()


def smem():
    return pl.BlockSpec(memory_space=pltpu.SMEM)


def vmem():
    return pl.BlockSpec(memory_space=pltpu.VMEM)


def hbm():
    return pl.BlockSpec(memory_space=pltpu.HBM)


def in_hbm(array):
    return pltpu.with_memory_space_constraint(array, pltpu.HBM)


def in_vmem(array):
    return pltpu.with_memory_space_constraint(array, pltpu.VMEM)


def run_forward(frame_clip, clip_patches, place, tokens, modulation, qkv_weight, chips):
    rows, model = tokens.shape[0], tokens.shape[1] // 2
    low = jnp.bfloat16
    groups = len(EDGES) - 1
    sizes = ((rows, 3 * model), (HEADS, rows, rows), (rows, model), (rows, model))
    sizes += ((2, chips * SHARE_ROWS, rows), (chips * SHARE_ROWS, model))
    return pl.pallas_call(
        forward_kernel,
        out_shape=tuple(pltpu.VMEM(size, low) for size in sizes),
        in_specs=[smem()] * 3 + [vmem()] * 2 + [hbm()],
        out_specs=(vmem(),) * 6,
        scratch_shapes=[
            pltpu.VMEM((model, 3 * model), low),
            pltpu.VMEM((rows, model), low),
            pltpu.VMEM((rows, rows), jnp.float32),
            pltpu.VMEM((model + 16, rows), jnp.float32),
            pltpu.SemaphoreType.DMA((groups, 3)),
        ],
        compiler_params=pltpu.CompilerParams(vmem_limit_bytes=36 * MIB),
        cost_estimate=pl.CostEstimate(
            flops=2 * rows * model * 4 * model, bytes_accessed=12 * MIB, transcendentals=0
        ),
        name="forward",
    )(frame_clip, clip_patches, place, in_vmem(tokens), modulation, in_hbm(qkv_weight))


def run_backward(frame_clip, clip_patches, place, tokens, modulation, saved, after):
    rows, model = tokens.shape[0], tokens.shape[1] // 2
    low = jnp.bfloat16
    return pl.pallas_call(
        backward_kernel,
        out_shape=pltpu.HBM(tokens.shape, low),
        in_specs=[smem()] * 3 + [vmem()] * 2 + [hbm()] * (len(saved) + 1),
        out_specs=hbm(),
        scratch_shapes=[pltpu.VMEM(array.shape, low) for array in saved]
        + [
            pltpu.VMEM((rows, model), low),
            pltpu.VMEM((rows, 3 * model), low),
            pltpu.VMEM((rows, model), jnp.float32),
            pltpu.VMEM((rows, model), jnp.float32),
            pltpu.VMEM(tokens.shape, low),
            pltpu.SemaphoreType.DMA((len(saved),)),
            pltpu.SemaphoreType.DMA((4,)),
        ],
        compiler_params=pltpu.CompilerParams(vmem_limit_bytes=36 * MIB),
        cost_estimate=pl.CostEstimate(
            flops=2 * rows * model * 6 * model, bytes_accessed=16 * MIB, transcendentals=0
        ),
        name="backward",
    )(
        frame_clip, clip_patches, place, in_vmem(tokens), modulation, *map(in_hbm, saved), in_hbm(after)
    )


def pack_kernel(latent_hbm, cotangent_hbm, out_hbm, both_ref, load_sems, store_sems):
    rows, model = latent_hbm.shape
    parts = store_sems.shape[0]
    spans = [slice(part * rows // parts, (part + 1) * rows // parts) for part in range(parts)]
    loads = []
    for part, where in enumerate(spans):
        for side, source in enumerate((latent_hbm, cotangent_hbm)):
            columns = slice(side * model, (side + 1) * model)
            load = pltpu.make_async_copy(
                source.at[where, :], both_ref.at[where, columns], load_sems.at[part, side]
            )
            load.start()
            loads.append(load)
    stores = []
    for part, where in enumerate(spans):
        loads[2 * part].wait()
        loads[2 * part + 1].wait()
        store = pltpu.make_async_copy(
            both_ref.at[where, :], out_hbm.at[where, :], store_sems.at[part]
        )
        store.start()
        stores.append(store)
    for store in stores:
        store.wait()


def run_pack(latents, cotangent):
    rows, model = latents.shape
    size = (rows, 2 * model)
    return pl.pallas_call(
        pack_kernel,
        out_shape=pltpu.HBM(size, latents.dtype),
        in_specs=[hbm()] * 2,
        out_specs=hbm(),
        scratch_shapes=[
            pltpu.VMEM(size, latents.dtype),
            pltpu.SemaphoreType.DMA((PARTS, 2)),
            pltpu.SemaphoreType.DMA((PARTS,)),
        ],
        compiler_params=pltpu.CompilerParams(vmem_limit_bytes=12 * MIB),
        name="pack",
    )(in_hbm(latents), in_hbm(cotangent))


def add_kernel(left_ref, right_ref, out_hbm, out_ref, store_sems):
    parts = store_sems.shape[0]
    rows = out_ref.shape[0] // parts
    stores = []
    for part in range(parts):
        where = slice(part * rows, (part + 1) * rows)
        out_ref[where, :] = (
            left_ref[where, :].astype(jnp.float32) + right_ref[where, :].astype(jnp.float32)
        ).astype(jnp.bfloat16)
        store = pltpu.make_async_copy(
            out_ref.at[where, :], out_hbm.at[where, :], store_sems.at[part]
        )
        store.start()
        stores.append(store)
    for store in stores:
        store.wait()


def run_add(left, right):
    return pl.pallas_call(
        add_kernel,
        out_shape=pltpu.HBM(left.shape, left.dtype),
        in_specs=[vmem()] * 2,
        out_specs=hbm(),
        scratch_shapes=[pltpu.VMEM(left.shape, left.dtype), pltpu.SemaphoreType.DMA((5,))],
        compiler_params=pltpu.CompilerParams(vmem_limit_bytes=12 * MIB),
        name="add",
    )(in_vmem(left), in_vmem(right))


def sum_kernel(terms_ref, after_ref, out_ref):
    del after_ref
    step_rows = 8
    for start in range(0, out_ref.shape[0], step_rows):
        where = slice(start, start + step_rows)
        total = terms_ref[0, where, :].astype(jnp.float32)
        for term in range(1, terms_ref.shape[0]):
            total = total + terms_ref[term, where, :].astype(jnp.float32)
        out_ref[where, :] = total


def run_sum(terms, after):
    return pl.pallas_call(
        sum_kernel,
        out_shape=jax.ShapeDtypeStruct(terms.shape[1:], jnp.float32),
        in_specs=[vmem(), hbm()],
        out_specs=vmem(),
        compiler_params=pltpu.CompilerParams(vmem_limit_bytes=12 * MIB),
        name="sum",
    )(terms, in_hbm(after))


def finish_kernel(returned_ref, own_ref, *refs):
    other_refs, (block_ref, latent_ref, grad_ref) = refs[:-3], refs[-3:]
    model = block_ref.shape[1]
    block_ref[...] = returned_ref[:, :model]
    latent_ref[...] = returned_ref[:, model:]
    total = own_ref[...].astype(jnp.float32)
    for other_ref in other_refs:
        total = total + other_ref[...].astype(jnp.float32)
    grad_ref[...] = total[: grad_ref.shape[0]]


def run_finish(returned, own, others, share):
    rows, model = returned.shape[0], returned.shape[1] // 2
    low = jnp.bfloat16
    return pl.pallas_call(
        finish_kernel,
        out_shape=(
            jax.ShapeDtypeStruct((rows, model), low),
            jax.ShapeDtypeStruct((rows, model), low),
            jax.ShapeDtypeStruct((share, model), jnp.float32),
        ),
        in_specs=[vmem()] * (2 + len(others)),
        out_specs=(vmem(),) * 3,
        compiler_params=pltpu.CompilerParams(vmem_limit_bytes=12 * MIB),
        cost_estimate=pl.CostEstimate(flops=0, bytes_accessed=4 * MIB, transcendentals=0),
        name="finish",
    )(returned, own, *others)


def per_device(latents, cotangent, qkv_weight, out_weight, modulation, frame_clip, clip_patches):
    seq = lax.axis_size("seq")
    groups = lax.axis_size("dp")
    chips = seq // 2
    patches, model = latents.shape[2], latents.shape[3]
    mine = patches // seq
    share = model // seq
    index = lax.axis_index("seq")
    place = jnp.stack([index * mine, index % 2]).astype(jnp.int32)

    def exchange(rows):
        pieces = rows.reshape(seq, mine, rows.shape[1])
        return lax.all_to_all(pieces, "seq", 0, 0, tiled=True).reshape(rows.shape)

    tokens = exchange(run_pack(latents.reshape(patches, model), cotangent.reshape(patches, model)))
    mod = modulation[0].transpose(1, 0, 2)
    qkv, prob, att, gdy, shares, send = run_forward(
        frame_clip, clip_patches, place, tokens, mod, qkv_weight, chips
    )
    other = lax.ppermute(send, "seq", [(i, i ^ 1) for i in range(seq)])
    keep, qkv, prob, att, gdy = run_keep(place, shares, (qkv, prob, att, gdy))
    pair = run_add(keep, other).reshape(chips, SHARE_ROWS, model)
    same_core = [[2 * chip + core for chip in range(chips)] for core in range(2)]
    terms = lax.all_to_all(pair, "seq", 0, 0, tiled=True, axis_index_groups=same_core)
    saved = (gdy, out_weight, att, qkv, prob, qkv_weight)
    results = run_backward(frame_clip, clip_patches, place, tokens, mod, saved, pair)
    total = run_sum(terms, results).astype(jnp.bfloat16)
    met = lax.ppermute(total, "dp", [(i, i ^ 1) for i in range(groups)])
    total = (total.astype(jnp.float32) + met.astype(jnp.float32)).astype(jnp.bfloat16)
    half = groups // 2
    strides = [stride for stride in range(2, groups, 2) if stride != half] + [half]
    others = [
        lax.ppermute(total, "dp", [(i, i ^ stride) for i in range(groups)]) for stride in strides
    ]
    returned = exchange(results)
    block_out, latent_grad, grad = run_finish(returned, total, others, share)
    return block_out.reshape(latents.shape), latent_grad.reshape(latents.shape), grad


def solution(mesh):
    in_specs = (
        P("dp", "seq", None, None),
        P("dp", "seq", None, None),
        P(),
        P(),
        P("dp", None, None, None),
        P("dp", None),
        P("dp", None),
    )
    out_specs = (P("dp", "seq", None, None), P("dp", "seq", None, None), P("seq", None))
    return jax.shard_map(
        per_device, mesh=mesh, in_specs=in_specs, out_specs=out_specs, check_vma=False
    )
```

```python
import jax
import jax.numpy as jnp
from jax import lax
from jax.experimental import pallas as pl
from jax.experimental.pallas import tpu as pltpu
from jax.sharding import PartitionSpec as P

HEADS = 16
LANES = 128
EDGES = (0, 512, 1152)
PARTS = 2
SHARE_ROWS = 40
MIB = 1024 * 1024

NN = (((1,), (0,)), ((), ()))
NT = (((1,), (1,)), ((), ()))
TN = (((0,), (0,)), ((), ()))


def dot(left, right, dims):
    return lax.dot_general(left, right, dims, preferred_element_type=jnp.float32)


def wide_columns(width):
    edges = list(range(0, width - 511, 512))
    return [slice(low, high) for low, high in zip(edges, edges[1:] + [width])]


def head_span(head, head_dim):
    first, last = head * head_dim, (head + 1) * head_dim
    low = first // LANES * LANES
    high = -(-last // LANES) * LANES
    return first, last, low, high


def head_mask(first, last, low, high):
    lane = lax.broadcasted_iota(jnp.int32, (1, high - low), 1) + low
    return jnp.where((lane >= first) & (lane < last), 1.0, 0.0).astype(jnp.bfloat16)


def add_tiles(parts, low, value):
    for start in range(0, value.shape[1], LANES):
        tile = (low + start) // LANES
        piece = value[:, start : start + LANES]
        parts[tile] = parts[tile] + piece if tile in parts else piece


def flush_tiles(parts, done, store):
    for tile in sorted(parts):
        if (tile + 1) * LANES <= done:
            store(tile * LANES, parts.pop(tile))


def normalize(tokens):
    center = tokens - jnp.mean(tokens, axis=-1, keepdims=True)
    spread = jnp.mean(center * center, axis=-1, keepdims=True)
    inv_std = lax.rsqrt(spread + 1e-06)
    return center * inv_std, inv_std


def valid_patches(base, count, patches):
    index = base + lax.broadcasted_iota(jnp.int32, (patches, 1), 0)
    return (index < count).astype(jnp.float32)


def forward_kernel(
    clip_ref, count_ref, place_ref, tokens_ref, mod_ref, wqkv_hbm,
    qkv_ref, prob_ref, att_ref, gdy_ref, share_ref, send_ref,
    wqkv_ref, xmod_ref, same_ref, turned_ref, load_sems,
):
    rows, model = xmod_ref.shape
    frames = clip_ref.shape[1]
    patches = rows // frames
    head_dim = model // HEADS
    base = place_ref[0]
    core = place_ref[1]

    parts_n = len(EDGES) - 1
    columns = [
        [slice(kind * model + EDGES[part], kind * model + EDGES[part + 1]) for kind in range(3)]
        for part in range(parts_n)
    ]
    loads = [
        [
            pltpu.make_async_copy(
                wqkv_hbm.at[:, where], wqkv_ref.at[:, where], load_sems.at[part, kind]
            )
            for kind, where in enumerate(columns[part])
        ]
        for part in range(parts_n)
    ]

    def start_loads(part):
        if part < parts_n:
            for load in loads[part]:
                load.start()

    start_loads(0)

    def pair_step(step, carry):
        where = pl.ds(pl.multiple_of(2 * step * patches, 2 * patches), 2 * patches)
        latent = tokens_ref[where, :model].astype(jnp.float32)
        cotangent = tokens_ref[where, model:].astype(jnp.float32)
        xmods, gdys = [], []
        for k in range(2):
            half = slice(k * patches, (k + 1) * patches)
            clip = clip_ref[0, 2 * step + k]
            shift = mod_ref[0, pl.ds(clip, 1), :]
            scale = mod_ref[1, pl.ds(clip, 1), :]
            gate = mod_ref[2, pl.ds(clip, 1), :]
            normed, _ = normalize(latent[half])
            xmods.append(normed * (1.0 + scale) + shift)
            valid = valid_patches(base, count_ref[0, clip], patches)
            gdys.append(valid * gate * cotangent[half])
        xmod_ref[where, :] = jnp.concatenate(xmods, axis=0).astype(jnp.bfloat16)
        gdy_ref[where, :] = jnp.concatenate(gdys, axis=0).astype(jnp.bfloat16)
        return carry

    lax.fori_loop(0, frames // 2, pair_step, 0, unroll=8)
    start_loads(1)

    starts = []
    for clip in range(1, mod_ref.shape[1]):
        start = jnp.int32(0)
        for frame in range(frames):
            start = start + jnp.where(clip_ref[0, frame] < clip, 1, 0)
        starts.append(start)

    def key_of(index):
        frame = index // patches
        key = index % patches
        for start in starts:
            key = key + jnp.where(frame >= start, patches, 0)
        return key

    key_e = key_of(lax.broadcasted_iota(jnp.int32, (rows, 1), 0))
    key_f = key_of(lax.broadcasted_iota(jnp.int32, (1, rows), 1))
    same_ref[...] = (key_e == key_f).astype(jnp.float32)

    held = SHARE_ROWS
    chips = share_ref.shape[1] // held
    share = model // (2 * chips)
    for start in range(0, model, LANES):
        turned_ref[start : start + LANES, :] = gdy_ref[:, start : start + LANES].astype(
            jnp.float32
        ).T
    turned_ref[model:, :] = jnp.zeros((turned_ref.shape[0] - model, rows), jnp.float32)
    for side in range(2):
        for chip in range(0, chips, 2):
            pieces = []
            for k in range(2):
                start = (2 * (chip + k) + side) * share
                pieces.append(turned_ref[start : start + held, :])
            share_ref[side, chip * held : (chip + 2) * held, :] = jnp.concatenate(
                pieces, axis=0
            ).astype(jnp.bfloat16)

    def store_att(low, value):
        att_ref[:, low : low + LANES] = value.astype(jnp.bfloat16)

    def score_of(head):
        first, last, low, high = head_span(head, head_dim)
        query = qkv_ref[:, low:high] * head_mask(first, last, low, high)
        return dot(qkv_ref[:, model + low : model + high], query, NT)

    xmod = xmod_ref[...]
    parts = {}
    head = 0
    for part in range(parts_n):
        for load in loads[part]:
            load.wait()
        start_loads(part + 2)
        for where in columns[part]:
            qkv_ref[:, where] = dot(xmod, wqkv_ref[:, where], NN).astype(jnp.bfloat16)
        scores = None
        while head < HEADS and (head + 1) * head_dim <= EDGES[part + 1]:
            first, last, low, high = head_span(head, head_dim)
            mask = head_mask(first, last, low, high)
            if scores is None:
                scores = score_of(head)
            last_head = (head + 2) * head_dim > EDGES[part + 1]
            later = None if last_head else score_of(head + 1)
            value = qkv_ref[:, 2 * model + low : 2 * model + high] * mask
            expo = jnp.exp(scores * head_dim ** (-0.5)) * same_ref[...]
            prob = (expo * (1.0 / jnp.sum(expo, axis=0, keepdims=True))).astype(jnp.bfloat16)
            prob_ref[head] = prob
            add_tiles(parts, low, dot(prob, value, TN))
            flush_tiles(parts, last, store_att)
            scores = later
            head += 1

    for where in wide_columns(model):
        send_ref[:, where] = dot(share_ref[1 - core], att_ref[:, where], NN).astype(jnp.bfloat16)


def keep_kernel(place_ref, share_ref, qkv_ref, prob_ref, att_ref, gdy_ref, *refs):
    keep_ref, targets, sems = refs[0], refs[1:-1], refs[-1]
    stores = []
    for source, target in zip((qkv_ref, prob_ref, att_ref, gdy_ref), targets):
        store = pltpu.make_async_copy(source, target, sems.at[len(stores)])
        store.start()
        stores.append(store)
    core = place_ref[1]
    model = keep_ref.shape[1]
    for where in wide_columns(model):
        keep_ref[:, where] = dot(share_ref[core], att_ref[:, where], NN).astype(jnp.bfloat16)
    for store in stores:
        store.wait()


def run_keep(place, share, saved):
    rows, model = share.shape[1], saved[2].shape[1]
    low = jnp.bfloat16
    return pl.pallas_call(
        keep_kernel,
        out_shape=(pltpu.VMEM((rows, model), low),)
        + tuple(pltpu.HBM(array.shape, low) for array in saved),
        in_specs=[smem()] + [vmem()] * (1 + len(saved)),
        out_specs=(vmem(),) + (hbm(),) * len(saved),
        scratch_shapes=[pltpu.SemaphoreType.DMA((len(saved),))],
        compiler_params=pltpu.CompilerParams(vmem_limit_bytes=12 * MIB),
        cost_estimate=pl.CostEstimate(
            flops=2 * rows * model * share.shape[2], bytes_accessed=6 * MIB, transcendentals=0
        ),
        name="keep",
    )(place, in_vmem(share), *map(in_vmem, saved))


def backward_kernel(
    clip_ref, count_ref, place_ref, tokens_ref, mod_ref,
    gdy_hbm, wout_hbm, att_hbm, qkv_hbm, prob_hbm, wqkv_hbm, after_ref,
    out_hbm,
    gdy_ref, wout_ref, att_ref, qkv_ref, prob_ref, wqkv_ref,
    datt_ref, dqkv_ref, proj_ref, dxmod_ref, out_ref, sems, store_sems,
):
    del after_ref
    rows, model = gdy_ref.shape
    frames = clip_ref.shape[1]
    patches = rows // frames
    head_dim = model // HEADS
    att_scale = head_dim ** (-0.5)
    base = place_ref[0]

    loads = []
    for source_hbm, target_ref in (
        (gdy_hbm, gdy_ref), (wout_hbm, wout_ref), (att_hbm, att_ref),
        (qkv_hbm, qkv_ref), (prob_hbm, prob_ref), (wqkv_hbm, wqkv_ref),
    ):
        load = pltpu.make_async_copy(source_hbm, target_ref, sems.at[len(loads)])
        load.start()
        loads.append(load)

    loads[0].wait()
    loads[1].wait()
    gdy = gdy_ref[...]
    for where in wide_columns(model):
        datt_ref[:, where] = dot(gdy, wout_ref[where, :], NT).astype(jnp.bfloat16)
    loads[2].wait()
    att = att_ref[...]
    for where in wide_columns(model):
        proj_ref[:, where] = dot(att, wout_ref[:, where], NN)
    loads[3].wait()
    loads[4].wait()

    def store_at(offset, factor):
        def store(low, value):
            dqkv_ref[:, offset + low : offset + low + LANES] = (value * factor).astype(jnp.bfloat16)
        return store

    parts_q, parts_k, parts_v = {}, {}, {}
    for head in range(HEADS):
        first, last, low, high = head_span(head, head_dim)
        mask = head_mask(first, last, low, high)
        query = qkv_ref[:, low:high] * mask
        key = qkv_ref[:, model + low : model + high] * mask
        value = qkv_ref[:, 2 * model + low : 2 * model + high]
        datt = datt_ref[:, low:high] * mask
        prob_low = prob_ref[head]
        add_tiles(parts_v, low, dot(prob_low, datt, NN))
        prob = prob_low.astype(jnp.float32)
        dprob = dot(value, datt, NT)
        total = jnp.sum(prob * dprob, axis=0, keepdims=True)
        dscore = (prob * (dprob - total)).astype(jnp.bfloat16)
        add_tiles(parts_k, low, dot(dscore, query, NN))
        add_tiles(parts_q, low, dot(dscore, key, TN))
        flush_tiles(parts_q, last, store_at(0, att_scale))
        flush_tiles(parts_k, last, store_at(model, att_scale))
        flush_tiles(parts_v, last, store_at(2 * model, 1.0))

    loads[5].wait()
    dqkv = dqkv_ref[...]
    for where in wide_columns(model):
        dxmod_ref[:, where] = dot(dqkv, wqkv_ref[where, :], NT)

    def pair_step(step, carry):
        where = pl.ds(pl.multiple_of(2 * step * patches, 2 * patches), 2 * patches)
        latent_pair = tokens_ref[where, :model].astype(jnp.float32)
        cotangent = tokens_ref[where, model:].astype(jnp.float32)
        blocks, branches = [], []
        for k in range(2):
            half = slice(k * patches, (k + 1) * patches)
            clip = clip_ref[0, 2 * step + k]
            scale = mod_ref[1, pl.ds(clip, 1), :]
            gate = mod_ref[2, pl.ds(clip, 1), :]
            valid = valid_patches(base, count_ref[0, clip], patches)
            own = pl.ds(pl.multiple_of((2 * step + k) * patches, patches), patches)
            latent = latent_pair[half]
            blocks.append(latent + valid * gate * proj_ref[own, :])
            normed, inv_std = normalize(latent)
            dnorm = dxmod_ref[own, :] * (1.0 + scale)
            branches.append(
                inv_std
                * (
                    dnorm
                    - jnp.mean(dnorm, axis=-1, keepdims=True)
                    - normed * jnp.mean(dnorm * normed, axis=-1, keepdims=True)
                )
            )
        out_ref[where, :model] = jnp.concatenate(blocks, axis=0).astype(jnp.bfloat16)
        out_ref[where, model:] = (cotangent + jnp.concatenate(branches, axis=0)).astype(
            jnp.bfloat16
        )
        return carry

    stores = []
    part_n = store_sems.shape[0]
    steps = frames // (2 * part_n)
    for part in range(part_n):
        lax.fori_loop(part * steps, (part + 1) * steps, pair_step, 0, unroll=steps)
        where = slice(2 * part * steps * patches, 2 * (part + 1) * steps * patches)
        store = pltpu.make_async_copy(
            out_ref.at[where, :], out_hbm.at[where, :], store_sems.at[part]
        )
        store.start()
        stores.append(store)
    for store in stores:
        store.wait()


def smem():
    return pl.BlockSpec(memory_space=pltpu.SMEM)


def vmem():
    return pl.BlockSpec(memory_space=pltpu.VMEM)


def hbm():
    return pl.BlockSpec(memory_space=pltpu.HBM)


def in_hbm(array):
    return pltpu.with_memory_space_constraint(array, pltpu.HBM)


def in_vmem(array):
    return pltpu.with_memory_space_constraint(array, pltpu.VMEM)


def run_forward(frame_clip, clip_patches, place, tokens, modulation, qkv_weight, chips):
    rows, model = tokens.shape[0], tokens.shape[1] // 2
    low = jnp.bfloat16
    groups = len(EDGES) - 1
    sizes = ((rows, 3 * model), (HEADS, rows, rows), (rows, model), (rows, model))
    sizes += ((2, chips * SHARE_ROWS, rows), (chips * SHARE_ROWS, model))
    return pl.pallas_call(
        forward_kernel,
        out_shape=tuple(pltpu.VMEM(size, low) for size in sizes),
        in_specs=[smem()] * 3 + [vmem()] * 2 + [hbm()],
        out_specs=(vmem(),) * 6,
        scratch_shapes=[
            pltpu.VMEM((model, 3 * model), low),
            pltpu.VMEM((rows, model), low),
            pltpu.VMEM((rows, rows), jnp.float32),
            pltpu.VMEM((model + 16, rows), jnp.float32),
            pltpu.SemaphoreType.DMA((groups, 3)),
        ],
        compiler_params=pltpu.CompilerParams(vmem_limit_bytes=36 * MIB),
        cost_estimate=pl.CostEstimate(
            flops=2 * rows * model * 4 * model, bytes_accessed=12 * MIB, transcendentals=0
        ),
        name="forward",
    )(frame_clip, clip_patches, place, in_vmem(tokens), modulation, in_hbm(qkv_weight))


def run_backward(frame_clip, clip_patches, place, tokens, modulation, saved, after):
    rows, model = tokens.shape[0], tokens.shape[1] // 2
    low = jnp.bfloat16
    return pl.pallas_call(
        backward_kernel,
        out_shape=pltpu.HBM(tokens.shape, low),
        in_specs=[smem()] * 3 + [vmem()] * 2 + [hbm()] * (len(saved) + 1),
        out_specs=hbm(),
        scratch_shapes=[pltpu.VMEM(array.shape, low) for array in saved]
        + [
            pltpu.VMEM((rows, model), low),
            pltpu.VMEM((rows, 3 * model), low),
            pltpu.VMEM((rows, model), jnp.float32),
            pltpu.VMEM((rows, model), jnp.float32),
            pltpu.VMEM(tokens.shape, low),
            pltpu.SemaphoreType.DMA((len(saved),)),
            pltpu.SemaphoreType.DMA((4,)),
        ],
        compiler_params=pltpu.CompilerParams(vmem_limit_bytes=36 * MIB),
        cost_estimate=pl.CostEstimate(
            flops=2 * rows * model * 6 * model, bytes_accessed=16 * MIB, transcendentals=0
        ),
        name="backward",
    )(
        frame_clip, clip_patches, place, in_vmem(tokens), modulation, *map(in_hbm, saved), in_hbm(after)
    )


def pack_kernel(latent_hbm, cotangent_hbm, out_hbm, both_ref, load_sems, store_sems):
    rows, model = latent_hbm.shape
    parts = store_sems.shape[0]
    spans = [slice(part * rows // parts, (part + 1) * rows // parts) for part in range(parts)]
    loads = []
    for part, where in enumerate(spans):
        for side, source in enumerate((latent_hbm, cotangent_hbm)):
            columns = slice(side * model, (side + 1) * model)
            load = pltpu.make_async_copy(
                source.at[where, :], both_ref.at[where, columns], load_sems.at[part, side]
            )
            load.start()
            loads.append(load)
    stores = []
    for part, where in enumerate(spans):
        loads[2 * part].wait()
        loads[2 * part + 1].wait()
        store = pltpu.make_async_copy(
            both_ref.at[where, :], out_hbm.at[where, :], store_sems.at[part]
        )
        store.start()
        stores.append(store)
    for store in stores:
        store.wait()


def run_pack(latents, cotangent):
    rows, model = latents.shape
    size = (rows, 2 * model)
    return pl.pallas_call(
        pack_kernel,
        out_shape=pltpu.HBM(size, latents.dtype),
        in_specs=[hbm()] * 2,
        out_specs=hbm(),
        scratch_shapes=[
            pltpu.VMEM(size, latents.dtype),
            pltpu.SemaphoreType.DMA((PARTS, 2)),
            pltpu.SemaphoreType.DMA((PARTS,)),
        ],
        compiler_params=pltpu.CompilerParams(vmem_limit_bytes=12 * MIB),
        name="pack",
    )(in_hbm(latents), in_hbm(cotangent))


def add_kernel(left_ref, right_ref, out_hbm, out_ref, store_sems):
    parts = store_sems.shape[0]
    rows = out_ref.shape[0] // parts
    stores = []
    for part in range(parts):
        where = slice(part * rows, (part + 1) * rows)
        out_ref[where, :] = (
            left_ref[where, :].astype(jnp.float32) + right_ref[where, :].astype(jnp.float32)
        ).astype(jnp.bfloat16)
        store = pltpu.make_async_copy(
            out_ref.at[where, :], out_hbm.at[where, :], store_sems.at[part]
        )
        store.start()
        stores.append(store)
    for store in stores:
        store.wait()


def run_add(left, right):
    return pl.pallas_call(
        add_kernel,
        out_shape=pltpu.HBM(left.shape, left.dtype),
        in_specs=[vmem()] * 2,
        out_specs=hbm(),
        scratch_shapes=[pltpu.VMEM(left.shape, left.dtype), pltpu.SemaphoreType.DMA((2,))],
        compiler_params=pltpu.CompilerParams(vmem_limit_bytes=12 * MIB),
        name="add",
    )(in_vmem(left), in_vmem(right))


def sum_kernel(terms_ref, after_ref, out_ref):
    del after_ref
    step_rows = 8
    for start in range(0, out_ref.shape[0], step_rows):
        where = slice(start, start + step_rows)
        total = terms_ref[0, where, :].astype(jnp.float32)
        for term in range(1, terms_ref.shape[0]):
            total = total + terms_ref[term, where, :].astype(jnp.float32)
        out_ref[where, :] = total


def run_sum(terms, after):
    return pl.pallas_call(
        sum_kernel,
        out_shape=jax.ShapeDtypeStruct(terms.shape[1:], jnp.float32),
        in_specs=[vmem(), hbm()],
        out_specs=vmem(),
        compiler_params=pltpu.CompilerParams(vmem_limit_bytes=12 * MIB),
        name="sum",
    )(terms, in_hbm(after))


def finish_kernel(returned_ref, left_ref, right_ref, block_ref, latent_ref, grad_ref):
    model = block_ref.shape[1]
    block_ref[...] = returned_ref[:, :model]
    latent_ref[...] = returned_ref[:, model:]
    total = left_ref[...].astype(jnp.float32) + right_ref[...].astype(jnp.float32)
    grad_ref[...] = total[: grad_ref.shape[0]]


def run_finish(returned, left, right, share):
    rows, model = returned.shape[0], returned.shape[1] // 2
    low = jnp.bfloat16
    return pl.pallas_call(
        finish_kernel,
        out_shape=(
            jax.ShapeDtypeStruct((rows, model), low),
            jax.ShapeDtypeStruct((rows, model), low),
            jax.ShapeDtypeStruct((share, model), jnp.float32),
        ),
        in_specs=[vmem()] * 3,
        out_specs=(vmem(),) * 3,
        compiler_params=pltpu.CompilerParams(vmem_limit_bytes=12 * MIB),
        cost_estimate=pl.CostEstimate(flops=0, bytes_accessed=4 * MIB, transcendentals=0),
        name="finish",
    )(returned, left, right)


def per_device(latents, cotangent, qkv_weight, out_weight, modulation, frame_clip, clip_patches):
    seq = lax.axis_size("seq")
    groups = lax.axis_size("dp")
    chips = seq // 2
    patches, model = latents.shape[2], latents.shape[3]
    mine = patches // seq
    share = model // seq
    index = lax.axis_index("seq")
    place = jnp.stack([index * mine, index % 2]).astype(jnp.int32)

    def exchange(rows):
        pieces = rows.reshape(seq, mine, rows.shape[1])
        return lax.all_to_all(pieces, "seq", 0, 0, tiled=True).reshape(rows.shape)

    tokens = exchange(run_pack(latents.reshape(patches, model), cotangent.reshape(patches, model)))
    mod = modulation[0].transpose(1, 0, 2)
    qkv, prob, att, gdy, shares, send = run_forward(
        frame_clip, clip_patches, place, tokens, mod, qkv_weight, chips
    )
    other = lax.ppermute(send, "seq", [(i, i ^ 1) for i in range(seq)])
    keep, qkv, prob, att, gdy = run_keep(place, shares, (qkv, prob, att, gdy))
    pair = run_add(keep, other).reshape(chips, SHARE_ROWS, model)
    same_core = [[2 * chip + core for chip in range(chips)] for core in range(2)]
    terms = lax.all_to_all(pair, "seq", 0, 0, tiled=True, axis_index_groups=same_core)
    saved = (gdy, out_weight, att, qkv, prob, qkv_weight)
    results = run_backward(frame_clip, clip_patches, place, tokens, mod, saved, pair)
    total = run_sum(terms, results).astype(jnp.bfloat16)
    stride = 1
    while True:
        met = lax.ppermute(total, "dp", [(i, i ^ stride) for i in range(groups)])
        stride *= 2
        if stride >= groups:
            break
        total = (total.astype(jnp.float32) + met.astype(jnp.float32)).astype(jnp.bfloat16)
    returned = exchange(results)
    block_out, latent_grad, grad = run_finish(returned, total, met, share)
    return block_out.reshape(latents.shape), latent_grad.reshape(latents.shape), grad


def solution(mesh):
    in_specs = (
        P("dp", "seq", None, None),
        P("dp", "seq", None, None),
        P(),
        P(),
        P("dp", None, None, None),
        P("dp", None),
        P("dp", None),
    )
    out_specs = (P("dp", "seq", None, None), P("dp", "seq", None, None), P("seq", None))
    return jax.shard_map(
        per_device, mesh=mesh, in_specs=in_specs, out_specs=out_specs, check_vma=False
    )
```
